128 devices in a mesh: batch: 16 (over y, z_lo, core), tensor: 8 (over x, z_hi).
Axes of the slice: x: 4, y: 4, z: 4 (z_hi: 2, z_lo: 2; z = z_hi * 2 + z_lo), core: 2. Of those that a mesh axis runs over, the one named last changes fastest.
Arguments:
- tokens: bfloat16 [8192, 1024], P('batch'), may hold values from -6 to 6
- cotangent: bfloat16 [8192, 1024], P('batch'), may hold values from -6 to 6
- bucket_of: int32 [16], P('batch'), may hold values from 0 to 3, as said below
- seq_lens: int32 [16, 8], P('batch'), may hold values from 0 to 512, as said below
- w_qkv: float32 [2, 1024, 3, 1024], P(None, 'batch', None, 'tensor'), may hold values from -0.1875 to 0.1875
- head_bias: float32 [2, 2, 1024], P(None, None, 'tensor'), may hold values from -1.2 to 1.2
- w_out: float32 [2, 1024, 1024], P(None, 'tensor', 'batch'), may hold values from -1 to 1
- w_up: float32 [2, 1024, 4096], P(None, 'batch', 'tensor'), may hold values from -0.1875 to 0.1875
- up_bias: float32 [2, 4096], P(None, 'tensor'), may hold values from -1.8 to 1.8
- w_down: float32 [2, 4096, 1024], P(None, 'tensor', 'batch'), may hold values from -0.09375 to 0.09375
- gains: float32 [2, 2, 1024], replicated, may hold values from 0.5 to 1.5
- biases: float32 [2, 4, 1024], replicated, may hold values from -1.8 to 1.8
- first_qkv: float32 [2, 1024, 3, 1024], P(None, 'batch', None, 'tensor'), may hold values from -16 to 16
- second_qkv: float32 [2, 1024, 3, 1024], P(None, 'batch', None, 'tensor'), may hold values from 0.73728 to 2.94912
- first_head: float32 [2, 2, 1024], P(None, None, 'tensor'), may hold values from -16 to 16
- second_head: float32 [2, 2, 1024], P(None, None, 'tensor'), may hold values from 0.73728 to 2.94912
- first_out: float32 [2, 1024, 1024], P(None, 'tensor', 'batch'), may hold values from -6 to 6
- second_out: float32 [2, 1024, 1024], P(None, 'tensor', 'batch'), may hold values from 0.08192 to 0.32768
- first_up: float32 [2, 1024, 4096], P(None, 'batch', 'tensor'), may hold values from -16 to 16
- second_up: float32 [2, 1024, 4096], P(None, 'batch', 'tensor'), may hold values from 0.73728 to 2.94912
- first_up_bias: float32 [2, 4096], P(None, 'tensor'), may hold values from -16 to 16
- second_up_bias: float32 [2, 4096], P(None, 'tensor'), may hold values from 0.73728 to 2.94912
- first_down: float32 [2, 4096, 1024], P(None, 'tensor', 'batch'), may hold values from -24 to 24
- second_down: float32 [2, 4096, 1024], P(None, 'tensor', 'batch'), may hold values from 1.31072 to 5.24288
- first_gains: float32 [2, 2, 1024], replicated, may hold values from -32 to 32
- second_gains: float32 [2, 2, 1024], replicated, may hold values from 2.048 to 8.192
- first_biases: float32 [2, 4, 1024], replicated, may hold values from -32 to 32
- second_biases: float32 [2, 4, 1024], replicated, may hold values from 2.048 to 8.192
Outputs:
- layer_out: bfloat16 [8192, 1024], P('batch')
- grad_tokens: float32 [8192, 1024], P('batch')
- grad_qkv: float32 [2, 1024, 3, 1024], P(None, 'batch', None, 'tensor')
- first_qkv_new: float32 [2, 1024, 3, 1024], P(None, 'batch', None, 'tensor')
- second_qkv_new: float32 [2, 1024, 3, 1024], P(None, 'batch', None, 'tensor')
- new_qkv: float32 [2, 1024, 3, 1024], P(None, 'batch', None, 'tensor')
- grad_head: float32 [2, 2, 1024], P(None, None, 'tensor')
- first_head_new: float32 [2, 2, 1024], P(None, None, 'tensor')
- second_head_new: float32 [2, 2, 1024], P(None, None, 'tensor')
- new_head: float32 [2, 2, 1024], P(None, None, 'tensor')
- grad_out: float32 [2, 1024, 1024], P(None, 'tensor', 'batch')
- first_out_new: float32 [2, 1024, 1024], P(None, 'tensor', 'batch')
- second_out_new: float32 [2, 1024, 1024], P(None, 'tensor', 'batch')
- new_out: float32 [2, 1024, 1024], P(None, 'tensor', 'batch')
- grad_up: float32 [2, 1024, 4096], P(None, 'batch', 'tensor')
- first_up_new: float32 [2, 1024, 4096], P(None, 'batch', 'tensor')
- second_up_new: float32 [2, 1024, 4096], P(None, 'batch', 'tensor')
- new_up: float32 [2, 1024, 4096], P(None, 'batch', 'tensor')
- grad_up_bias: float32 [2, 4096], P(None, 'tensor')
- first_up_bias_new: float32 [2, 4096], P(None, 'tensor')
- second_up_bias_new: float32 [2, 4096], P(None, 'tensor')
- new_up_bias: float32 [2, 4096], P(None, 'tensor')
- grad_down: float32 [2, 4096, 1024], P(None, 'tensor', 'batch')
- first_down_new: float32 [2, 4096, 1024], P(None, 'tensor', 'batch')
- second_down_new: float32 [2, 4096, 1024], P(None, 'tensor', 'batch')
- new_down: float32 [2, 4096, 1024], P(None, 'tensor', 'batch')
- grad_gains: float32 [2, 2, 1024], replicated
- first_gains_new: float32 [2, 2, 1024], replicated
- second_gains_new: float32 [2, 2, 1024], replicated
- new_gains: float32 [2, 2, 1024], replicated
- grad_biases: float32 [2, 4, 1024], replicated
- first_biases_new: float32 [2, 4, 1024], replicated
- second_biases_new: float32 [2, 4, 1024], replicated
- new_biases: float32 [2, 4, 1024], replicated
The draws below stay inside these ranges and needn't reach their ends.
Inputs may be any that keep to these rules, and one draw needn't show every extreme that they name: `bucket_of`: each of the 4 buckets is held by 4 groups. A group with bucket b holds 2 ** b sequences, one in each slot of 512 >> b consecutive tokens. `seq_lens`: entry s of a group with bucket b is the length of the sequence in slot s: for s < 2 ** b it lies between half of the slot (rounded up) and the whole slot, and slot 0 is always full; entries for s >= 2 ** b are 0.
All inputs are finite; a program needn't handle non-finite values.
Results may differ from the reference program's by a relative error of at most 0.035.
Values may be sent and summed in bfloat16 or wider, within the bound.
A program may use at most 128 MiB of HBM per device.

```python
import math
import jax
import jax.numpy as jnp
from jax import lax

D = 1024
HEADS = 16
HEAD_DIM = 64
FF = 4096
LAYERS = 2
TOK_G = 512
BUCKETS = 4
STEP = 10
SLOTS = 8
GROUPS = 16
SPLITS = 8
TOKENS = 8192


def bucket_draw(key):
    return jax.random.permutation(key, jnp.arange(GROUPS, dtype=jnp.int32) % BUCKETS)


def draw_bucket_of(key, part):
    buckets = bucket_draw(key)
    return buckets.astype(jnp.int32)


def draw_seq_lens(key, part):
    buckets = bucket_draw(key)
    key = jax.random.fold_in(key, 2)
    slot_size = jnp.right_shift(jnp.int32(TOK_G), buckets)[:, None]
    upper_half = slot_size // 2 + 1
    raw_values = jax.random.randint(key, (GROUPS, SLOTS), 0, 1 << 20, dtype=jnp.int32)
    lengths_drawn = raw_values % upper_half + (slot_size - slot_size // 2)
    column = jnp.arange(SLOTS, dtype=jnp.int32)[None, :]
    lengths_drawn = jnp.where(column == 0, slot_size, lengths_drawn)
    in_use = column < jnp.left_shift(jnp.int32(1), buckets)[:, None]
    return jnp.where(in_use, lengths_drawn, 0).astype(jnp.int32)


def block_levels(key, dims, shards, low, high):
    def one(axis_at, blocks):
        draws = jax.random.uniform(jax.random.fold_in(jax.random.fold_in(key, 6), axis_at), (blocks,), jnp.float32, low / len(shards), high / len(shards))
        return jnp.repeat(jnp.exp(draws), dims[axis_at] // blocks).reshape((-1,) + (1,) * (len(dims) - axis_at - 1))

    loudness = one(*shards[0])
    for cut in shards[1:]:
        loudness = loudness * one(*cut)
    return loudness


def gaussian(key, dims, width, bound, shards=(), kind=jnp.bfloat16):
    array = width * jax.random.normal(key, dims, jnp.float32)
    if shards:
        array = array * block_levels(key, dims, shards, -0.22, 0.18)
    return jnp.clip(array, -bound, bound).astype(kind)


def setup_inputs(seed: int = 0) -> dict:
    key_of = jax.random.split(jax.random.key(seed), 29)
    tokens = gaussian(key_of[0], (TOKENS, D), 1.0, 6.0, ((0, 16),))
    cotangent = gaussian(key_of[1], (TOKENS, D), 1.0, 6.0, ((0, 16),))
    bucket_of = draw_bucket_of(jax.random.fold_in(key_of[28], 71), 0)
    seq_lens = draw_seq_lens(jax.random.fold_in(key_of[28], 71), 0)
    w_qkv = gaussian(key_of[4], (LAYERS, D, 3, D), D ** -0.5, 0.1875, ((1, 16), (3, 8)), jnp.float32)
    head_bias = gaussian(key_of[5], (LAYERS, 2, D), 0.2, 1.2, ((2, 8),), jnp.float32)
    w_out = gaussian(key_of[6], (LAYERS, D, D), (D * 16 // TOK_G) ** -0.5, 1.0, ((1, 8), (2, 16)), jnp.float32)
    w_up = gaussian(key_of[7], (LAYERS, D, FF), D ** -0.5, 0.1875, ((1, 16), (2, 8)), jnp.float32)
    up_bias = gaussian(key_of[8], (LAYERS, FF), 0.3, 1.8, ((1, 8),), jnp.float32)
    w_down = gaussian(key_of[9], (LAYERS, FF, D), FF ** -0.5, 0.09375, ((1, 8), (2, 16)), jnp.float32)
    gains = jnp.clip(1.0 + 0.1 * jax.random.normal(key_of[10], (LAYERS, 2, D), jnp.float32), 0.5, 1.5)
    biases = gaussian(key_of[11], (LAYERS, 4, D), 0.3, 1.8, (), jnp.float32)
    first_qkv = gaussian(key_of[12], (LAYERS, D, 3, D), (0.033 * TOKENS ** 0.5), 16.0, ((1, 16), (3, 8)), jnp.float32)
    second_qkv = jnp.clip(jnp.exp(math.log(2.94912) - 1.3862944 * jax.random.uniform(key_of[13], (LAYERS, D, 3, D), jnp.float32) ** block_levels(key_of[13], (LAYERS, D, 3, D), ((1, 16), (3, 8)), -0.2, 0.2)), 0.73728, 2.94912)
    first_head = gaussian(key_of[14], (LAYERS, 2, D), (0.033 * TOKENS ** 0.5), 16.0, ((2, 8),), jnp.float32)
    second_head = jnp.clip(jnp.exp(math.log(2.94912) - 1.3862944 * jax.random.uniform(key_of[15], (LAYERS, 2, D), jnp.float32) ** block_levels(key_of[15], (LAYERS, 2, D), ((2, 8),), -0.2, 0.2)), 0.73728, 2.94912)
    first_out = gaussian(key_of[16], (LAYERS, D, D), (0.011 * TOKENS ** 0.5), 6.0, ((1, 8), (2, 16)), jnp.float32)
    second_out = jnp.clip(jnp.exp(math.log(0.32768) - 1.3862944 * jax.random.uniform(key_of[17], (LAYERS, D, D), jnp.float32) ** block_levels(key_of[17], (LAYERS, D, D), ((1, 8), (2, 16)), -0.2, 0.2)), 0.08192, 0.32768)
    first_up = gaussian(key_of[18], (LAYERS, D, FF), (0.033 * TOKENS ** 0.5), 16.0, ((1, 16), (2, 8)), jnp.float32)
    second_up = jnp.clip(jnp.exp(math.log(2.94912) - 1.3862944 * jax.random.uniform(key_of[19], (LAYERS, D, FF), jnp.float32) ** block_levels(key_of[19], (LAYERS, D, FF), ((1, 16), (2, 8)), -0.2, 0.2)), 0.73728, 2.94912)
    first_up_bias = gaussian(key_of[20], (LAYERS, FF), (0.033 * TOKENS ** 0.5), 16.0, ((1, 8),), jnp.float32)
    second_up_bias = jnp.clip(jnp.exp(math.log(2.94912) - 1.3862944 * jax.random.uniform(key_of[21], (LAYERS, FF), jnp.float32) ** block_levels(key_of[21], (LAYERS, FF), ((1, 8),), -0.2, 0.2)), 0.73728, 2.94912)
    first_down = gaussian(key_of[22], (LAYERS, FF, D), (0.044 * TOKENS ** 0.5), 24.0, ((1, 8), (2, 16)), jnp.float32)
    second_down = jnp.clip(jnp.exp(math.log(5.24288) - 1.3862944 * jax.random.uniform(key_of[23], (LAYERS, FF, D), jnp.float32) ** block_levels(key_of[23], (LAYERS, FF, D), ((1, 8), (2, 16)), -0.2, 0.2)), 1.31072, 5.24288)
    first_gains = gaussian(key_of[24], (LAYERS, 2, D), (0.055 * TOKENS ** 0.5), 32.0, (), jnp.float32)
    second_gains = jnp.clip(jnp.exp(jax.random.uniform(key_of[25], (LAYERS, 2, D), jnp.float32, math.log(2.048), math.log(8.192))), 2.048, 8.192)
    first_biases = gaussian(key_of[26], (LAYERS, 4, D), (0.055 * TOKENS ** 0.5), 32.0, (), jnp.float32)
    second_biases = jnp.clip(jnp.exp(jax.random.uniform(key_of[27], (LAYERS, 4, D), jnp.float32, math.log(2.048), math.log(8.192))), 2.048, 8.192)
    return dict(tokens=tokens, cotangent=cotangent, bucket_of=bucket_of, seq_lens=seq_lens, w_qkv=w_qkv, head_bias=head_bias, w_out=w_out, w_up=w_up, up_bias=up_bias, w_down=w_down, gains=gains, biases=biases, first_qkv=first_qkv, second_qkv=second_qkv, first_head=first_head, second_head=second_head, first_out=first_out, second_out=second_out, first_up=first_up, second_up=second_up, first_up_bias=first_up_bias, second_up_bias=second_up_bias, first_down=first_down, second_down=second_down, first_gains=first_gains, second_gains=second_gains, first_biases=first_biases, second_biases=second_biases)


@jax.custom_vjp
def low(v):
    return lax.optimization_barrier(v.astype(jnp.bfloat16)).astype(jnp.float32)

@jax.custom_vjp
def low_back(v):
    return v

def low_keep(v):
    return (low(v), None)

def low_pass(kept, grad):
    return (grad,)

def back_keep(v):
    return (v, None)

def back_low(kept, grad):
    return (low(grad),)
low.defvjp(low_keep, low_pass)
low_back.defvjp(back_keep, back_low)
exact_mode = lax.Precision.HIGHEST
eps_norm = 1e-05
beta_one = 0.9
beta_two = 0.999
eps_adam = 1e-08
step_rate = 0.1
output_rate = 0.3
bias_rate = 0.3
gain_rate = 1.0
weight_decay = 0.01
masked_score = -1000000000.0

def both_ways(values):
    return low(low_back(values))

def token_masks(bucket, lengths):
    position = jnp.arange(TOK_G, dtype=jnp.int32)
    slot_size = jnp.right_shift(jnp.int32(TOK_G), bucket.astype(jnp.int32))
    slot_ids = position // slot_size
    within = position - slot_ids * slot_size
    match = slot_ids[:, None] == jnp.arange(SLOTS, dtype=jnp.int32)[None, :]
    length_at = lax.optimization_barrier(jnp.sum(jnp.where(match, lengths[None, :], 0), axis=1, dtype=jnp.int32))
    return (slot_ids, within < length_at)

def layer_norm(values, scale_row, shift_row):
    centred = values - lax.optimization_barrier(jnp.mean(values, axis=-1, keepdims=True))
    spread = lax.optimization_barrier(jnp.mean(centred * centred, axis=-1, keepdims=True))
    return centred * lax.rsqrt(spread + eps_norm) * scale_row + shift_row

def split_sum(mixture, weight):
    blocks = mixture.reshape(TOK_G, SPLITS, mixture.shape[1] // SPLITS)
    weight_blocks = low(weight).reshape(SPLITS, weight.shape[0] // SPLITS, weight.shape[1])
    terms = jnp.einsum('rtc,tcd->trd', blocks, weight_blocks, precision=exact_mode)
    return low_back(lax.optimization_barrier(jnp.sum(low(terms), axis=0)))

def group_forward(weights, row_values, slot_ids, valid):
    w_qkv, head_bias, w_out, w_up, up_bias, w_down, gains, biases = weights
    allowed = (slot_ids[:, None] == slot_ids[None, :]) & valid[None, :]
    score_scale = HEAD_DIM ** (-0.5)
    for layer_no in range(LAYERS):
        rows_low = low(row_values)
        projected = jnp.einsum('rd,dce->rce', rows_low, low(w_qkv[layer_no]), precision=exact_mode)
        queries = both_ways(projected[:, 0] + head_bias[layer_no, 0]).reshape(TOK_G, HEADS, HEAD_DIM)
        key_rows = both_ways(projected[:, 1]).reshape(TOK_G, HEADS, HEAD_DIM)
        value_rows = both_ways(projected[:, 2] + head_bias[layer_no, 1]).reshape(TOK_G, HEADS, HEAD_DIM)
        scores = low_back(jnp.einsum('qhe,khe->hqk', queries, key_rows, precision=exact_mode) * score_scale)
        scores = jnp.where(allowed[None], scores, masked_score)
        row_peak = lax.optimization_barrier(jnp.max(scores, axis=-1, keepdims=True))
        exponent = jnp.exp(scores - row_peak)
        attend = low(exponent / lax.optimization_barrier(jnp.sum(exponent, axis=-1, keepdims=True)))
        mixture = jnp.einsum('hqk,khe->qhe', attend, value_rows, precision=exact_mode)
        mixture = both_ways(mixture.reshape(TOK_G, D))
        summed = row_values + split_sum(mixture, w_out[layer_no]) + biases[layer_no, 0]
        normed = layer_norm(summed, gains[layer_no, 0], biases[layer_no, 1])
        normed_low = low(normed)
        hidden = low_back(jnp.dot(normed_low, low(w_up[layer_no]), precision=exact_mode, preferred_element_type=jnp.float32) + up_bias[layer_no])
        active = low(jax.nn.gelu(hidden, approximate=False))
        summed_two = normed + split_sum(active, w_down[layer_no]) + biases[layer_no, 2]
        row_values = layer_norm(summed_two, gains[layer_no, 1], biases[layer_no, 3])
    return row_values

def adam_step(weight, grad, first, second, with_decay, rate):
    first_new = beta_one * first + (1.0 - beta_one) * grad
    second_new = beta_two * second + (1.0 - beta_two) * grad * grad
    first_hat = first_new / (1.0 - beta_one ** STEP)
    second_hat = second_new / (1.0 - beta_two ** STEP)
    change = first_hat / (jnp.sqrt(second_hat) + eps_adam)
    if with_decay:
        change = change + weight_decay * weight
    return (first_new, second_new, weight - rate * change)

def reference(tokens, cotangent, bucket_of, seq_lens, w_qkv, head_bias, w_out, w_up, up_bias, w_down, gains, biases, first_qkv, second_qkv, first_head, second_head, first_out, second_out, first_up, second_up, first_up_bias, second_up_bias, first_down, second_down, first_gains, second_gains, first_biases, second_biases):
    slot_all, valid_all = jax.vmap(token_masks)(bucket_of, seq_lens)
    params = (w_qkv, head_bias, w_out, w_up, up_bias, w_down, gains, biases)

    def forward_all(weights, token_rows):

        def one_group(packed):
            group_rows, slot_ids, valid = packed
            return group_forward(weights, group_rows, slot_ids, valid)
        outputs = lax.map(jax.checkpoint(one_group), (token_rows.reshape(GROUPS, TOK_G, D), slot_all, valid_all))
        return outputs.reshape(TOKENS, D)
    layer_final, pullback = jax.vjp(forward_all, params, tokens.astype(jnp.float32))
    row_weight = valid_all.reshape(TOKENS, 1).astype(jnp.float32)
    grads, grad_tokens = pullback(cotangent.astype(jnp.float32) * row_weight)
    grad_qkv, grad_head, grad_out, grad_up, grad_up_bias, grad_down, grad_gains, grad_biases = grads
    first_qkv_new, second_qkv_new, new_qkv = adam_step(w_qkv, grad_qkv, first_qkv, second_qkv, True, step_rate)
    first_head_new, second_head_new, new_head = adam_step(head_bias, grad_head, first_head, second_head, False, bias_rate)
    first_out_new, second_out_new, new_out = adam_step(w_out, grad_out, first_out, second_out, True, output_rate)
    first_up_new, second_up_new, new_up = adam_step(w_up, grad_up, first_up, second_up, True, step_rate)
    first_up_bias_new, second_up_bias_new, new_up_bias = adam_step(up_bias, grad_up_bias, first_up_bias, second_up_bias, False, bias_rate)
    first_down_new, second_down_new, new_down = adam_step(w_down, grad_down, first_down, second_down, True, step_rate)
    first_gains_new, second_gains_new, new_gains = adam_step(gains, grad_gains, first_gains, second_gains, False, gain_rate)
    first_biases_new, second_biases_new, new_biases = adam_step(biases, grad_biases, first_biases, second_biases, False, bias_rate)
    return (layer_final.astype(jnp.bfloat16), grad_tokens, grad_qkv, first_qkv_new, second_qkv_new, new_qkv, grad_head, first_head_new, second_head_new, new_head, grad_out, first_out_new, second_out_new, new_out, grad_up, first_up_new, second_up_new, new_up, grad_up_bias, first_up_bias_new, second_up_bias_new, new_up_bias, grad_down, first_down_new, second_down_new, new_down, grad_gains, first_gains_new, second_gains_new, new_gains, grad_biases, first_biases_new, second_biases_new, new_biases)
```

```python
import jax
import jax.numpy as jnp
from jax import lax
from jax.experimental import pallas as pl
from jax.experimental.pallas import tpu as pltpu
from jax.sharding import Mesh
from jax.sharding import PartitionSpec as P

LAYERS = 2
STEP = 10
ROWS = 512
D = 1024
BLK = 128
OWN = 64

eps_norm = 1e-05
beta_one = 0.9
beta_two = 0.999
eps_adam = 1e-08
step_rate = 0.1
output_rate = 0.3
bias_rate = 0.3
gain_rate = 1.0
weight_decay = 0.01
masked_score = -1000000000.0

MESH = pl.DeviceIdType.MESH
BF = jnp.bfloat16
F32 = jnp.float32
NT = (((1,), (1,)), ((), ()))
TN = (((0,), (0,)), ((), ()))
NN = (((1,), (0,)), ((), ()))

SCRATCH = dict(
    XB=((2, ROWS, D), BF),
    HB=((2, ROWS, D), BF),
    DFB=((2, ROWS, D), BF),
    DSB=((2, ROWS, D), BF),
    WA=((2, D, 512), BF),
    WB=((2, D, 1024), BF),
    GA=((2, D, 512), BF),
    GB=((2, D, 1024), BF),
    GAR=((2, 16, 64, 512), BF),
    GBR=((2, 16, 64, 1024), BF),
    QKV=((2, ROWS, 384), BF),
    O=((2, ROWS, 128), BF),
    PR=((2, 4, 2 * BLK, ROWS), F32),
    A=((2, ROWS, 512), BF),
    GP=((2, ROWS, 512), F32),
    DU=((ROWS, 512), BF),
    DQKV=((ROWS, 384), BF),
    DK=((ROWS, 128), F32),
    DV=((ROWS, 128), F32),
    PART=((4, BLK, D), BF),
    SND=((4, OWN, D), BF),
    CR=((8, 4, OWN, D), BF),
    XR=((8, 4, OWN, D), BF),
    OWNSUM=((OWN, D), F32),
    RES=((OWN, D), F32),
    XH=((4, OWN, D), F32),
    SC=((4, OWN, 128), F32),
    COT=((OWN, D), BF),
    QS=((ROWS, 128), F32),
    KC=((8, ROWS), F32),
    BIAS=((8, 512), F32),
    LOB=((ROWS, D), BF),
    GTB=((ROWS, D), BF),
    FIN=((2, OWN, D), BF),
    COL=((8, 512), F32),
    CB=((16, 8, 512), F32),
    ROWP=((8, 16, 128), F32),
    RA=((8, 16, 128), F32),
    RS1=((16, 128), F32),
    RB=((16, 16, 128), F32),
    RS2=((16, 128), F32),
    RC=((8, 16, 128), F32),
)
SEMS = dict(
    ws=(4, 16), wr=(4, 16), gs=(4, 16), gr=(4, 16),
    cs=(8, 4), cr=(8, 4), xs=(8, 4), xr=(8, 4),
    axs=(7, 4), axr=(7, 4), acs=(7, 4), acr=(7, 4),
    fs=(2, 8), fr=(2, 8), ras=(8,), rar=(8,), rbs=(16,), rbr=(16,),
    rcs=(8,), rcr=(8,), cbs=(16,), cbr=(16,), ms=(8,), mr=(8,),
)
N_IN, N_OUT = 8, 6


class Refs:
    pass


def loop(n, body):
    def step(k, carry):
        body(k)
        return carry

    lax.fori_loop(0, n, step, 0)


def gray(k):
    return k + lax.div(k, 2) - 2 * lax.div(k, 3)


def dot(a, b, dims=NN):
    return lax.dot_general(a, b, dims, preferred_element_type=F32)


def kernel(*refs):
    tok, cot, qs_in, kc_in, pa, pb, bias_in, gb = refs[:N_IN]
    lo_out, gt_out, ga_out, gbm_out, col_out, row_out = refs[N_IN : N_IN + N_OUT]
    r = Refs()
    for name, ref in zip(list(SCRATCH) + list(SEMS), refs[N_IN + N_OUT :], strict=True):
        setattr(r, name, ref)

    y, zl, c = lax.axis_index("y"), lax.axis_index("zl"), lax.axis_index("core")
    x, zh = lax.axis_index("x"), lax.axis_index("zh")
    z = zh * 2 + zl
    s_me = y * 4 + z
    b_me = y * 4 + zl * 2 + c
    t_me = x * 2 + c
    home = c == zh
    away = c != zh
    sib = (y, zl, 1 - c, x, zh)

    def xdev(j):
        return (y, zl, c, j, zh)

    def out_dev(i):
        zz = lax.rem(i, 4)
        return (lax.div(i, 4), lax.rem(zz, 2), zh, x, lax.div(zz, 2))

    def in_dev(i):
        return (lax.div(i, 4), lax.rem(lax.div(i, 2), 2), lax.rem(i, 2), x, c)

    def remote(src, dst, ss, rs, dev):
        return pltpu.make_async_remote_copy(
            src_ref=src, dst_ref=dst, send_sem=ss, recv_sem=rs, device_id=dev, device_id_type=MESH
        )

    def got(dst, sem):
        remote(dst, dst, sem, sem, sib).wait_recv()

    def sent(src, sem):
        remote(src, src, sem, sem, sib).wait_send()

    def tile(at, size):
        return pl.ds(pl.multiple_of(at * size, size), size)

    def rows_of(j, core):
        return tile(j * 2 + core, OWN)

    bar = pltpu.get_barrier_semaphore()

    def greet(dev):
        pl.semaphore_signal(bar, inc=1, device_id=dev, device_id_type=MESH)

    def greet_plane(i):
        cc, rest = lax.rem(i, 2), lax.div(i, 2)
        hh, xx = lax.rem(rest, 2), lax.div(rest, 2)

        @pl.when(jnp.logical_not((cc == c) & (hh == zh) & (xx == x)))
        def _():
            greet((y, zl, cc, xx, hh))

    loop(16, greet_plane)

    def greet_yz(i):
        @pl.when(jnp.logical_not(home & (i == s_me)))
        def _():
            greet(out_dev(i))

        @pl.when(jnp.logical_not(home & (i == b_me)))
        def _():
            greet(in_dev(i))

    loop(16, greet_yz)

    @pl.when(home)
    def _():
        pl.semaphore_wait(bar, 45)

    @pl.when(away)
    def _():
        pl.semaphore_wait(bar, 47)

    def w_refs(lp):
        layer, part = divmod(lp, 2)
        return ((pa, r.WA) if part == 0 else (pb, r.WB)) + (layer,)

    def w_send(lp):
        src, dst, layer = w_refs(lp)

        def one(k):
            i = lax.rem(s_me + k, 16)
            here = dst.at[layer, tile(b_me, 64)]
            local = home & (k == 0)

            @pl.when(local)
            def _():
                pltpu.make_async_copy(src.at[layer], here, r.wr.at[lp, b_me]).start()

            @pl.when(jnp.logical_not(local))
            def _():
                remote(src.at[layer], here, r.ws.at[lp, i], r.wr.at[lp, b_me], out_dev(i)).start()

        loop(16, one)

    def w_wait(lp):
        src, dst, layer = w_refs(lp)
        loop(16, lambda i: got(dst.at[layer, tile(i, 64)], r.wr.at[lp, i]))

    def w_done(lp):
        src, dst, layer = w_refs(lp)

        def one(k):
            i = lax.rem(s_me + k, 16)

            @pl.when(jnp.logical_not(home & (k == 0)))
            def _():
                sent(src.at[layer], r.ws.at[lp, i])

        loop(16, one)

    def g_refs(lp):
        layer, part = divmod(lp, 2)
        return ((r.GA, r.GAR) if part == 0 else (r.GB, r.GBR)) + (layer,)

    def g_send(lp):
        src, dst, layer = g_refs(lp)

        def one(k):
            i = lax.rem(b_me + k, 16)
            block = src.at[layer, tile(i, 64)]
            there = dst.at[layer, s_me]
            local = home & (k == 0)

            @pl.when(local)
            def _():
                pltpu.make_async_copy(block, there, r.gr.at[lp, s_me]).start()

            @pl.when(jnp.logical_not(local))
            def _():
                remote(block, there, r.gs.at[lp, i], r.gr.at[lp, s_me], in_dev(i)).start()

        loop(16, one)

    def g_sum(lp, out):
        src, dst, layer = g_refs(lp)
        out[layer] = jnp.zeros(out.shape[1:], F32)

        def one(i):
            got(dst.at[layer, i], r.gr.at[lp, i])
            out[layer] += dst[layer, i].astype(F32)

        loop(16, one)

    def g_done(lp):
        src, dst, layer = g_refs(lp)

        def one(k):
            i = lax.rem(b_me + k, 16)

            @pl.when(jnp.logical_not(home & (k == 0)))
            def _():
                sent(src.at[layer, tile(i, 64)], r.gs.at[lp, i])

        loop(16, one)

    def ag_start(s, buf):
        own = buf.at[rows_of(x, c)]
        remote(own, own, r.acs.at[s, x], r.acr.at[s, x], sib).start()
        for d in (2, 1, 3):
            j = lax.rem(x + d, 4)
            remote(own, own, r.axs.at[s, j], r.axr.at[s, x], xdev(j)).start()

    def ag_forward(s, buf, j):
        part = buf.at[rows_of(j, c)]
        got(part, r.axr.at[s, j])
        remote(part, part, r.acs.at[s, j], r.acr.at[s, j], sib).start()

    def ag_done(s, buf):
        own = buf.at[rows_of(x, c)]
        for d in (1, 2, 3):
            j = lax.rem(x + d, 4)
            sent(own, r.axs.at[s, j])
        loop(4, lambda j: sent(buf.at[rows_of(j, c)], r.acs.at[s, j]))

    def near(k):
        return lax.rem(x + gray(k), 4)

    def ag_loop(s, buf, body):
        def one(k):
            j = near(k)
            got(buf.at[rows_of(j, 1 - c)], r.acr.at[s, j])
            body(k, j)

            @pl.when(k == 0)
            def _():
                ag_forward(s, buf, near(1))
                ag_forward(s, buf, near(2))

            @pl.when(k == 1)
            def _():
                ag_forward(s, buf, near(3))

        loop(4, one)

    def rs_push(s, j, part):
        r.PART[j] = part.astype(BF)
        remote(
            r.PART.at[j, tile(1 - c, OWN)], r.CR.at[s, j], r.cs.at[s, j], r.cr.at[s, j], sib
        ).start()

    def rs_comb(s, j):
        got(r.CR.at[s, j], r.cr.at[s, j])
        both = r.PART[j, tile(c, OWN), :].astype(F32) + r.CR[s, j].astype(F32)

        @pl.when(j == x)
        def _():
            r.OWNSUM[...] = both

        @pl.when(j != x)
        def _():
            r.SND[j] = both.astype(BF)
            remote(r.SND.at[j], r.XR.at[s, x], r.xs.at[s, j], r.xr.at[s, x], xdev(j)).start()

    def rs_finish(s):
        total = r.OWNSUM[...]
        for d in (1, 3, 2):
            j = lax.rem(x + d, 4)
            got(r.XR.at[s, j], r.xr.at[s, j])
            total = total + r.XR[s, j].astype(F32)
        return total

    def rs_done(s):
        for d in (1, 2, 3):
            j = lax.rem(x + d, 4)
            sent(r.SND.at[j], r.xs.at[s, j])
        loop(4, lambda j: sent(r.PART.at[j, tile(1 - c, OWN)], r.cs.at[s, j]))

    def gb_row(layer, n):
        return gb[layer * 6 + n : layer * 6 + n + 1, :]

    def norm(values, n, gain, shift):
        centred = values - jnp.mean(values, axis=-1, keepdims=True)
        scale = lax.rsqrt(jnp.mean(centred * centred, axis=-1, keepdims=True) + eps_norm)
        hat = centred * scale
        r.XH[n] = hat
        r.SC[n] = jnp.broadcast_to(scale, (OWN, 128))
        return hat * gain + shift

    def row_part(row, vec):
        for p in range(8):
            r.ROWP[p, row : row + 1, :] = vec[:, p * 128 : (p + 1) * 128]

    def norm_back(dy, n, layer, which):
        hat = r.XH[n]
        scale = r.SC[n][:, 0:1]
        dyg = dy * gb_row(layer, which)
        one = jnp.mean(dyg, axis=-1, keepdims=True)
        two = jnp.mean(dyg * hat, axis=-1, keepdims=True)
        dz = scale * (dyg - one - hat * two)
        base = layer * 6
        row_part(base + which, jnp.sum(dy * hat, axis=0, keepdims=True))
        row_part(base + 3 + 2 * which, jnp.sum(dy, axis=0, keepdims=True))
        row_part(base + 2 + 2 * which, jnp.sum(dz, axis=0, keepdims=True))
        return dz

    own_rows = rows_of(x, c)
    lane = lax.broadcasted_iota(jnp.int32, (BLK, 128), 1)
    low_half = lane < 64

    def two_heads(v):
        zero = jnp.zeros_like(v)
        return jnp.concatenate(
            [jnp.where(low_half, v, zero), jnp.where(low_half, zero, v)], axis=0
        )

    def one_row(v):
        return jnp.where(low_half, v[:BLK], v[BLK:])

    w_send(0)

    @pl.when(home)
    def _():
        other = rows_of(x, 1 - c)
        for n, (src, dst) in enumerate(
            ((tok, r.XB.at[0]), (qs_in, r.QS), (kc_in, r.KC), (bias_in, r.BIAS))
        ):
            pltpu.make_async_copy(src, dst, r.mr.at[n]).start()
            if n < 3:
                remote(src, dst, r.ms.at[n], r.mr.at[n], sib).start()
        pltpu.make_async_copy(cot.at[own_rows], r.COT, r.mr.at[4]).start()
        remote(cot.at[other], r.COT, r.ms.at[4], r.mr.at[4], sib).start()

    @pl.when(away)
    def _():
        remote(bias_in, r.BIAS, r.ms.at[3], r.mr.at[3], (y, zl, zh, x, c)).start()

    for n, dst in enumerate((r.XB.at[0], r.QS, r.KC, r.BIAS, r.COT)):
        got(dst, r.mr.at[n])

    for layer in range(LAYERS):
        wa, wb = r.WA.at[layer], r.WB.at[layer]
        qkv = r.QKV.at[layer]
        w_wait(2 * layer)
        if layer == 0:
            w_send(1)

        def project(k, j, layer=layer, wa=wa, qkv=qkv):
            at = tile(j, BLK)
            out = dot(r.XB[layer, at, :], wa[:, 0:384]) + r.BIAS[4 * layer : 4 * layer + 1, 0:384]
            qkv[at, :] = out.astype(BF)

        if layer == 0:
            loop(4, lambda k: project(k, k))
        else:
            ag_loop(1, r.XB.at[1], project)
            w_send(3)

        s = 2 * layer

        def attend(k, layer=layer, wa=wa, qkv=qkv, s=s):
            j = near(3 - k)
            at = tile(j, BLK)
            score = dot(two_heads(qkv[at, 0:128]), qkv[:, 128:256], NT) * 0.125
            allowed = r.QS[at, 0:1] == r.KC[0:1, :]
            score = jnp.where(jnp.concatenate([allowed, allowed], axis=0), score, masked_score)
            weight = jnp.exp(score - jnp.max(score, axis=-1, keepdims=True))
            prob = weight * (1.0 / jnp.sum(weight, axis=-1, keepdims=True))
            r.PR[layer, j] = prob
            mixed = one_row(dot(prob.astype(BF), qkv[:, 256:384])).astype(BF)
            r.O[layer, at, :] = mixed
            rs_push(s, j, dot(mixed, wa[:, 384:512], NT))

            @pl.when(k > 0)
            def _():
                rs_comb(s, near(4 - k))

        loop(4, attend)
        rs_comb(s, near(0))
        stream = r.XB[0, own_rows, :].astype(F32) if layer == 0 else r.RES[...]
        z_one = rs_finish(s) + stream + gb_row(layer, 2)
        h_val = norm(z_one, 2 * layer, gb_row(layer, 0), gb_row(layer, 3))
        r.RES[...] = h_val
        r.HB[layer, own_rows, :] = h_val.astype(BF)
        ag_start(2 * layer, r.HB.at[layer])
        rs_done(s)
        w_wait(2 * layer + 1)
        if layer == 0:
            w_send(2)

        s = 2 * layer + 1

        def feed(k, j, layer=layer, wb=wb, s=s):
            at = tile(j, BLK)
            u = dot(r.HB[layer, at, :], wb[:, 0:512]) + r.BIAS[4 * layer + 1 : 4 * layer + 2, :]
            phi = 0.5 * (1.0 + lax.erf(u * 0.7071067811865476))
            r.GP[layer, at, :] = phi + u * jnp.exp(-0.5 * u * u) * 0.3989422804014327
            act = (u * phi).astype(BF)
            r.A[layer, at, :] = act
            rs_push(s, j, dot(act, wb[:, 512:1024], NT))

            @pl.when(k > 0)
            def _():
                rs_comb(s, near(k - 1))

        ag_loop(2 * layer, r.HB.at[layer], feed)
        rs_comb(s, near(3))
        z_two = rs_finish(s) + r.RES[...] + gb_row(layer, 4)
        x_val = norm(z_two, 2 * layer + 1, gb_row(layer, 1), gb_row(layer, 5))
        if layer == 0:
            r.RES[...] = x_val
            r.XB[1, own_rows, :] = x_val.astype(BF)
            ag_start(1, r.XB.at[1])
        else:
            r.FIN[0] = x_val.astype(BF)
        rs_done(s)

    def f_send(n, buf):
        def one(k):
            xx, hh = lax.div(k, 2), lax.rem(k, 2)
            self = home & (xx == x) & (hh == zh)
            there = buf.at[own_rows]

            @pl.when(self)
            def _():
                pltpu.make_async_copy(r.FIN.at[n], there, r.fr.at[n, t_me]).start()

            @pl.when(jnp.logical_not(self))
            def _():
                remote(
                    r.FIN.at[n], there, r.fs.at[n, k], r.fr.at[n, t_me], (y, zl, zh, xx, hh)
                ).start()

        loop(8, one)

    def f_wait(n, buf):
        loop(8, lambda t: got(buf.at[tile(t, OWN)], r.fr.at[n, t]))

    def f_done(n):
        def one(k):
            @pl.when(jnp.logical_not(home & (lax.div(k, 2) == x) & (lax.rem(k, 2) == zh)))
            def _():
                sent(r.FIN.at[n], r.fs.at[n, k])

        loop(8, one)

    r.ROWP[...] = jnp.zeros_like(r.ROWP)
    r.COL[...] = jnp.zeros_like(r.COL)
    dy = r.COT[...].astype(F32)
    for layer in (1, 0):
        wa, wb = r.WA.at[layer], r.WB.at[layer]
        qkv = r.QKV.at[layer]
        ag_a, ag_b = (3, 4) if layer == 1 else (5, 6)
        dz = norm_back(dy, 2 * layer + 1, layer, 1)
        r.RES[...] = dz
        r.DFB[layer, own_rows, :] = dz.astype(BF)
        ag_start(ag_a, r.DFB.at[layer])
        if layer == 1:
            f_send(0, r.LOB)

        s = 4 + 2 * (1 - layer)

        def feed_back(k, j, layer=layer, wb=wb, s=s):
            at = tile(j, BLK)
            da = dot(r.DFB[layer, at, :], wb[:, 512:1024])
            du = (da * r.GP[layer, at, :]).astype(BF)
            r.DU[at, :] = du
            up_row = 4 * layer + 1
            r.COL[up_row : up_row + 1, :] += jnp.sum(du.astype(F32), axis=0, keepdims=True)
            rs_push(s, j, dot(du, wb[:, 0:512], NT))

            @pl.when(k > 0)
            def _():
                rs_comb(s, near(k - 1))

        ag_loop(ag_a, r.DFB.at[layer], feed_back)
        rs_comb(s, near(3))

        def grad_b(t, layer=layer):
            at = tile(t, 256)
            r.GB[layer, at, 0:512] = dot(r.HB[layer, :, at], r.DU[...], TN).astype(BF)
            r.GB[layer, at, 512:1024] = dot(r.DFB[layer, :, at], r.A[layer], TN).astype(BF)

        loop(4, grad_b)
        g_send(2 * layer + 1)

        dh = rs_finish(s) + r.RES[...]
        dz = norm_back(dh, 2 * layer, layer, 0)
        r.RES[...] = dz
        r.DSB[layer, own_rows, :] = dz.astype(BF)
        ag_start(ag_b, r.DSB.at[layer])
        rs_done(s)
        if layer == 0:
            def ra_send(k):
                cc, xx = lax.rem(k, 2), lax.div(k, 2)

                @pl.when(k == t_me)
                def _():
                    pltpu.make_async_copy(r.ROWP.at[k], r.RA.at[k], r.rar.at[k]).start()

                @pl.when(k != t_me)
                def _():
                    remote(
                        r.ROWP.at[k], r.RA.at[t_me], r.ras.at[k], r.rar.at[t_me],
                        (y, zl, cc, xx, zh),
                    ).start()

            loop(8, ra_send)

        r.DK[...] = jnp.zeros_like(r.DK)
        r.DV[...] = jnp.zeros_like(r.DV)

        def attend_back(k, j, layer=layer, wa=wa, qkv=qkv):
            at = tile(j, BLK)
            do = two_heads(dot(r.DSB[layer, at, :], wa[:, 384:512]).astype(BF))
            prob = r.PR[layer, j]
            dp = dot(do, qkv[:, 256:384], NT)
            inner = jnp.sum(prob * dp, axis=-1, keepdims=True)
            dscore = (prob * (dp - inner)).astype(BF)
            dq = one_row(dot(dscore, qkv[:, 128:256])) * 0.125
            r.DQKV[at, 0:128] = dq.astype(BF)
            r.DK[...] += dot(dscore, two_heads(qkv[at, 0:128]), TN)
            r.DV[...] += dot(prob.astype(BF), do, TN)

        ag_loop(ag_b, r.DSB.at[layer], attend_back)
        r.DQKV[:, 128:256] = (r.DK[...] * 0.125).astype(BF)
        r.DQKV[:, 256:384] = r.DV[...].astype(BF)
        s += 1

        def input_back(k, wa=wa, s=s):
            j = near(3 - k)
            rs_push(s, j, dot(r.DQKV[tile(j, BLK), :], wa[:, 0:384], NT))

            @pl.when(k > 0)
            def _():
                rs_comb(s, near(4 - k))

        loop(4, input_back)
        rs_comb(s, near(0))

        def grad_a(t, layer=layer):
            at = tile(t, 256)
            r.GA[layer, at, 0:384] = dot(r.XB[layer, :, at], r.DQKV[...], TN).astype(BF)
            r.GA[layer, at, 384:512] = dot(r.DSB[layer, :, at], r.O[layer], TN).astype(BF)

        loop(4, grad_a)
        g_send(2 * layer)
        r.COL[4 * layer : 4 * layer + 1, 0:384] = jnp.sum(
            r.DQKV[...].astype(F32), axis=0, keepdims=True
        )
        if layer == 0:
            def spread(src, dst, ss, rs):
                def one(k):
                    i = lax.rem(b_me + k, 16)
                    local = home & (k == 0)

                    @pl.when(local)
                    def _():
                        pltpu.make_async_copy(src, dst.at[s_me], rs.at[s_me]).start()

                    @pl.when(jnp.logical_not(local))
                    def _():
                        remote(src, dst.at[s_me], ss.at[i], rs.at[s_me], in_dev(i)).start()

                loop(16, one)

            def spread_done(src, ss):
                def one(k):
                    i = lax.rem(b_me + k, 16)

                    @pl.when(jnp.logical_not(home & (k == 0)))
                    def _():
                        sent(src, ss.at[i])

                loop(16, one)

            spread(r.COL, r.CB, r.cbs, r.cbr)
            r.RS1[...] = jnp.zeros_like(r.RS1)

            def ra_sum(t):
                got(r.RA.at[t], r.rar.at[t])
                r.RS1[...] += r.RA[t]

            loop(8, ra_sum)
            spread(r.RS1, r.RB, r.rbs, r.rbr)
        dy = rs_finish(s) + r.RES[...]
        rs_done(s)

    r.FIN[1] = dy.astype(BF)
    f_send(1, r.GTB)

    r.RS2[...] = jnp.zeros_like(r.RS2)

    def rb_sum(i):
        got(r.RB.at[i], r.rbr.at[i])
        r.RS2[...] += r.RB[i]

    loop(16, rb_sum)
    h_me = x * 2 + zh

    def rc_send(k):
        hh, xx = lax.rem(k, 2), lax.div(k, 2)

        @pl.when(k == h_me)
        def _():
            pltpu.make_async_copy(r.RS2, r.RC.at[k], r.rcr.at[k]).start()

        @pl.when(k != h_me)
        def _():
            remote(r.RS2, r.RC.at[h_me], r.rcs.at[k], r.rcr.at[h_me], (y, zl, c, xx, hh)).start()

    loop(8, rc_send)

    g_sum(3, gbm_out)
    g_sum(2, ga_out)
    g_sum(1, gbm_out)
    f_wait(0, r.LOB)
    lo_out[...] = r.LOB[...]
    g_sum(0, ga_out)
    col_out[...] = jnp.zeros_like(col_out)

    def cb_sum(i):
        got(r.CB.at[i], r.cbr.at[i])
        col_out[...] += r.CB[i]

    loop(16, cb_sum)
    loop(8, lambda t: got(r.RC.at[t], r.rcr.at[t]))
    row_out[...] = r.RC[...]
    f_wait(1, r.GTB)
    gt_out[...] = r.GTB[...].astype(F32)

    for lp in range(4):
        w_done(lp)
        g_done(lp)
    for s, buf in enumerate(
        (r.HB.at[0], r.XB.at[1], r.HB.at[1], r.DFB.at[1], r.DSB.at[1], r.DFB.at[0], r.DSB.at[0])
    ):
        ag_done(s, buf)
    f_done(0)
    f_done(1)
    spread_done(r.COL, r.cbs)
    spread_done(r.RS1, r.rbs)

    def small_done(k):
        @pl.when(k != t_me)
        def _():
            sent(r.ROWP.at[k], r.ras.at[k])

        @pl.when(k != h_me)
        def _():
            sent(r.RS2, r.rcs.at[k])

    loop(8, small_done)

    @pl.when(home)
    def _():
        for n, src in enumerate((tok, qs_in, kc_in)):
            sent(src, r.ms.at[n])
        sent(r.COT, r.ms.at[4])

    @pl.when(away)
    def _():
        sent(bias_in, r.ms.at[3])


def token_masks(bucket, lengths, row_count):
    position = jnp.arange(row_count, dtype=jnp.int32)
    slot_size = jnp.right_shift(jnp.int32(row_count), bucket)
    slot_ids = position // slot_size
    within = position - slot_ids * slot_size
    match = slot_ids[:, None] == jnp.arange(lengths.shape[0], dtype=jnp.int32)[None, :]
    length_at = jnp.sum(jnp.where(match, lengths[None, :], 0), axis=1, dtype=jnp.int32)
    return (slot_ids, within < length_at)


def adam_step(weight, grad, first, second, with_decay, rate):
    first_new = beta_one * first + (1.0 - beta_one) * grad
    second_new = beta_two * second + (1.0 - beta_two) * grad * grad
    first_hat = first_new / (1.0 - beta_one**STEP)
    second_hat = second_new / (1.0 - beta_two**STEP)
    change = first_hat / (jnp.sqrt(second_hat) + eps_adam)
    if with_decay:
        change = change + weight_decay * weight
    return (first_new, second_new, weight - rate * change)


def local(
    tokens, cotangent, bucket_of, seq_lens, w_qkv, head_bias, w_out, w_up, up_bias, w_down, gains,
    biases, first_qkv, second_qkv, first_head, second_head, first_out, second_out, first_up,
    second_up, first_up_bias, second_up_bias, first_down, second_down, first_gains, second_gains,
    first_biases, second_biases,
):
    slot_ids, valid = token_masks(bucket_of[0], seq_lens[0], ROWS)
    masked = jnp.where(valid[:, None], cotangent, jnp.zeros_like(cotangent))
    slot_f = slot_ids.astype(F32)
    q_slot = jnp.broadcast_to(slot_f[:, None], (ROWS, 128))
    k_code = jnp.broadcast_to(jnp.where(valid, slot_f, -1.0)[None, :], (8, ROWS))
    pack_a = jnp.concatenate(
        [w_qkv.reshape(2, 64, 384), jnp.swapaxes(w_out, 1, 2)], axis=-1
    ).astype(BF)
    pack_b = jnp.concatenate([w_up, jnp.swapaxes(w_down, 1, 2)], axis=-1).astype(BF)
    bias_rows = []
    for layer in range(LAYERS):
        zero = jnp.zeros((128,), F32)
        bias_rows.append(jnp.concatenate([head_bias[layer, 0], zero, head_bias[layer, 1], zero]))
        bias_rows += [up_bias[layer], jnp.zeros((512,), F32), jnp.zeros((512,), F32)]
    bias_pack = jnp.stack(bias_rows)
    gb_pack = jnp.concatenate(
        [gains[0], biases[0], gains[1], biases[1], jnp.zeros((4, D), F32)], axis=0
    )
    vmem = pl.BlockSpec(memory_space=pltpu.VMEM)
    layer_out, grad_tokens, ga, gbm, col, row = pl.pallas_call(
        kernel,
        out_shape=(
            jax.ShapeDtypeStruct((ROWS, D), BF),
            jax.ShapeDtypeStruct((ROWS, D), F32),
            jax.ShapeDtypeStruct((2, 64, 512), F32),
            jax.ShapeDtypeStruct((2, 64, 1024), F32),
            jax.ShapeDtypeStruct((8, 512), F32),
            jax.ShapeDtypeStruct((8, 16, 128), F32),
        ),
        in_specs=[vmem] * N_IN,
        out_specs=(vmem,) * N_OUT,
        scratch_shapes=[pltpu.VMEM(s, t) for s, t in SCRATCH.values()]
        + [pltpu.SemaphoreType.DMA(s) for s in SEMS.values()],
        compiler_params=pltpu.CompilerParams(
            collective_id=0, has_side_effects=True, vmem_limit_bytes=63 << 20
        ),
    )(tokens, masked, q_slot, k_code, pack_a, pack_b, bias_pack, gb_pack)
    grad_qkv = ga[:, :, 0:384].reshape(2, 64, 3, 128)
    grad_out = jnp.swapaxes(ga[:, :, 384:512], 1, 2)
    grad_up = gbm[:, :, 0:512]
    grad_down = jnp.swapaxes(gbm[:, :, 512:1024], 1, 2)
    col = col.reshape(2, 4, 512)
    grad_head = jnp.stack([col[:, 0, 0:128], col[:, 0, 256:384]], axis=1)
    grad_up_bias = col[:, 1, :]
    row = jnp.swapaxes(row, 0, 1).reshape(16, D)[0:12].reshape(2, 6, D)
    grad_gains = row[:, 0:2]
    grad_biases = row[:, 2:6]
    return (
        layer_out,
        grad_tokens,
        grad_qkv, *adam_step(w_qkv, grad_qkv, first_qkv, second_qkv, True, step_rate),
        grad_head, *adam_step(head_bias, grad_head, first_head, second_head, False, bias_rate),
        grad_out, *adam_step(w_out, grad_out, first_out, second_out, True, output_rate),
        grad_up, *adam_step(w_up, grad_up, first_up, second_up, True, step_rate),
        grad_up_bias,
        *adam_step(up_bias, grad_up_bias, first_up_bias, second_up_bias, False, bias_rate),
        grad_down, *adam_step(w_down, grad_down, first_down, second_down, True, step_rate),
        grad_gains, *adam_step(gains, grad_gains, first_gains, second_gains, False, gain_rate),
        grad_biases, *adam_step(biases, grad_biases, first_biases, second_biases, False, bias_rate),
    )


def solution(mesh):
    fine = Mesh(mesh.devices.reshape(4, 2, 2, 4, 2), ("y", "zl", "core", "x", "zh"))
    b, t = ("y", "zl", "core"), ("x", "zh")
    qkv, head = P(None, b, None, t), P(None, None, t)
    out, up, up_bias, down, rep = P(None, t, b), P(None, b, t), P(None, t), P(None, t, b), P()
    in_specs = (
        P(b, None), P(b, None), P(b), P(b, None), qkv, head, out, up, up_bias, down, rep, rep,
        qkv, qkv, head, head, out, out, up, up, up_bias, up_bias, down, down, rep, rep, rep, rep,
    )
    out_specs = (P(b, None), P(b, None))
    for spec in (qkv, head, out, up, up_bias, down, rep, rep):
        out_specs += (spec,) * 4
    return jax.shard_map(
        local, mesh=fine, in_specs=in_specs, out_specs=out_specs, check_vma=False
    )
```

```python
import jax
import jax.numpy as jnp
from jax import lax
from jax.experimental import pallas as pl
from jax.experimental.pallas import tpu as pltpu
from jax.sharding import Mesh
from jax.sharding import PartitionSpec as P

LAYERS = 2
STEP = 10
ROWS = 512
D = 1024
BLK = 128
HALF = 256
OWN = 32

eps_norm = 1e-05
beta_one = 0.9
beta_two = 0.999
eps_adam = 1e-08
step_rate = 0.1
output_rate = 0.3
bias_rate = 0.3
gain_rate = 1.0
weight_decay = 0.01
masked_score = -1000000000.0

MESH = pl.DeviceIdType.MESH
BF = jnp.bfloat16
F32 = jnp.float32
NT = (((1,), (1,)), ((), ()))
TN = (((0,), (0,)), ((), ()))
NN = (((1,), (0,)), ((), ()))

SCRATCH = dict(
    XB=((2, ROWS, D), BF),
    HB=((2, ROWS, D), BF),
    DFB=((2, ROWS, D), BF),
    DSB=((2, ROWS, D), BF),
    WAY=((2, 4, 4, 64, 256), BF),
    WAZ=((2, 4, 4, 64, 256), BF),
    WBY=((2, 4, 4, 64, 512), BF),
    WBZ=((2, 4, 4, 64, 512), BF),
    SYA=((2, 4, 64, 256), BF),
    SYB=((2, 4, 64, 512), BF),
    GAY=((2, 4, 4, 64, 256), BF),
    GAZ=((2, 4, 4, 64, 256), BF),
    GBY=((2, 4, 4, 64, 512), BF),
    GBZ=((2, 4, 4, 64, 512), BF),
    R1AY=((2, 4, 4, 64, 256), BF),
    R1AZ=((2, 4, 4, 64, 256), BF),
    R1BY=((2, 4, 4, 64, 512), BF),
    R1BZ=((2, 4, 4, 64, 512), BF),
    S2AY=((2, 4, 64, 256), BF),
    S2AZ=((2, 4, 64, 256), BF),
    S2BY=((2, 4, 64, 512), BF),
    S2BZ=((2, 4, 64, 512), BF),
    R2AY=((2, 4, 64, 256), BF),
    R2AZ=((2, 4, 64, 256), BF),
    R2BY=((2, 4, 64, 512), BF),
    R2BZ=((2, 4, 64, 512), BF),
    QKV=((2, ROWS, 384), BF),
    O=((2, ROWS, 128), BF),
    PR=((2, 4, 2 * BLK, ROWS), F32),
    A=((2, ROWS, 512), BF),
    GP=((2, ROWS, 512), F32),
    DU=((ROWS, 512), BF),
    DQKV=((ROWS, 384), BF),
    DK=((ROWS, 128), F32),
    DV=((ROWS, 128), F32),
    PART=((2, 4, 2, OWN, D), BF),
    SND=((2, 4, OWN, D), BF),
    CR=((8, 2, 4, OWN, D), BF),
    XR=((8, 2, 4, OWN, D), BF),
    OWNSUM=((2, OWN, D), F32),
    RES=((2, OWN, D), F32),
    XH=((4, 2, OWN, D), F32),
    SC=((4, 2, OWN, 128), F32),
    COT=((2, OWN, D), BF),
    QS=((ROWS, 128), F32),
    KC=((8, ROWS), F32),
    BIAS=((8, 512), F32),
    LOB=((ROWS, D), BF),
    GTB=((ROWS, D), BF),
    FIN=((2, 2, OWN, D), BF),
    COL=((8, 512), F32),
    CY=((4, 8, 512), F32),
    COL2=((8, 512), F32),
    CZ=((4, 8, 512), F32),
    ROWP=((8, 16, 128), F32),
    RA=((8, 16, 128), F32),
    RW1=((16, 128), F32),
    RY=((4, 16, 128), F32),
    RW2=((16, 128), F32),
    RZ=((4, 16, 128), F32),
    RW3=((16, 128), F32),
    RC=((8, 16, 128), F32),
)
SEMS = dict(
    wsy1=(4, 4), wry1=(4, 4), wsy2=(4, 4), wry2=(4, 4),
    wsz1=(4, 4), wrz1=(4, 4), wsz2=(4, 4), wrz2=(4, 4),
    gsy1=(4, 4), gry1=(4, 4), gsy2=(4, 4), gry2=(4, 4),
    gsz1=(4, 4), grz1=(4, 4), gsz2=(4, 4), grz2=(4, 4),
    cs=(8, 2), cr=(8, 2), xs=(16, 4), xr=(16, 4),
    axs=(14, 4), axr=(14, 4), acs=(14, 4), acr=(14, 4),
    fs=(4, 8), fr=(4, 8), ras=(8,), rar=(8,), rys=(4,), ryr=(4,), rzs=(4,), rzr=(4,),
    rcs=(8,), rcr=(8,), cys=(4,), cyr=(4,), czs=(4,), czr=(4,), ms=(8,), mr=(8,),
)
N_IN, N_OUT = 8, 6


class Refs:
    pass


def loop(n, body):
    def step(k, carry):
        body(k)
        return carry

    lax.fori_loop(0, n, step, 0)


def dot(a, b, dims=NN):
    return lax.dot_general(a, b, dims, preferred_element_type=F32)


def kernel(*refs):
    tok, cot, qs_in, kc_in, pa, pb, bias_in, gb = refs[:N_IN]
    lo_out, gt_out, ga_out, gbm_out, col_out, row_out = refs[N_IN : N_IN + N_OUT]
    r = Refs()
    for name, ref in zip(list(SCRATCH) + list(SEMS), refs[N_IN + N_OUT :], strict=True):
        setattr(r, name, ref)

    y, zl, c = lax.axis_index("y"), lax.axis_index("zl"), lax.axis_index("core")
    x, zh = lax.axis_index("x"), lax.axis_index("zh")
    z = zh * 2 + zl
    q_me = zl * 2 + c
    t_me = x * 2 + c
    h_me = x * 2 + zh
    home = c == zh
    away = c != zh
    sib = (y, zl, 1 - c, x, zh)

    def xdev(j):
        return (y, zl, c, j, zh)

    def ydev(yy):
        return (yy, zl, c, x, zh)

    def zout(zz):
        return (y, lax.rem(zz, 2), zh, x, lax.div(zz, 2))

    def zin(q):
        return (y, lax.div(q, 2), lax.rem(q, 2), x, c)

    def remote(src, dst, ss, rs, dev):
        return pltpu.make_async_remote_copy(
            src_ref=src, dst_ref=dst, send_sem=ss, recv_sem=rs, device_id=dev, device_id_type=MESH
        )

    def got(dst, sem):
        remote(dst, dst, sem, sem, sib).wait_recv()

    def sent(src, sem):
        remote(src, src, sem, sem, sib).wait_send()

    def when(cond, body):
        pl.when(cond)(body)

    def unless(cond, body):
        pl.when(jnp.logical_not(cond))(body)

    def others(me, body):
        for d in (2, 1, 3):
            body(lax.rem(me + d, 4))

    bar = pltpu.get_barrier_semaphore()

    def greet(dev):
        pl.semaphore_signal(bar, inc=1, device_id=dev, device_id_type=MESH)

    def greet_plane(i):
        cc, rest = lax.rem(i, 2), lax.div(i, 2)
        hh, xx = lax.rem(rest, 2), lax.div(rest, 2)
        unless((cc == c) & (hh == zh) & (xx == x), lambda: greet((y, zl, cc, xx, hh)))

    others(y, lambda yy: greet(ydev(yy)))
    for n in range(2):
        greet((y, 1 - zl, zh, x, n))
        greet((y, 1 - zl, n, x, c))
    loop(16, greet_plane)
    pl.semaphore_wait(bar, 22)

    def y_send(src, dst, ss, rs):
        others(y, lambda yy: remote(src(yy), dst, ss.at[yy], rs.at[y], ydev(yy)).start())

    def y_sent(src, ss):
        others(y, lambda yy: sent(src(yy), ss.at[yy]))

    def y_got(dst, rs):
        others(y, lambda yy: got(dst(yy), rs.at[yy]))

    def z_send(src, dst, ss, rs, me, slot, dev):
        def one(k):
            n = lax.rem(me + k, 4)
            local = home & (k == 0)
            when(local, pltpu.make_async_copy(src(n), dst, rs.at[slot]).start)
            unless(local, remote(src(n), dst, ss.at[n], rs.at[slot], dev(n)).start)

        loop(4, one)

    def z_sent(src, ss, me):
        def one(k):
            n = lax.rem(me + k, 4)
            unless(home & (k == 0), lambda: sent(src(n), ss.at[n]))

        loop(4, one)

    def z_got(dst, rs):
        loop(4, lambda n: got(dst(n), rs.at[n]))

    def w_refs(lp):
        layer, part = divmod(lp, 2)
        if part == 0:
            return pa, 256, r.SYA.at[layer], r.WAY.at[layer], r.WAZ.at[layer], layer
        return pb, 512, r.SYB.at[layer], r.WBY.at[layer], r.WBZ.at[layer], layer

    def w_one(lp):
        src, n, mid, wy, wz, layer = w_refs(lp)
        left, right = src.at[layer, :, 0:n], src.at[layer, :, n : 2 * n]
        y_send(lambda _: left, mid.at[y], r.wsy1.at[lp], r.wry1.at[lp])
        mid[y] = left[...]
        z_send(
            lambda _: right, wz.at[y, q_me], r.wsz1.at[lp], r.wrz1.at[lp], z, q_me, zout
        )

    def w_two(lp):
        src, n, mid, wy, wz, layer = w_refs(lp)
        y_got(lambda yy: mid.at[yy], r.wry1.at[lp])
        z_send(lambda _: mid, wy.at[:, q_me], r.wsy2.at[lp], r.wry2.at[lp], z, q_me, zout)
        z_got(lambda q: wz.at[y, q], r.wrz1.at[lp])
        y_send(lambda _: wz.at[y], wz.at[y], r.wsz2.at[lp], r.wrz2.at[lp])

    def w_wait(lp):
        src, n, mid, wy, wz, layer = w_refs(lp)
        z_got(lambda q: wy.at[:, q], r.wry2.at[lp])
        y_got(lambda yy: wz.at[yy], r.wrz2.at[lp])

    def w_done(lp):
        src, n, mid, wy, wz, layer = w_refs(lp)
        left, right = src.at[layer, :, 0:n], src.at[layer, :, n : 2 * n]
        y_sent(lambda _: left, r.wsy1.at[lp])
        z_sent(lambda _: right, r.wsz1.at[lp], z)
        z_sent(lambda _: mid, r.wsy2.at[lp], z)
        y_sent(lambda _: wz.at[y], r.wsz2.at[lp])

    def g_refs(lp):
        layer, part = divmod(lp, 2)
        names = "GAY GAZ R1AY R1AZ S2AY S2AZ R2AY R2AZ" if part == 0 else (
            "GBY GBZ R1BY R1BZ S2BY S2BZ R2BY R2BZ"
        )
        return [getattr(r, name).at[layer] for name in names.split()]

    def g_one(lp):
        gy, gz, r1y, r1z = g_refs(lp)[:4]
        z_send(lambda q: gy.at[:, q], r1y.at[z], r.gsy1.at[lp], r.gry1.at[lp], q_me, z, zin)
        y_send(lambda yy: gz.at[yy], r1z.at[y], r.gsz1.at[lp], r.grz1.at[lp])

    def g_two(lp):
        gy, gz, r1y, r1z, s2y, s2z, r2y, r2z = g_refs(lp)
        z_got(lambda zz: r1y.at[zz], r.gry1.at[lp])

        def sum_y(n):
            total = r1y[0, n].astype(F32)
            for k in range(1, 4):
                total = total + r1y[k, n].astype(F32)
            s2y[n] = total.astype(BF)

        loop(4, sum_y)
        y_send(lambda yy: s2y.at[yy], r2y.at[y], r.gsy2.at[lp], r.gry2.at[lp])
        y_got(lambda yy: r1z.at[yy], r.grz1.at[lp])

        def sum_z(n):
            total = gz[y, n].astype(F32)
            for d in (1, 2, 3):
                total = total + r1z[lax.rem(y + d, 4), n].astype(F32)
            s2z[n] = total.astype(BF)

        loop(4, sum_z)
        z_send(lambda q: s2z.at[q], r2z.at[z], r.gsz2.at[lp], r.grz2.at[lp], q_me, z, zin)

    def g_three(lp, out):
        gy, gz, r1y, r1z, s2y, s2z, r2y, r2z = g_refs(lp)
        layer, n = lp // 2, out.shape[2] // 2
        y_got(lambda yy: r2y.at[yy], r.gry2.at[lp])
        total = s2y[y].astype(F32)
        for d in (1, 2, 3):
            total = total + r2y[lax.rem(y + d, 4)].astype(F32)
        out[layer, :, 0:n] = total
        z_got(lambda zz: r2z.at[zz], r.grz2.at[lp])
        total = r2z[0].astype(F32)
        for k in range(1, 4):
            total = total + r2z[k].astype(F32)
        out[layer, :, n : 2 * n] = total

    def g_done(lp):
        gy, gz, r1y, r1z, s2y, s2z, r2y, r2z = g_refs(lp)
        z_sent(lambda q: gy.at[:, q], r.gsy1.at[lp], q_me)
        y_sent(lambda yy: gz.at[yy], r.gsz1.at[lp])
        y_sent(lambda yy: s2y.at[yy], r.gsy2.at[lp])
        z_sent(lambda q: s2z.at[q], r.gsz2.at[lp], q_me)

    def rows_of(u, j, core):
        return pl.ds(pl.multiple_of(u * HALF + (j * 2 + core) * OWN, OWN), OWN)

    def ag_start(s, u, buf):
        own, n = buf.at[rows_of(u, x, c)], 2 * s + u
        remote(own, own, r.acs.at[n, x], r.acr.at[n, x], sib).start()
        others(x, lambda j: remote(own, own, r.axs.at[n, j], r.axr.at[n, x], xdev(j)).start())

    def ag_forward(s, u, buf):
        n = 2 * s + u
        for d in (1, 3, 2):
            j = lax.rem(x + d, 4)
            part = buf.at[rows_of(u, j, c)]
            got(part, r.axr.at[n, j])
            remote(part, part, r.acs.at[n, j], r.acr.at[n, j], sib).start()

    def ag_wait(s, u, buf):
        for j in range(4):
            got(buf.at[rows_of(u, j, 1 - c)], r.acr.at[2 * s + u, j])

    def ag_done(s, u, buf):
        n = 2 * s + u
        own = buf.at[rows_of(u, x, c)]
        others(x, lambda j: sent(own, r.axs.at[n, j]))
        for j in range(4):
            sent(buf.at[rows_of(u, j, c)], r.acs.at[n, j])

    def rs_push(s, u, part):
        if s > 0:
            others(x, lambda j: sent(r.SND.at[u, j], r.xs.at[2 * (s - 1) + u, j]))
            sent(r.PART.at[u, :, 1 - c], r.cs.at[s - 1, u])
        r.PART[u] = part.astype(BF).reshape(4, 2, OWN, D)
        remote(
            r.PART.at[u, :, 1 - c], r.CR.at[s, u], r.cs.at[s, u], r.cr.at[s, u], sib
        ).start()

    def rs_comb(s, u):
        n = 2 * s + u
        got(r.CR.at[s, u], r.cr.at[s, u])
        both = r.PART[u, :, c].astype(F32) + r.CR[s, u].astype(F32)
        r.SND[u] = both.astype(BF)
        others(
            x,
            lambda j: remote(
                r.SND.at[u, j], r.XR.at[s, u, x], r.xs.at[n, j], r.xr.at[n, x], xdev(j)
            ).start(),
        )
        r.OWNSUM[u] = r.PART[u, x, c].astype(F32) + r.CR[s, u, x].astype(F32)

    def rs_finish(s, u):
        total = r.OWNSUM[u]
        for d in (1, 3, 2):
            j = lax.rem(x + d, 4)
            got(r.XR.at[s, u, j], r.xr.at[2 * s + u, j])
            total = total + r.XR[s, u, j].astype(F32)
        return total

    def rs_done(s, u):
        others(x, lambda j: sent(r.SND.at[u, j], r.xs.at[2 * s + u, j]))
        sent(r.PART.at[u, :, 1 - c], r.cs.at[s, u])

    def gb_row(layer, n):
        return gb[layer * 6 + n : layer * 6 + n + 1, :]

    def norm(values, n, u, gain, shift):
        centred = values - jnp.mean(values, axis=-1, keepdims=True)
        scale = lax.rsqrt(jnp.mean(centred * centred, axis=-1, keepdims=True) + eps_norm)
        hat = centred * scale
        r.XH[n, u] = hat
        r.SC[n, u] = jnp.broadcast_to(scale, (OWN, 128))
        return hat * gain + shift

    def row_part(row, vec):
        for p in range(8):
            r.ROWP[p, row : row + 1, :] += vec[:, p * 128 : (p + 1) * 128]

    def norm_back(dy, n, u, layer, which):
        hat = r.XH[n, u]
        scale = r.SC[n, u][:, 0:1]
        dyg = dy * gb_row(layer, which)
        one = jnp.mean(dyg, axis=-1, keepdims=True)
        two = jnp.mean(dyg * hat, axis=-1, keepdims=True)
        dz = scale * (dyg - one - hat * two)
        return dz

    def norm_sums(dy, dz, n, u, layer, which):
        base = layer * 6
        row_part(base + which, jnp.sum(dy * r.XH[n, u], axis=0, keepdims=True))
        row_part(base + 3 + 2 * which, jnp.sum(dy, axis=0, keepdims=True))
        row_part(base + 2 + 2 * which, jnp.sum(dz, axis=0, keepdims=True))

    lane = lax.broadcasted_iota(jnp.int32, (BLK, 128), 1)
    low_half = lane < 64

    def two_heads(v):
        zero = jnp.zeros_like(v)
        return jnp.concatenate(
            [jnp.where(low_half, v, zero), jnp.where(low_half, zero, v)], axis=0
        )

    def one_row(v):
        return jnp.where(low_half, v[:BLK], v[BLK:])

    def whole(ref):
        return ref[...].reshape(D, ref.shape[-1])

    def half_at(u):
        return pl.ds(u * HALF, HALF)

    w_one(0)

    @pl.when(home)
    def _():
        for n, (src, dst) in enumerate(
            ((tok, r.XB.at[0]), (qs_in, r.QS), (kc_in, r.KC), (bias_in, r.BIAS))
        ):
            pltpu.make_async_copy(src, dst, r.mr.at[n]).start()
            if n < 3:
                remote(src, dst, r.ms.at[n], r.mr.at[n], sib).start()
        for u in range(2):
            mine, other = cot.at[rows_of(u, x, c)], cot.at[rows_of(u, x, 1 - c)]
            pltpu.make_async_copy(mine, r.COT.at[u], r.mr.at[4 + u]).start()
            remote(other, r.COT.at[u], r.ms.at[4 + u], r.mr.at[4 + u], sib).start()

    @pl.when(away)
    def _():
        remote(bias_in, r.BIAS, r.ms.at[3], r.mr.at[3], (y, zl, zh, x, c)).start()

    w_two(0)
    w_one(1)
    for n, dst in enumerate((r.XB.at[0], r.QS, r.KC, r.BIAS, r.COT.at[0], r.COT.at[1])):
        got(dst, r.mr.at[n])

    def f_send(n, u, hh, buf):
        there, m = buf.at[rows_of(u, x, c)], 2 * n + u

        def one(k):
            xx = lax.rem(x + 2 + k, 4)
            self = home & (xx == x) & (hh == zh)
            when(self, pltpu.make_async_copy(r.FIN.at[n, u], there, r.fr.at[m, t_me]).start)
            unless(
                self,
                remote(
                    r.FIN.at[n, u], there, r.fs.at[m, 4 * hh + xx], r.fr.at[m, t_me],
                    (y, zl, zh, xx, hh),
                ).start,
            )

        loop(4, one)

    def f_wait(n, u, buf):
        loop(
            8,
            lambda t: got(
                buf.at[pl.ds(pl.multiple_of(u * HALF + t * OWN, OWN), OWN)], r.fr.at[2 * n + u, t]
            ),
        )

    def f_done(n, u):
        def one(k):
            xx, hh = lax.rem(k, 4), lax.div(k, 4)
            unless(
                home & (xx == x) & (hh == zh),
                lambda: sent(r.FIN.at[n, u], r.fs.at[2 * n + u, k]),
            )

        loop(8, one)

    for layer in range(LAYERS):
        way, waz = r.WAY.at[layer], r.WAZ.at[layer]
        wby, wbz = r.WBY.at[layer], r.WBZ.at[layer]
        qkv = r.QKV.at[layer]
        s = 2 * layer

        def project(u, layer=layer, way=way, waz=waz, qkv=qkv):
            at = half_at(u)
            rows = r.XB[layer, at, :]
            bias = r.BIAS[4 * layer : 4 * layer + 1, :]
            qkv[at, 0:256] = (dot(rows, whole(way)) + bias[:, 0:256]).astype(BF)
            qkv[at, 256:384] = (
                dot(rows, whole(waz.at[:, :, :, 0:128])) + bias[:, 256:384]
            ).astype(BF)

        def attend(j, layer=layer, qkv=qkv):
            at = pl.ds(j * BLK, BLK)
            score = dot(two_heads(qkv[at, 0:128]), qkv[:, 128:256], NT) * 0.125
            allowed = r.QS[at, 0:1] == r.KC[0:1, :]
            score = jnp.where(jnp.concatenate([allowed, allowed], axis=0), score, masked_score)
            weight = jnp.exp(score - jnp.max(score, axis=-1, keepdims=True))
            prob = weight * (1.0 / jnp.sum(weight, axis=-1, keepdims=True))
            r.PR[layer, j] = prob
            r.O[layer, at, :] = one_row(dot(prob.astype(BF), qkv[:, 256:384])).astype(BF)

        def mixed(u, layer=layer, waz=waz):
            return dot(r.O[layer, half_at(u), :], whole(waz.at[:, :, :, 128:256]), NT)

        w_wait(2 * layer)
        if layer == 0:
            project(0)
            project(1)
            w_two(1)
            w_one(2)
        else:
            for u in range(2):
                ag_forward(1, u, r.XB.at[1])
                ag_wait(1, u, r.XB.at[1])
                project(u)
            w_two(3)
        attend(0)
        attend(1)
        rs_push(s, 0, mixed(0))
        attend(2)
        rs_comb(s, 0)
        attend(3)
        rs_push(s, 1, mixed(1))
        rs_comb(s, 1)
        for u in range(2):
            if layer == 0:
                stream = r.XB[0, rows_of(u, x, c), :].astype(F32)
            else:
                stream = r.RES[u]
            z_one = rs_finish(s, u) + stream + gb_row(layer, 2)
            h_val = norm(z_one, 2 * layer, u, gb_row(layer, 0), gb_row(layer, 3))
            r.HB[layer, rows_of(u, x, c), :] = h_val.astype(BF)
            ag_start(2 * layer, u, r.HB.at[layer])
            r.RES[u] = h_val

        def feed(u, layer=layer, wby=wby, wbz=wbz):
            at = half_at(u)
            up = dot(r.HB[layer, at, :], whole(wby)) + r.BIAS[4 * layer + 1 : 4 * layer + 2, :]
            phi = 0.5 * (1.0 + lax.erf(up * 0.7071067811865476))
            r.GP[layer, at, :] = phi + up * jnp.exp(-0.5 * up * up) * 0.3989422804014327
            act = (up * phi).astype(BF)
            r.A[layer, at, :] = act
            return dot(act, whole(wbz), NT)

        w_wait(2 * layer + 1)
        buf = r.HB.at[layer]
        ag_forward(2 * layer, 0, buf)
        ag_wait(2 * layer, 0, buf)
        rs_push(s + 1, 0, feed(0))
        ag_forward(2 * layer, 1, buf)
        rs_comb(s + 1, 0)
        ag_wait(2 * layer, 1, buf)
        rs_push(s + 1, 1, feed(1))
        rs_comb(s + 1, 1)
        if layer == 0:
            w_two(2)
            w_one(3)
        for u in range(2):
            z_two = rs_finish(s + 1, u) + r.RES[u] + gb_row(layer, 4)
            x_val = norm(z_two, 2 * layer + 1, u, gb_row(layer, 1), gb_row(layer, 5))
            if layer == 0:
                r.XB[1, rows_of(u, x, c), :] = x_val.astype(BF)
                ag_start(1, u, r.XB.at[1])
                r.RES[u] = x_val
            else:
                r.FIN[0, u] = x_val.astype(BF)

    def ra_send(k):
        cc, xx = lax.rem(k, 2), lax.div(k, 2)
        when(k == t_me, pltpu.make_async_copy(r.ROWP.at[k], r.RA.at[k], r.rar.at[k]).start)
        unless(
            k == t_me,
            remote(
                r.ROWP.at[k], r.RA.at[t_me], r.ras.at[k], r.rar.at[t_me], (y, zl, cc, xx, zh)
            ).start,
        )

    def row_one():
        loop(8, lambda t: got(r.RA.at[t], r.rar.at[t]))
        r.RW1[...] = jnp.sum(r.RA[...], axis=0)
        y_send(lambda _: r.RW1, r.RY.at[y], r.rys, r.ryr)
        r.RY[y] = r.RW1[...]

    def row_two():
        y_got(lambda yy: r.RY.at[yy], r.ryr)
        r.RW2[...] = jnp.sum(r.RY[...], axis=0)
        z_send(lambda _: r.RW2, r.RZ.at[z], r.rzs, r.rzr, q_me, z, zin)

    def row_three():
        z_got(lambda zz: r.RZ.at[zz], r.rzr)
        r.RW3[...] = jnp.sum(r.RZ[...], axis=0)

        def rc_send(k):
            hh, xx = lax.rem(k, 2), lax.div(k, 2)
            when(k == h_me, pltpu.make_async_copy(r.RW3, r.RC.at[k], r.rcr.at[k]).start)
            unless(
                k == h_me,
                remote(
                    r.RW3, r.RC.at[h_me], r.rcs.at[k], r.rcr.at[h_me], (y, zl, c, xx, hh)
                ).start,
            )

        loop(8, rc_send)

    def col_one():
        y_send(lambda _: r.COL, r.CY.at[y], r.cys, r.cyr)
        r.CY[y] = r.COL[...]

    def col_two():
        y_got(lambda yy: r.CY.at[yy], r.cyr)
        r.COL2[...] = jnp.sum(r.CY[...], axis=0)
        z_send(lambda _: r.COL2, r.CZ.at[z], r.czs, r.czr, q_me, z, zin)

    r.ROWP[...] = jnp.zeros_like(r.ROWP)
    r.COL[...] = jnp.zeros_like(r.COL)
    for layer in (1, 0):
        way, waz = r.WAY.at[layer], r.WAZ.at[layer]
        wby, wbz = r.WBY.at[layer], r.WBZ.at[layer]
        qkv = r.QKV.at[layer]
        ag_a, ag_b = (3, 4) if layer == 1 else (5, 6)
        s = 4 + 2 * (1 - layer)
        df, ds = r.DFB.at[layer], r.DSB.at[layer]

        def grad_a(t, layer=layer):
            at = pl.ds(pl.multiple_of(t * 256, 256), 256)
            lhs = r.XB[layer, :, at]
            r.GAY[layer, t] = dot(lhs, r.DQKV[:, 0:256], TN).astype(BF).reshape(4, 64, 256)
            r.GAZ[layer, t, :, :, 0:128] = (
                dot(lhs, r.DQKV[:, 256:384], TN).astype(BF).reshape(4, 64, 128)
            )
            r.GAZ[layer, t, :, :, 128:256] = (
                dot(r.DSB[layer, :, at], r.O[layer], TN).astype(BF).reshape(4, 64, 128)
            )

        def grad_b(t, layer=layer):
            at = pl.ds(pl.multiple_of(t * 256, 256), 256)
            r.GBY[layer, t] = dot(r.HB[layer, :, at], r.DU[...], TN).astype(BF).reshape(4, 64, 512)
            r.GBZ[layer, t] = (
                dot(r.DFB[layer, :, at], r.A[layer], TN).astype(BF).reshape(4, 64, 512)
            )

        for u in range(2):
            if layer == 1:
                dy = r.COT[u].astype(F32)
            else:
                dy = rs_finish(5, u) + r.RES[u]
            dz = norm_back(dy, 2 * layer + 1, u, layer, 1)
            df[rows_of(u, x, c), :] = dz.astype(BF)
            ag_start(ag_a, u, df)
            r.RES[u] = dz
            norm_sums(dy, dz, 2 * layer + 1, u, layer, 1)
            if layer == 0 and u == 0:
                loop(2, lambda t: grad_one_a(t + 2))
        if layer == 0:
            g_one(2)

        def feed_back(u, layer=layer, wby=wby, wbz=wbz):
            at = half_at(u)
            da = dot(r.DFB[layer, at, :], whole(wbz))
            du = (da * r.GP[layer, at, :]).astype(BF)
            r.DU[at, :] = du
            up_row = 4 * layer + 1
            r.COL[up_row : up_row + 1, :] += jnp.sum(du.astype(F32), axis=0, keepdims=True)
            return dot(du, whole(wby), NT)

        ag_forward(ag_a, 0, df)
        ag_wait(ag_a, 0, df)
        f_send(0, 0, layer, r.LOB)
        rs_push(s, 0, feed_back(0))
        ag_forward(ag_a, 1, df)
        rs_comb(s, 0)
        ag_wait(ag_a, 1, df)
        rs_push(s, 1, feed_back(1))
        rs_comb(s, 1)
        loop(2, grad_b)
        for u in range(2):
            dh = rs_finish(s, u) + r.RES[u]
            dz = norm_back(dh, 2 * layer, u, layer, 0)
            ds[rows_of(u, x, c), :] = dz.astype(BF)
            ag_start(ag_b, u, ds)
            r.RES[u] = dz
            norm_sums(dh, dz, 2 * layer, u, layer, 0)
            if u == 0:
                loop(2, lambda t: grad_b(t + 2))
        g_one(2 * layer + 1)
        if layer == 0:
            loop(8, ra_send)
            g_two(2)

        r.DK[...] = jnp.zeros_like(r.DK)
        r.DV[...] = jnp.zeros_like(r.DV)

        def attend_back(j, layer=layer, waz=waz, qkv=qkv):
            at = pl.ds(j * BLK, BLK)
            do = two_heads(dot(r.DSB[layer, at, :], whole(waz.at[:, :, :, 128:256])).astype(BF))
            prob = r.PR[layer, j]
            dp = dot(do, qkv[:, 256:384], NT)
            inner = jnp.sum(prob * dp, axis=-1, keepdims=True)
            dscore = (prob * (dp - inner)).astype(BF)
            dq = one_row(dot(dscore, qkv[:, 128:256])) * 0.125
            r.DQKV[at, 0:128] = dq.astype(BF)
            r.DK[...] += dot(dscore, two_heads(qkv[at, 0:128]), TN)
            r.DV[...] += dot(prob.astype(BF), do, TN)

        ag_forward(ag_b, 0, ds)
        ag_wait(ag_b, 0, ds)
        f_send(0, 1, layer, r.LOB)
        attend_back(0)
        attend_back(1)
        if layer == 0:
            row_one()
        ag_forward(ag_b, 1, ds)
        ag_wait(ag_b, 1, ds)
        attend_back(2)
        attend_back(3)
        r.DQKV[:, 128:256] = (r.DK[...] * 0.125).astype(BF)
        r.DQKV[:, 256:384] = r.DV[...].astype(BF)
        s += 1

        def input_back(u, way=way, waz=waz):
            at = half_at(u)
            return dot(r.DQKV[at, 0:256], whole(way), NT) + dot(
                r.DQKV[at, 256:384], whole(waz.at[:, :, :, 0:128]), NT
            )

        rs_push(s, 0, input_back(0))
        part = input_back(1)
        rs_comb(s, 0)
        rs_push(s, 1, part)
        rs_comb(s, 1)
        r.COL[4 * layer : 4 * layer + 1, 0:384] = jnp.sum(
            r.DQKV[...].astype(F32), axis=0, keepdims=True
        )
        if layer == 0:
            col_one()
            row_two()
        g_two(2 * layer + 1)
        loop(2, grad_a)
        grad_one_a = grad_a
        if layer == 0:
            loop(2, lambda t: grad_a(t + 2))
            g_one(0)

    for u in range(2):
        r.FIN[1, u] = (rs_finish(7, u) + r.RES[u]).astype(BF)
        f_send(1, u, 0, r.GTB)
        f_send(1, u, 1, r.GTB)
    row_three()
    col_two()
    g_three(3, gbm_out)
    g_three(2, ga_out)
    g_three(1, gbm_out)
    g_two(0)
    f_wait(0, 0, r.LOB)
    f_wait(0, 1, r.LOB)
    lo_out[...] = r.LOB[...]
    z_got(lambda zz: r.CZ.at[zz], r.czr)
    col_out[...] = jnp.sum(r.CZ[...], axis=0)
    loop(8, lambda t: got(r.RC.at[t], r.rcr.at[t]))
    row_out[...] = r.RC[...]
    g_three(0, ga_out)
    for u in range(2):
        f_wait(1, u, r.GTB)
        gt_out[half_at(u), :] = r.GTB[half_at(u), :].astype(F32)

    for lp in range(4):
        w_done(lp)
        g_done(lp)
    gathers = (
        r.HB.at[0], r.XB.at[1], r.HB.at[1], r.DFB.at[1], r.DSB.at[1], r.DFB.at[0], r.DSB.at[0]
    )
    for s, buf in enumerate(gathers):
        for u in range(2):
            ag_done(s, u, buf)
    for u in range(2):
        rs_done(7, u)
        f_done(0, u)
        f_done(1, u)
    y_sent(lambda _: r.RW1, r.rys)
    z_sent(lambda _: r.RW2, r.rzs, q_me)
    y_sent(lambda _: r.COL, r.cys)
    z_sent(lambda _: r.COL2, r.czs, q_me)

    def small_done(k):
        unless(k == t_me, lambda: sent(r.ROWP.at[k], r.ras.at[k]))
        unless(k == h_me, lambda: sent(r.RW3, r.rcs.at[k]))

    loop(8, small_done)

    @pl.when(home)
    def _():
        for n, src in enumerate((tok, qs_in, kc_in)):
            sent(src, r.ms.at[n])
        for u in range(2):
            sent(r.COT.at[u], r.ms.at[4 + u])

    @pl.when(away)
    def _():
        sent(bias_in, r.ms.at[3])


def token_masks(bucket, lengths, row_count):
    position = jnp.arange(row_count, dtype=jnp.int32)
    slot_size = jnp.right_shift(jnp.int32(row_count), bucket)
    slot_ids = position // slot_size
    within = position - slot_ids * slot_size
    match = slot_ids[:, None] == jnp.arange(lengths.shape[0], dtype=jnp.int32)[None, :]
    length_at = jnp.sum(jnp.where(match, lengths[None, :], 0), axis=1, dtype=jnp.int32)
    return (slot_ids, within < length_at)


def adam_step(weight, grad, first, second, with_decay, rate):
    first_new = beta_one * first + (1.0 - beta_one) * grad
    second_new = beta_two * second + (1.0 - beta_two) * grad * grad
    first_hat = first_new / (1.0 - beta_one**STEP)
    second_hat = second_new / (1.0 - beta_two**STEP)
    change = first_hat / (jnp.sqrt(second_hat) + eps_adam)
    if with_decay:
        change = change + weight_decay * weight
    return (first_new, second_new, weight - rate * change)


def local(
    tokens, cotangent, bucket_of, seq_lens, w_qkv, head_bias, w_out, w_up, up_bias, w_down, gains,
    biases, first_qkv, second_qkv, first_head, second_head, first_out, second_out, first_up,
    second_up, first_up_bias, second_up_bias, first_down, second_down, first_gains, second_gains,
    first_biases, second_biases,
):
    slot_ids, valid = token_masks(bucket_of[0], seq_lens[0], ROWS)
    masked = jnp.where(valid[:, None], cotangent, jnp.zeros_like(cotangent))
    slot_f = slot_ids.astype(F32)
    q_slot = jnp.broadcast_to(slot_f[:, None], (ROWS, 128))
    k_code = jnp.broadcast_to(jnp.where(valid, slot_f, -1.0)[None, :], (8, ROWS))
    pack_a = jnp.concatenate(
        [w_qkv.reshape(2, 64, 384), jnp.swapaxes(w_out, 1, 2)], axis=-1
    ).astype(BF)
    pack_b = jnp.concatenate([w_up, jnp.swapaxes(w_down, 1, 2)], axis=-1).astype(BF)
    bias_rows = []
    for layer in range(LAYERS):
        zero = jnp.zeros((128,), F32)
        bias_rows.append(jnp.concatenate([head_bias[layer, 0], zero, head_bias[layer, 1], zero]))
        bias_rows += [up_bias[layer], jnp.zeros((512,), F32), jnp.zeros((512,), F32)]
    bias_pack = jnp.stack(bias_rows)
    gb_pack = jnp.concatenate(
        [gains[0], biases[0], gains[1], biases[1], jnp.zeros((4, D), F32)], axis=0
    )
    vmem = pl.BlockSpec(memory_space=pltpu.VMEM)
    layer_out, grad_tokens, ga, gbm, col, row = pl.pallas_call(
        kernel,
        out_shape=(
            jax.ShapeDtypeStruct((ROWS, D), BF),
            jax.ShapeDtypeStruct((ROWS, D), F32),
            jax.ShapeDtypeStruct((2, 64, 512), F32),
            jax.ShapeDtypeStruct((2, 64, 1024), F32),
            jax.ShapeDtypeStruct((8, 512), F32),
            jax.ShapeDtypeStruct((8, 16, 128), F32),
        ),
        in_specs=[vmem] * N_IN,
        out_specs=(vmem,) * N_OUT,
        scratch_shapes=[pltpu.VMEM(s, t) for s, t in SCRATCH.values()]
        + [pltpu.SemaphoreType.DMA(s) for s in SEMS.values()],
        compiler_params=pltpu.CompilerParams(
            collective_id=0, has_side_effects=True, vmem_limit_bytes=63 << 20
        ),
    )(tokens, masked, q_slot, k_code, pack_a, pack_b, bias_pack, gb_pack)
    grad_qkv = ga[:, :, 0:384].reshape(2, 64, 3, 128)
    grad_out = jnp.swapaxes(ga[:, :, 384:512], 1, 2)
    grad_up = gbm[:, :, 0:512]
    grad_down = jnp.swapaxes(gbm[:, :, 512:1024], 1, 2)
    col = col.reshape(2, 4, 512)
    grad_head = jnp.stack([col[:, 0, 0:128], col[:, 0, 256:384]], axis=1)
    grad_up_bias = col[:, 1, :]
    row = jnp.swapaxes(row, 0, 1).reshape(16, D)[0:12].reshape(2, 6, D)
    grad_gains = row[:, 0:2]
    grad_biases = row[:, 2:6]
    return (
        layer_out,
        grad_tokens,
        grad_qkv, *adam_step(w_qkv, grad_qkv, first_qkv, second_qkv, True, step_rate),
        grad_head, *adam_step(head_bias, grad_head, first_head, second_head, False, bias_rate),
        grad_out, *adam_step(w_out, grad_out, first_out, second_out, True, output_rate),
        grad_up, *adam_step(w_up, grad_up, first_up, second_up, True, step_rate),
        grad_up_bias,
        *adam_step(up_bias, grad_up_bias, first_up_bias, second_up_bias, False, bias_rate),
        grad_down, *adam_step(w_down, grad_down, first_down, second_down, True, step_rate),
        grad_gains, *adam_step(gains, grad_gains, first_gains, second_gains, False, gain_rate),
        grad_biases, *adam_step(biases, grad_biases, first_biases, second_biases, False, bias_rate),
    )


def solution(mesh):
    fine = Mesh(mesh.devices.reshape(4, 2, 2, 4, 2), ("y", "zl", "core", "x", "zh"))
    b, t = ("y", "zl", "core"), ("x", "zh")
    qkv, head = P(None, b, None, t), P(None, None, t)
    out, up, up_bias, down, rep = P(None, t, b), P(None, b, t), P(None, t), P(None, t, b), P()
    in_specs = (
        P(b, None), P(b, None), P(b), P(b, None), qkv, head, out, up, up_bias, down, rep, rep,
        qkv, qkv, head, head, out, out, up, up, up_bias, up_bias, down, down, rep, rep, rep, rep,
    )
    out_specs = (P(b, None), P(b, None))
    for spec in (qkv, head, out, up, up_bias, down, rep, rep):
        out_specs += (spec,) * 4
    return jax.shard_map(
        local, mesh=fine, in_specs=in_specs, out_specs=out_specs, check_vma=False
    )
```

```python
import jax
import jax.numpy as jnp
from jax import lax
from jax.experimental import pallas as pl
from jax.experimental.pallas import tpu as pltpu
from jax.sharding import Mesh
from jax.sharding import PartitionSpec as P

LAYERS = 2
STEP = 10
ROWS = 512
D = 1024
BLK = 128
HALF = 256
OWN = 32

eps_norm = 1e-05
beta_one = 0.9
beta_two = 0.999
eps_adam = 1e-08
step_rate = 0.1
output_rate = 0.3
bias_rate = 0.3
gain_rate = 1.0
weight_decay = 0.01
masked_score = -1000000000.0

MESH = pl.DeviceIdType.MESH
BF = jnp.bfloat16
F32 = jnp.float32
NT = (((1,), (1,)), ((), ()))
TN = (((0,), (0,)), ((), ()))
NN = (((1,), (0,)), ((), ()))

SCRATCH = dict(
    XB=((2, ROWS, D), BF),
    HB=((2, ROWS, D), BF),
    DFB=((2, ROWS, D), BF),
    DSB=((2, ROWS, D), BF),
    WAY=((2, 4, 4, 64, 256), BF),
    WAZ=((2, 4, 4, 64, 256), BF),
    WBY=((2, 4, 4, 64, 512), BF),
    WBZ=((2, 4, 4, 64, 512), BF),
    SYA=((2, 4, 64, 256), BF),
    SYB=((2, 4, 64, 512), BF),
    GAY=((2, 4, 4, 64, 256), BF),
    GAZ=((2, 4, 4, 64, 256), BF),
    GBY=((2, 4, 4, 64, 512), BF),
    GBZ=((2, 4, 4, 64, 512), BF),
    R1AY=((2, 4, 4, 64, 256), BF),
    R1AZ=((2, 4, 4, 64, 256), BF),
    R1BY=((2, 4, 4, 64, 512), BF),
    R1BZ=((2, 4, 4, 64, 512), BF),
    S2AY=((2, 4, 64, 256), BF),
    S2AZ=((2, 4, 64, 256), BF),
    S2BY=((2, 4, 64, 512), BF),
    S2BZ=((2, 4, 64, 512), BF),
    R2AY=((2, 4, 64, 256), BF),
    R2AZ=((2, 4, 64, 256), BF),
    R2BY=((2, 4, 64, 512), BF),
    R2BZ=((2, 4, 64, 512), BF),
    QKV=((2, ROWS, 384), BF),
    O=((2, ROWS, 128), BF),
    PR=((2, 4, 2 * BLK, ROWS), F32),
    A=((2, ROWS, 512), BF),
    GP=((2, ROWS, 512), F32),
    DU=((ROWS, 512), BF),
    DQKV=((ROWS, 384), BF),
    DK=((ROWS, 128), F32),
    DV=((ROWS, 128), F32),
    PART=((2, 4, 2, OWN, D), BF),
    SND=((2, 4, OWN, D), BF),
    CR=((8, 2, 4, OWN, D), BF),
    XR=((8, 2, 4, OWN, D), BF),
    OWNSUM=((2, OWN, D), F32),
    RES=((2, OWN, D), F32),
    XH=((4, 2, OWN, D), F32),
    SC=((4, 2, OWN, 128), F32),
    COT=((2, OWN, D), BF),
    COTF=((2, 2, OWN, D), BF),
    COTM=((2, 2, OWN, D), BF),
    QS0=((ROWS, 128), F32),
    KC0=((8, ROWS), F32),
    QS=((ROWS, 128), F32),
    KC=((8, ROWS), F32),
    WQF=((2, 3, 64, 128), F32),
    WOF=((2, 64, 128), F32),
    WUF=((2, 64, 512), F32),
    WDF=((2, 64, 512), F32),
    PA=((2, 64, 512), BF),
    PB=((2, 64, 1024), BF),
    GNS=((2, 2, D), F32),
    BIS=((2, 4, D), F32),
    HBB=((2, 2, 128), F32),
    UBB=((2, 512), F32),
    GQ=((2, 3, 64, 128), F32),
    GO=((2, 64, 128), F32),
    GU=((2, 64, 512), F32),
    GD=((2, 64, 512), F32),
    GHB=((2, 2, 128), F32),
    GUB=((2, 512), F32),
    GGN=((2, 2, D), F32),
    GBI=((2, 4, D), F32),
    LOB=((ROWS, D), BF),
    GTB=((ROWS, D), BF),
    FIN=((2, 2, OWN, D), BF),
    COL=((8, 512), F32),
    CY=((4, 8, 512), F32),
    COL2=((8, 512), F32),
    CZ=((4, 8, 512), F32),
    ROWP=((8, 16, 128), F32),
    RA=((8, 16, 128), F32),
    RW1=((16, 128), F32),
    RY=((4, 16, 128), F32),
    RW2=((16, 128), F32),
    RZ=((4, 16, 128), F32),
    RW3=((16, 128), F32),
    RC=((8, 16, 128), F32),
)
SEMS = dict(
    wsy1=(4, 4), wry1=(4, 4), wsy2=(4, 4), wry2=(4, 4),
    wsz1=(4, 4), wrz1=(4, 4), wsz2=(4, 4), wrz2=(4, 4),
    gsy1=(4, 4), gry1=(4, 4), gsy2=(4, 4), gry2=(4, 4),
    gsz1=(4, 4), grz1=(4, 4), gsz2=(4, 4), grz2=(4, 4),
    cs=(8, 2), cr=(8, 2), xs=(16, 4), xr=(16, 4),
    axs=(14, 4), axr=(14, 4), acs=(14, 4), acr=(14, 4),
    fs=(4, 8), fr=(4, 8), ras=(8,), rar=(8,), rys=(4,), ryr=(4,), rzs=(4,), rzr=(4,),
    rcs=(8,), rcr=(8,), cys=(4,), cyr=(4,), czs=(4,), czr=(4,), ms=(8,), mr=(8,), ld=(16,), st=(16,),
)
N_IN, N_OUT = 12, 10


class Refs:
    pass


def loop(n, body):
    def step(k, carry):
        body(k)
        return carry

    lax.fori_loop(0, n, step, 0)


def dot(a, b, dims=NN):
    return lax.dot_general(a, b, dims, preferred_element_type=F32)


def kernel(*refs):
    tok, cot, bucket, lens, wq, hb, wo, wu, ub, wd, gains, biases = refs[:N_IN]
    outs = refs[N_IN : N_IN + N_OUT]
    r = Refs()
    for name, ref in zip(list(SCRATCH) + list(SEMS), refs[N_IN + N_OUT :], strict=True):
        setattr(r, name, ref)

    y, zl, c = lax.axis_index("y"), lax.axis_index("zl"), lax.axis_index("core")
    x, zh = lax.axis_index("x"), lax.axis_index("zh")
    z = zh * 2 + zl
    q_me = zl * 2 + c
    t_me = x * 2 + c
    h_me = x * 2 + zh
    home = c == zh
    away = c != zh
    sib = (y, zl, 1 - c, x, zh)

    def xdev(j):
        return (y, zl, c, j, zh)

    def ydev(yy):
        return (yy, zl, c, x, zh)

    def zout(zz):
        return (y, lax.rem(zz, 2), zh, x, lax.div(zz, 2))

    def zin(q):
        return (y, lax.div(q, 2), lax.rem(q, 2), x, c)

    def remote(src, dst, ss, rs, dev):
        return pltpu.make_async_remote_copy(
            src_ref=src, dst_ref=dst, send_sem=ss, recv_sem=rs, device_id=dev, device_id_type=MESH
        )

    def got(dst, sem):
        remote(dst, dst, sem, sem, sib).wait_recv()

    def sent(src, sem):
        remote(src, src, sem, sem, sib).wait_send()

    def when(cond, body):
        pl.when(cond)(body)

    def unless(cond, body):
        pl.when(jnp.logical_not(cond))(body)

    def others(me, body):
        for d in (2, 1, 3):
            body(lax.rem(me + d, 4))

    bar = pltpu.get_barrier_semaphore()

    def greet(dev):
        pl.semaphore_signal(bar, inc=1, device_id=dev, device_id_type=MESH)

    def greet_plane(i):
        cc, rest = lax.rem(i, 2), lax.div(i, 2)
        hh, xx = lax.rem(rest, 2), lax.div(rest, 2)
        unless((cc == c) & (hh == zh) & (xx == x), lambda: greet((y, zl, cc, xx, hh)))

    others(y, lambda yy: greet(ydev(yy)))
    for n in range(2):
        greet((y, 1 - zl, zh, x, n))
        greet((y, 1 - zl, n, x, c))
    loop(16, greet_plane)

    loads = [
        (wq, r.WQF), (wo, r.WOF), (wu, r.WUF), (wd, r.WDF), (gains, r.GNS), (biases, r.BIS)
    ]
    for u in range(2):
        for core in range(2):
            at = pl.ds(pl.multiple_of(u * HALF + (x * 2 + core) * OWN, OWN), OWN)
            loads.append((cot.at[at], r.COTF.at[u, core]))
    loads = [pltpu.make_async_copy(a, b, r.ld.at[n]) for n, (a, b) in enumerate(loads)]
    for load in loads:
        load.start()
    for load in loads[:2]:
        load.wait()
    for layer in range(LAYERS):
        for n in range(3):
            r.PA[layer, :, n * 128 : (n + 1) * 128] = r.WQF[layer, n].astype(BF)
        r.PA[layer, :, 384:512] = r.WOF[layer].astype(BF)
    pa, pb = r.PA, r.PB
    b = bucket[0]
    slots = jnp.where(b == 0, 1, jnp.where(b == 1, 2, jnp.where(b == 2, 4, 8)))
    size = jnp.where(b == 0, 512, jnp.where(b == 1, 256, jnp.where(b == 2, 128, 64)))

    def slot_and_valid(pos):
        slot = lax.shift_right_logical(pos * slots, 9)
        length = jnp.zeros_like(pos)
        for n in range(8):
            length = jnp.where(slot == n, lens[0, n], length)
        return slot, pos - slot * size < length

    pos = lax.broadcasted_iota(jnp.int32, (8, ROWS), 1)
    slot, valid = slot_and_valid(pos)
    r.KC0[...] = jnp.where(valid, slot, -1).astype(F32)
    pos = lax.broadcasted_iota(jnp.int32, (ROWS, 128), 0)
    r.QS0[...] = lax.shift_right_logical(pos * slots, 9).astype(F32)
    for load in loads[6:]:
        load.wait()
    for u in range(2):
        for core in range(2):
            first = u * HALF + (x * 2 + core) * OWN
            slot, valid = slot_and_valid(first + lax.broadcasted_iota(jnp.int32, (OWN, 128), 0))
            keep = jnp.where(valid, 1.0, 0.0)[:, 0:1]
            r.COTM[u, core] = (r.COTF[u, core].astype(F32) * keep).astype(BF)
    pl.semaphore_wait(bar, 22)

    def y_send(src, dst, ss, rs):
        others(y, lambda yy: remote(src(yy), dst, ss.at[yy], rs.at[y], ydev(yy)).start())

    def y_sent(src, ss):
        others(y, lambda yy: sent(src(yy), ss.at[yy]))

    def y_got(dst, rs):
        others(y, lambda yy: got(dst(yy), rs.at[yy]))

    def z_send(src, dst, ss, rs, me, slot, dev):
        def one(k):
            n = lax.rem(me + k, 4)
            local = home & (k == 0)
            when(local, pltpu.make_async_copy(src(n), dst, rs.at[slot]).start)
            unless(local, remote(src(n), dst, ss.at[n], rs.at[slot], dev(n)).start)

        loop(4, one)

    def z_sent(src, ss, me):
        def one(k):
            n = lax.rem(me + k, 4)
            unless(home & (k == 0), lambda: sent(src(n), ss.at[n]))

        loop(4, one)

    def z_got(dst, rs):
        loop(4, lambda n: got(dst(n), rs.at[n]))

    def w_refs(lp):
        layer, part = divmod(lp, 2)
        if part == 0:
            return pa, 256, r.SYA.at[layer], r.WAY.at[layer], r.WAZ.at[layer], layer
        return pb, 512, r.SYB.at[layer], r.WBY.at[layer], r.WBZ.at[layer], layer

    def w_one(lp):
        src, n, mid, wy, wz, layer = w_refs(lp)
        left, right = src.at[layer, :, 0:n], src.at[layer, :, n : 2 * n]
        y_send(lambda _: left, mid.at[y], r.wsy1.at[lp], r.wry1.at[lp])
        mid[y] = left[...]
        z_send(
            lambda _: right, wz.at[y, q_me], r.wsz1.at[lp], r.wrz1.at[lp], z, q_me, zout
        )

    def w_two(lp):
        src, n, mid, wy, wz, layer = w_refs(lp)
        y_got(lambda yy: mid.at[yy], r.wry1.at[lp])
        z_send(lambda _: mid, wy.at[:, q_me], r.wsy2.at[lp], r.wry2.at[lp], z, q_me, zout)
        z_got(lambda q: wz.at[y, q], r.wrz1.at[lp])
        y_send(lambda _: wz.at[y], wz.at[y], r.wsz2.at[lp], r.wrz2.at[lp])

    def w_wait(lp):
        src, n, mid, wy, wz, layer = w_refs(lp)
        z_got(lambda q: wy.at[:, q], r.wry2.at[lp])
        y_got(lambda yy: wz.at[yy], r.wrz2.at[lp])

    def w_done(lp):
        src, n, mid, wy, wz, layer = w_refs(lp)
        left, right = src.at[layer, :, 0:n], src.at[layer, :, n : 2 * n]
        y_sent(lambda _: left, r.wsy1.at[lp])
        z_sent(lambda _: right, r.wsz1.at[lp], z)
        z_sent(lambda _: mid, r.wsy2.at[lp], z)
        y_sent(lambda _: wz.at[y], r.wsz2.at[lp])

    def g_refs(lp):
        layer, part = divmod(lp, 2)
        if part == 0:
            group = (r.GAY, r.GAZ, r.R1AY, r.R1AZ, r.S2AY, r.S2AZ, r.R2AY, r.R2AZ)
        else:
            group = (r.GBY, r.GBZ, r.R1BY, r.R1BZ, r.S2BY, r.S2BZ, r.R2BY, r.R2BZ)
        return [ref.at[layer] for ref in group]

    def g_one(lp):
        gy, gz, r1y, r1z = g_refs(lp)[:4]
        z_send(lambda q: gy.at[:, q], r1y.at[z], r.gsy1.at[lp], r.gry1.at[lp], q_me, z, zin)
        y_send(lambda yy: gz.at[yy], r1z.at[y], r.gsz1.at[lp], r.grz1.at[lp])

    def g_two(lp):
        gy, gz, r1y, r1z, s2y, s2z, r2y, r2z = g_refs(lp)
        z_got(lambda zz: r1y.at[zz], r.gry1.at[lp])

        def sum_y(n):
            total = r1y[0, n].astype(F32)
            for k in range(1, 4):
                total = total + r1y[k, n].astype(F32)
            s2y[n] = total.astype(BF)

        loop(4, sum_y)
        y_send(lambda yy: s2y.at[yy], r2y.at[y], r.gsy2.at[lp], r.gry2.at[lp])
        y_got(lambda yy: r1z.at[yy], r.grz1.at[lp])

        def sum_z(n):
            total = gz[y, n].astype(F32)
            for d in (1, 2, 3):
                total = total + r1z[lax.rem(y + d, 4), n].astype(F32)
            s2z[n] = total.astype(BF)

        loop(4, sum_z)
        z_send(lambda q: s2z.at[q], r2z.at[z], r.gsz2.at[lp], r.grz2.at[lp], q_me, z, zin)

    def g_three(lp):
        gy, gz, r1y, r1z, s2y, s2z, r2y, r2z = g_refs(lp)
        layer, part = divmod(lp, 2)
        y_got(lambda yy: r2y.at[yy], r.gry2.at[lp])
        total = s2y[y].astype(F32)
        for d in (1, 2, 3):
            total = total + r2y[lax.rem(y + d, 4)].astype(F32)
        if part == 0:
            r.GQ[layer, 0] = total[:, 0:128]
            r.GQ[layer, 1] = total[:, 128:256]
        else:
            r.GU[layer] = total
        z_got(lambda zz: r2z.at[zz], r.grz2.at[lp])
        total = r2z[0].astype(F32)
        for k in range(1, 4):
            total = total + r2z[k].astype(F32)
        if part == 0:
            r.GQ[layer, 2] = total[:, 0:128]
            r.GO[layer] = total[:, 128:256]
        else:
            r.GD[layer] = total

    def g_done(lp):
        gy, gz, r1y, r1z, s2y, s2z, r2y, r2z = g_refs(lp)
        z_sent(lambda q: gy.at[:, q], r.gsy1.at[lp], q_me)
        y_sent(lambda yy: gz.at[yy], r.gsz1.at[lp])
        y_sent(lambda yy: s2y.at[yy], r.gsy2.at[lp])
        z_sent(lambda q: s2z.at[q], r.gsz2.at[lp], q_me)

    def rows_of(u, j, core):
        return pl.ds(pl.multiple_of(u * HALF + (j * 2 + core) * OWN, OWN), OWN)

    def ag_start(s, u, buf):
        own, n = buf.at[rows_of(u, x, c)], 2 * s + u
        remote(own, own, r.acs.at[n, x], r.acr.at[n, x], sib).start()
        others(x, lambda j: remote(own, own, r.axs.at[n, j], r.axr.at[n, x], xdev(j)).start())

    def ag_forward(s, u, buf):
        n = 2 * s + u
        for d in (1, 3, 2):
            j = lax.rem(x + d, 4)
            part = buf.at[rows_of(u, j, c)]
            got(part, r.axr.at[n, j])
            remote(part, part, r.acs.at[n, j], r.acr.at[n, j], sib).start()

    def ag_wait(s, u, buf):
        for j in range(4):
            got(buf.at[rows_of(u, j, 1 - c)], r.acr.at[2 * s + u, j])

    def ag_done(s, u, buf):
        n = 2 * s + u
        own = buf.at[rows_of(u, x, c)]
        others(x, lambda j: sent(own, r.axs.at[n, j]))
        for j in range(4):
            sent(buf.at[rows_of(u, j, c)], r.acs.at[n, j])

    def rs_push(s, u, part):
        if s > 0:
            others(x, lambda j: sent(r.SND.at[u, j], r.xs.at[2 * (s - 1) + u, j]))
            sent(r.PART.at[u, :, 1 - c], r.cs.at[s - 1, u])
        r.PART[u] = part.astype(BF).reshape(4, 2, OWN, D)
        remote(
            r.PART.at[u, :, 1 - c], r.CR.at[s, u], r.cs.at[s, u], r.cr.at[s, u], sib
        ).start()

    def rs_comb(s, u):
        n = 2 * s + u
        got(r.CR.at[s, u], r.cr.at[s, u])
        both = r.PART[u, :, c].astype(F32) + r.CR[s, u].astype(F32)
        r.SND[u] = both.astype(BF)
        others(
            x,
            lambda j: remote(
                r.SND.at[u, j], r.XR.at[s, u, x], r.xs.at[n, j], r.xr.at[n, x], xdev(j)
            ).start(),
        )
        r.OWNSUM[u] = r.PART[u, x, c].astype(F32) + r.CR[s, u, x].astype(F32)

    def rs_finish(s, u):
        total = r.OWNSUM[u]
        for d in (1, 3, 2):
            j = lax.rem(x + d, 4)
            got(r.XR.at[s, u, j], r.xr.at[2 * s + u, j])
            total = total + r.XR[s, u, j].astype(F32)
        return total

    def rs_done(s, u):
        others(x, lambda j: sent(r.SND.at[u, j], r.xs.at[2 * s + u, j]))
        sent(r.PART.at[u, :, 1 - c], r.cs.at[s, u])

    def gb_row(layer, n):
        return r.GNS[layer, n : n + 1, :] if n < 2 else r.BIS[layer, n - 2 : n - 1, :]

    def norm(values, n, u, gain, shift):
        centred = values - jnp.mean(values, axis=-1, keepdims=True)
        scale = lax.rsqrt(jnp.mean(centred * centred, axis=-1, keepdims=True) + eps_norm)
        hat = centred * scale
        r.XH[n, u] = hat
        r.SC[n, u] = jnp.broadcast_to(scale, (OWN, 128))
        return hat * gain + shift

    def row_part(row, vec):
        for p in range(8):
            r.ROWP[p, row : row + 1, :] += vec[:, p * 128 : (p + 1) * 128]

    def norm_back(dy, n, u, layer, which):
        hat = r.XH[n, u]
        scale = r.SC[n, u][:, 0:1]
        dyg = dy * gb_row(layer, which)
        one = jnp.mean(dyg, axis=-1, keepdims=True)
        two = jnp.mean(dyg * hat, axis=-1, keepdims=True)
        dz = scale * (dyg - one - hat * two)
        return dz

    def norm_sums(dy, dz, n, u, layer, which):
        base = layer * 6
        row_part(base + which, jnp.sum(dy * r.XH[n, u], axis=0, keepdims=True))
        row_part(base + 3 + 2 * which, jnp.sum(dy, axis=0, keepdims=True))
        row_part(base + 2 + 2 * which, jnp.sum(dz, axis=0, keepdims=True))

    lane = lax.broadcasted_iota(jnp.int32, (BLK, 128), 1)
    low_half = lane < 64

    def two_heads(v):
        zero = jnp.zeros_like(v)
        return jnp.concatenate(
            [jnp.where(low_half, v, zero), jnp.where(low_half, zero, v)], axis=0
        )

    def one_row(v):
        return jnp.where(low_half, v[:BLK], v[BLK:])

    def whole(ref):
        return ref[...].reshape(D, ref.shape[-1])

    def half_at(u):
        return pl.ds(u * HALF, HALF)

    w_one(0)

    @pl.when(home)
    def _():
        for n, (src, dst) in enumerate(
            ((tok, r.XB.at[0]), (r.QS0, r.QS), (r.KC0, r.KC), (hb, r.HBB), (ub, r.UBB))
        ):
            pltpu.make_async_copy(src, dst, r.mr.at[n]).start()
            if n < 3:
                remote(src, dst, r.ms.at[n], r.mr.at[n], sib).start()
        pltpu.make_async_copy(r.COTM.at[:, c], r.COT, r.mr.at[5]).start()
        remote(r.COTM.at[:, 1 - c], r.COT, r.ms.at[5], r.mr.at[5], sib).start()

    @pl.when(away)
    def _():
        for n, (src, dst) in ((3, (hb, r.HBB)), (4, (ub, r.UBB))):
            remote(src, dst, r.ms.at[n], r.mr.at[n], (y, zl, zh, x, c)).start()

    for load in loads[2:6]:
        load.wait()
    for layer in range(LAYERS):
        r.PB[layer, :, 0:512] = r.WUF[layer].astype(BF)
        r.PB[layer, :, 512:1024] = r.WDF[layer].astype(BF)
    w_two(0)
    w_one(1)
    for n, dst in enumerate((r.XB.at[0], r.QS, r.KC, r.HBB, r.UBB, r.COT)):
        got(dst, r.mr.at[n])

    def f_send(n, u, hh, buf):
        there, m = buf.at[rows_of(u, x, c)], 2 * n + u

        def one(k):
            xx = lax.rem(x + 2 + k, 4)
            self = home & (xx == x) & (hh == zh)
            when(self, pltpu.make_async_copy(r.FIN.at[n, u], there, r.fr.at[m, t_me]).start)
            unless(
                self,
                remote(
                    r.FIN.at[n, u], there, r.fs.at[m, 4 * hh + xx], r.fr.at[m, t_me],
                    (y, zl, zh, xx, hh),
                ).start,
            )

        loop(4, one)

    def f_wait(n, u, buf):
        loop(
            8,
            lambda t: got(
                buf.at[pl.ds(pl.multiple_of(u * HALF + t * OWN, OWN), OWN)], r.fr.at[2 * n + u, t]
            ),
        )

    def f_done(n, u):
        def one(k):
            xx, hh = lax.rem(k, 4), lax.div(k, 4)
            unless(
                home & (xx == x) & (hh == zh),
                lambda: sent(r.FIN.at[n, u], r.fs.at[2 * n + u, k]),
            )

        loop(8, one)

    for layer in range(LAYERS):
        way, waz = r.WAY.at[layer], r.WAZ.at[layer]
        wby, wbz = r.WBY.at[layer], r.WBZ.at[layer]
        qkv = r.QKV.at[layer]
        s = 2 * layer

        def project(u, layer=layer, way=way, waz=waz, qkv=qkv):
            at = half_at(u)
            rows = r.XB[layer, at, :]
            both = dot(rows, whole(way))
            qkv[at, 0:128] = (both[:, 0:128] + r.HBB[layer, 0:1, :]).astype(BF)
            qkv[at, 128:256] = both[:, 128:256].astype(BF)
            last = dot(rows, whole(waz.at[:, :, :, 0:128]))
            qkv[at, 256:384] = (last + r.HBB[layer, 1:2, :]).astype(BF)

        def attend(j, layer=layer, qkv=qkv):
            at = pl.ds(j * BLK, BLK)
            score = dot(two_heads(qkv[at, 0:128]), qkv[:, 128:256], NT) * 0.125
            allowed = r.QS[at, 0:1] == r.KC[0:1, :]
            score = jnp.where(jnp.concatenate([allowed, allowed], axis=0), score, masked_score)
            weight = jnp.exp(score - jnp.max(score, axis=-1, keepdims=True))
            prob = weight * (1.0 / jnp.sum(weight, axis=-1, keepdims=True))
            r.PR[layer, j] = prob
            r.O[layer, at, :] = one_row(dot(prob.astype(BF), qkv[:, 256:384])).astype(BF)

        def mixed(u, layer=layer, waz=waz):
            return dot(r.O[layer, half_at(u), :], whole(waz.at[:, :, :, 128:256]), NT)

        w_wait(2 * layer)
        if layer == 0:
            project(0)
            project(1)
            w_two(1)
            w_one(2)
        else:
            for u in range(2):
                ag_forward(1, u, r.XB.at[1])
                ag_wait(1, u, r.XB.at[1])
                project(u)
            w_two(3)
        attend(0)
        attend(1)
        rs_push(s, 0, mixed(0))
        attend(2)
        rs_comb(s, 0)
        attend(3)
        rs_push(s, 1, mixed(1))
        rs_comb(s, 1)
        for u in range(2):
            if layer == 0:
                stream = r.XB[0, rows_of(u, x, c), :].astype(F32)
            else:
                stream = r.RES[u]
            z_one = rs_finish(s, u) + stream + gb_row(layer, 2)
            h_val = norm(z_one, 2 * layer, u, gb_row(layer, 0), gb_row(layer, 3))
            r.HB[layer, rows_of(u, x, c), :] = h_val.astype(BF)
            ag_start(2 * layer, u, r.HB.at[layer])
            r.RES[u] = h_val

        def feed(u, layer=layer, wby=wby, wbz=wbz):
            at = half_at(u)
            up = dot(r.HB[layer, at, :], whole(wby)) + r.UBB[layer : layer + 1, :]
            phi = 0.5 * (1.0 + lax.erf(up * 0.7071067811865476))
            r.GP[layer, at, :] = phi + up * jnp.exp(-0.5 * up * up) * 0.3989422804014327
            act = (up * phi).astype(BF)
            r.A[layer, at, :] = act
            return dot(act, whole(wbz), NT)

        w_wait(2 * layer + 1)
        buf = r.HB.at[layer]
        ag_forward(2 * layer, 0, buf)
        ag_wait(2 * layer, 0, buf)
        rs_push(s + 1, 0, feed(0))
        ag_forward(2 * layer, 1, buf)
        rs_comb(s + 1, 0)
        ag_wait(2 * layer, 1, buf)
        rs_push(s + 1, 1, feed(1))
        rs_comb(s + 1, 1)
        if layer == 0:
            w_two(2)
            w_one(3)
        for u in range(2):
            z_two = rs_finish(s + 1, u) + r.RES[u] + gb_row(layer, 4)
            x_val = norm(z_two, 2 * layer + 1, u, gb_row(layer, 1), gb_row(layer, 5))
            if layer == 0:
                r.XB[1, rows_of(u, x, c), :] = x_val.astype(BF)
                ag_start(1, u, r.XB.at[1])
                r.RES[u] = x_val
            else:
                r.FIN[0, u] = x_val.astype(BF)

    def ra_send(k):
        cc, xx = lax.rem(k, 2), lax.div(k, 2)
        when(k == t_me, pltpu.make_async_copy(r.ROWP.at[k], r.RA.at[k], r.rar.at[k]).start)
        unless(
            k == t_me,
            remote(
                r.ROWP.at[k], r.RA.at[t_me], r.ras.at[k], r.rar.at[t_me], (y, zl, cc, xx, zh)
            ).start,
        )

    def row_one():
        loop(8, lambda t: got(r.RA.at[t], r.rar.at[t]))
        r.RW1[...] = jnp.sum(r.RA[...], axis=0)
        y_send(lambda _: r.RW1, r.RY.at[y], r.rys, r.ryr)
        r.RY[y] = r.RW1[...]

    def row_two():
        y_got(lambda yy: r.RY.at[yy], r.ryr)
        r.RW2[...] = jnp.sum(r.RY[...], axis=0)
        z_send(lambda _: r.RW2, r.RZ.at[z], r.rzs, r.rzr, q_me, z, zin)

    def row_three():
        z_got(lambda zz: r.RZ.at[zz], r.rzr)
        r.RW3[...] = jnp.sum(r.RZ[...], axis=0)

        def rc_send(k):
            hh, xx = lax.rem(k, 2), lax.div(k, 2)
            when(k == h_me, pltpu.make_async_copy(r.RW3, r.RC.at[k], r.rcr.at[k]).start)
            unless(
                k == h_me,
                remote(
                    r.RW3, r.RC.at[h_me], r.rcs.at[k], r.rcr.at[h_me], (y, zl, c, xx, hh)
                ).start,
            )

        loop(8, rc_send)

    def col_one():
        y_send(lambda _: r.COL, r.CY.at[y], r.cys, r.cyr)
        r.CY[y] = r.COL[...]

    def col_two():
        y_got(lambda yy: r.CY.at[yy], r.cyr)
        r.COL2[...] = jnp.sum(r.CY[...], axis=0)
        z_send(lambda _: r.COL2, r.CZ.at[z], r.czs, r.czr, q_me, z, zin)

    r.ROWP[...] = jnp.zeros_like(r.ROWP)
    r.COL[...] = jnp.zeros_like(r.COL)
    for layer in (1, 0):
        way, waz = r.WAY.at[layer], r.WAZ.at[layer]
        wby, wbz = r.WBY.at[layer], r.WBZ.at[layer]
        qkv = r.QKV.at[layer]
        ag_a, ag_b = (3, 4) if layer == 1 else (5, 6)
        s = 4 + 2 * (1 - layer)
        df, ds = r.DFB.at[layer], r.DSB.at[layer]

        def grad_a(t, layer=layer):
            at = pl.ds(pl.multiple_of(t * 256, 256), 256)
            lhs = r.XB[layer, :, at]
            r.GAY[layer, t] = dot(lhs, r.DQKV[:, 0:256], TN).astype(BF).reshape(4, 64, 256)
            r.GAZ[layer, t, :, :, 0:128] = (
                dot(lhs, r.DQKV[:, 256:384], TN).astype(BF).reshape(4, 64, 128)
            )
            r.GAZ[layer, t, :, :, 128:256] = (
                dot(r.DSB[layer, :, at], r.O[layer], TN).astype(BF).reshape(4, 64, 128)
            )

        def grad_b(t, layer=layer):
            at = pl.ds(pl.multiple_of(t * 256, 256), 256)
            r.GBY[layer, t] = dot(r.HB[layer, :, at], r.DU[...], TN).astype(BF).reshape(4, 64, 512)
            r.GBZ[layer, t] = (
                dot(r.DFB[layer, :, at], r.A[layer], TN).astype(BF).reshape(4, 64, 512)
            )

        for u in range(2):
            if layer == 1:
                dy = r.COT[u].astype(F32)
            else:
                dy = rs_finish(5, u) + r.RES[u]
            dz = norm_back(dy, 2 * layer + 1, u, layer, 1)
            df[rows_of(u, x, c), :] = dz.astype(BF)
            ag_start(ag_a, u, df)
            r.RES[u] = dz
            norm_sums(dy, dz, 2 * layer + 1, u, layer, 1)
            if layer == 0 and u == 0:
                loop(2, lambda t: grad_one_a(t + 2))
        if layer == 0:
            g_one(2)

        def feed_back(u, layer=layer, wby=wby, wbz=wbz):
            at = half_at(u)
            da = dot(r.DFB[layer, at, :], whole(wbz))
            du = (da * r.GP[layer, at, :]).astype(BF)
            r.DU[at, :] = du
            up_row = 4 * layer + 1
            r.COL[up_row : up_row + 1, :] += jnp.sum(du.astype(F32), axis=0, keepdims=True)
            return dot(du, whole(wby), NT)

        ag_forward(ag_a, 0, df)
        ag_wait(ag_a, 0, df)
        f_send(0, 0, layer, r.LOB)
        rs_push(s, 0, feed_back(0))
        ag_forward(ag_a, 1, df)
        rs_comb(s, 0)
        ag_wait(ag_a, 1, df)
        rs_push(s, 1, feed_back(1))
        rs_comb(s, 1)
        loop(2, grad_b)
        for u in range(2):
            dh = rs_finish(s, u) + r.RES[u]
            dz = norm_back(dh, 2 * layer, u, layer, 0)
            ds[rows_of(u, x, c), :] = dz.astype(BF)
            ag_start(ag_b, u, ds)
            r.RES[u] = dz
            norm_sums(dh, dz, 2 * layer, u, layer, 0)
            if u == 0:
                loop(2, lambda t: grad_b(t + 2))
        g_one(2 * layer + 1)
        if layer == 0:
            loop(8, ra_send)
            g_two(2)

        r.DK[...] = jnp.zeros_like(r.DK)
        r.DV[...] = jnp.zeros_like(r.DV)

        def attend_back(j, layer=layer, waz=waz, qkv=qkv):
            at = pl.ds(j * BLK, BLK)
            do = two_heads(dot(r.DSB[layer, at, :], whole(waz.at[:, :, :, 128:256])).astype(BF))
            prob = r.PR[layer, j]
            dp = dot(do, qkv[:, 256:384], NT)
            inner = jnp.sum(prob * dp, axis=-1, keepdims=True)
            dscore = (prob * (dp - inner)).astype(BF)
            dq = one_row(dot(dscore, qkv[:, 128:256])) * 0.125
            r.DQKV[at, 0:128] = dq.astype(BF)
            r.DK[...] += dot(dscore, two_heads(qkv[at, 0:128]), TN)
            r.DV[...] += dot(prob.astype(BF), do, TN)

        ag_forward(ag_b, 0, ds)
        ag_wait(ag_b, 0, ds)
        f_send(0, 1, layer, r.LOB)
        attend_back(0)
        attend_back(1)
        if layer == 0:
            row_one()
        ag_forward(ag_b, 1, ds)
        ag_wait(ag_b, 1, ds)
        attend_back(2)
        attend_back(3)
        r.DQKV[:, 128:256] = (r.DK[...] * 0.125).astype(BF)
        r.DQKV[:, 256:384] = r.DV[...].astype(BF)
        s += 1

        def input_back(u, way=way, waz=waz):
            at = half_at(u)
            return dot(r.DQKV[at, 0:256], whole(way), NT) + dot(
                r.DQKV[at, 256:384], whole(waz.at[:, :, :, 0:128]), NT
            )

        rs_push(s, 0, input_back(0))
        part = input_back(1)
        rs_comb(s, 0)
        rs_push(s, 1, part)
        rs_comb(s, 1)
        r.COL[4 * layer : 4 * layer + 1, 0:384] = jnp.sum(
            r.DQKV[...].astype(F32), axis=0, keepdims=True
        )
        if layer == 0:
            col_one()
            row_two()
        g_two(2 * layer + 1)
        loop(2, grad_a)
        grad_one_a = grad_a
        if layer == 0:
            loop(2, lambda t: grad_a(t + 2))
            g_one(0)

    for u in range(2):
        r.FIN[1, u] = (rs_finish(7, u) + r.RES[u]).astype(BF)
        f_send(1, u, 0, r.GTB)
        f_send(1, u, 1, r.GTB)
    stores = []

    def store(n, src):
        copy = pltpu.make_async_copy(src, outs[n], r.st.at[n])
        copy.start()
        stores.append(copy)

    row_three()
    col_two()
    g_three(3)
    g_three(2)
    g_three(1)
    store(4, r.GU)
    store(5, r.GD)
    g_two(0)
    f_wait(0, 0, r.LOB)
    f_wait(0, 1, r.LOB)
    store(0, r.LOB)
    z_got(lambda zz: r.CZ.at[zz], r.czr)
    z_sent(lambda _: r.COL2, r.czs, q_me)
    r.COL2[...] = jnp.sum(r.CZ[...], axis=0)
    for layer in range(LAYERS):
        at = 4 * layer
        r.GHB[layer, 0:1, :] = r.COL2[at : at + 1, 0:128]
        r.GHB[layer, 1:2, :] = r.COL2[at : at + 1, 256:384]
        r.GUB[layer : layer + 1, :] = r.COL2[at + 1 : at + 2, :]
    store(6, r.GHB)
    store(7, r.GUB)
    loop(8, lambda t: got(r.RC.at[t], r.rcr.at[t]))
    for p in range(8):
        for layer in range(LAYERS):
            at = 6 * layer
            r.GGN[layer, :, p * 128 : (p + 1) * 128] = r.RC[p, at : at + 2, :]
            r.GBI[layer, :, p * 128 : (p + 1) * 128] = r.RC[p, at + 2 : at + 6, :]
    store(8, r.GGN)
    store(9, r.GBI)
    g_three(0)
    store(2, r.GQ)
    store(3, r.GO)
    for u in range(2):
        f_wait(1, u, r.GTB)
    store(1, r.GTB)

    for lp in range(4):
        w_done(lp)
        g_done(lp)
    gathers = (
        r.HB.at[0], r.XB.at[1], r.HB.at[1], r.DFB.at[1], r.DSB.at[1], r.DFB.at[0], r.DSB.at[0]
    )
    for s, buf in enumerate(gathers):
        for u in range(2):
            ag_done(s, u, buf)
    for u in range(2):
        rs_done(7, u)
        f_done(0, u)
        f_done(1, u)
    y_sent(lambda _: r.RW1, r.rys)
    z_sent(lambda _: r.RW2, r.rzs, q_me)
    y_sent(lambda _: r.COL, r.cys)

    def small_done(k):
        unless(k == t_me, lambda: sent(r.ROWP.at[k], r.ras.at[k]))
        unless(k == h_me, lambda: sent(r.RW3, r.rcs.at[k]))

    loop(8, small_done)

    @pl.when(home)
    def _():
        for n, src in ((0, tok), (1, r.QS0), (2, r.KC0), (5, r.COT)):
            sent(src, r.ms.at[n])

    @pl.when(away)
    def _():
        sent(hb, r.ms.at[3])
        sent(ub, r.ms.at[4])

    for copy in stores:
        copy.wait()


SHAPES = (
    ((2, 3, 64, 128), True, step_rate),
    ((2, 2, 128), False, bias_rate),
    ((2, 64, 128), True, output_rate),
    ((2, 64, 512), True, step_rate),
    ((2, 512), False, bias_rate),
    ((2, 64, 512), True, step_rate),
    ((2, 2, D), False, gain_rate),
    ((2, 4, D), False, bias_rate),
)
N_W = len(SHAPES)


def adam_kernel(*refs):
    lo_in, gt_in = refs[:2]
    grads, states = refs[2 : 2 + N_W], refs[2 + N_W : 2 + 4 * N_W]
    refs = refs[2 + 4 * N_W :]
    lo_out, gt_out = refs[:2]
    outs = refs[2 : 2 + 4 * N_W]
    refs = refs[2 + 4 * N_W :]
    gt_low, gt_full, lo_low = refs[:3]
    held = refs[3 : 3 + 4 * N_W]
    in_sem, out_sem = refs[3 + 4 * N_W :]

    def copy(src, dst, sem):
        made = pltpu.make_async_copy(src, dst, sem)
        made.start()
        return made

    gt_load = copy(gt_in, gt_low, in_sem.at[4 * N_W])
    lo_load = copy(lo_in, lo_low, in_sem.at[4 * N_W + 1])
    loads = []
    for n in range(N_W):
        srcs = (grads[n],) + tuple(states[3 * n : 3 * n + 3])
        loads.append(
            [copy(a, held[4 * n + k], in_sem.at[4 * n + k]) for k, a in enumerate(srcs)]
        )
    gt_load.wait()
    gt_full[...] = gt_low[...].astype(F32)
    last = [copy(gt_full, gt_out, out_sem.at[4 * N_W + 1])]
    lo_load.wait()
    last.append(copy(lo_low, lo_out, out_sem.at[4 * N_W]))
    for n, (_, with_decay, rate) in enumerate(SHAPES):
        for load in loads[n]:
            load.wait()
        g_ref, w_ref, m_ref, v_ref = held[4 * n : 4 * n + 4]
        grad, weight = g_ref[...], w_ref[...]
        first_new = beta_one * m_ref[...] + (1.0 - beta_one) * grad
        second_new = beta_two * v_ref[...] + (1.0 - beta_two) * grad * grad
        first_hat = first_new / (1.0 - beta_one**STEP)
        second_hat = second_new / (1.0 - beta_two**STEP)
        change = first_hat / (jnp.sqrt(second_hat) + eps_adam)
        if with_decay:
            change = change + weight_decay * weight
        m_ref[...] = first_new
        v_ref[...] = second_new
        w_ref[...] = weight - rate * change
        for k, ref in enumerate((g_ref, m_ref, v_ref, w_ref)):
            last.append(copy(ref, outs[4 * n + k], out_sem.at[4 * n + k]))
    for made in last:
        made.wait()


def local(
    tokens, cotangent, bucket_of, seq_lens, w_qkv, head_bias, w_out, w_up, up_bias, w_down, gains,
    biases, first_qkv, second_qkv, first_head, second_head, first_out, second_out, first_up,
    second_up, first_up_bias, second_up_bias, first_down, second_down, first_gains, second_gains,
    first_biases, second_biases,
):
    def turned(v):
        return jnp.swapaxes(v, 1, 2)

    any_ref = pl.BlockSpec(memory_space=pl.ANY)
    smem = pl.BlockSpec(memory_space=pltpu.SMEM)
    wq, wo, wd = turned(w_qkv), turned(w_out), turned(w_down)
    grad_shapes = tuple(jax.ShapeDtypeStruct(shape, F32) for shape, _, _ in SHAPES)
    order = (0, 2, 3, 5, 1, 4, 6, 7)
    rows_low = jax.ShapeDtypeStruct((ROWS, D), BF)
    layer_low, grad_low, *grads = pl.pallas_call(
        kernel,
        out_shape=(rows_low, rows_low) + tuple(grad_shapes[n] for n in order),
        in_specs=[any_ref] * 2 + [smem] * 2 + [any_ref] * 8,
        out_specs=(any_ref,) * N_OUT,
        scratch_shapes=[pltpu.VMEM(s, t) for s, t in SCRATCH.values()]
        + [pltpu.SemaphoreType.DMA(s) for s in SEMS.values()],
        compiler_params=pltpu.CompilerParams(
            collective_id=0, has_side_effects=True, vmem_limit_bytes=63 << 20
        ),
    )(
        tokens, cotangent, bucket_of, seq_lens, wq, head_bias, wo, w_up, up_bias, wd, gains, biases
    )
    grads = [grads[order.index(n)] for n in range(N_W)]
    states = (
        wq, turned(first_qkv), turned(second_qkv), head_bias, first_head, second_head,
        wo, turned(first_out), turned(second_out), w_up, first_up, second_up,
        up_bias, first_up_bias, second_up_bias, wd, turned(first_down), turned(second_down),
        gains, first_gains, second_gains, biases, first_biases, second_biases,
    )
    held = [pltpu.VMEM(shape, F32) for shape, _, _ in SHAPES for _ in range(4)]
    layer_out, grad_tokens, *results = pl.pallas_call(
        adam_kernel,
        out_shape=(rows_low, jax.ShapeDtypeStruct((ROWS, D), F32))
        + tuple(shape for shape in grad_shapes for _ in range(4)),
        in_specs=[any_ref] * (2 + 4 * N_W),
        out_specs=(any_ref,) * (2 + 4 * N_W),
        scratch_shapes=[pltpu.VMEM((ROWS, D), t) for t in (BF, F32, BF)]
        + held
        + [pltpu.SemaphoreType.DMA((4 * N_W + 2,))] * 2,
        compiler_params=pltpu.CompilerParams(vmem_limit_bytes=63 << 20),
    )(layer_low, grad_low, *grads, *states)
    for n in (0, 2, 5):
        results[4 * n : 4 * n + 4] = [turned(v) for v in results[4 * n : 4 * n + 4]]
    return (layer_out, grad_tokens, *results)


def solution(mesh):
    fine = Mesh(mesh.devices.reshape(4, 2, 2, 4, 2), ("y", "zl", "core", "x", "zh"))
    b, t = ("y", "zl", "core"), ("x", "zh")
    qkv, head = P(None, b, None, t), P(None, None, t)
    out, up, up_bias, down, rep = P(None, t, b), P(None, b, t), P(None, t), P(None, t, b), P()
    in_specs = (
        P(b, None), P(b, None), P(b), P(b, None), qkv, head, out, up, up_bias, down, rep, rep,
        qkv, qkv, head, head, out, out, up, up, up_bias, up_bias, down, down, rep, rep, rep, rep,
    )
    out_specs = (P(b, None), P(b, None))
    for spec in (qkv, head, out, up, up_bias, down, rep, rep):
        out_specs += (spec,) * 4
    return jax.shard_map(
        local, mesh=fine, in_specs=in_specs, out_specs=out_specs, check_vma=False
    )
```

```python
import jax
import jax.numpy as jnp
from jax import lax
from jax.experimental import pallas as pl
from jax.experimental.pallas import tpu as pltpu
from jax.sharding import Mesh
from jax.sharding import PartitionSpec as P

LAYERS = 2
STEP = 10
ROWS = 512
D = 1024
BLK = 128
NH = 4
HALF = ROWS // NH
OWN = 64 // NH

eps_norm = 1e-05
beta_one = 0.9
beta_two = 0.999
eps_adam = 1e-08
step_rate = 0.1
output_rate = 0.3
bias_rate = 0.3
gain_rate = 1.0
weight_decay = 0.01
masked_score = -1000000000.0

MESH = pl.DeviceIdType.MESH
BF = jnp.bfloat16
F32 = jnp.float32
NT = (((1,), (1,)), ((), ()))
TN = (((0,), (0,)), ((), ()))
NN = (((1,), (0,)), ((), ()))

SCRATCH = dict(
    XB=((2, ROWS, D), BF),
    HB=((2, ROWS, D), BF),
    DFB=((2, ROWS, D), BF),
    DSB=((2, ROWS, D), BF),
    WQ=((2, 4, 4, 64, 384), BF),
    WO=((2, 4, 4, 64, 128), BF),
    WB=((2, 4, 4, 64, 1024), BF),
    SYQ=((2, 4, 32, 384), BF),
    SYO=((2, 4, 32, 128), BF),
    SYB=((2, 4, 32, 1024), BF),
    GA=((2, 4, 4, 64, 512), BF),
    GB=((2, 4, 4, 64, 1024), BF),
    R1AY=((2, 4, 4, 32, 512), BF),
    R1AZ=((2, 4, 4, 32, 512), BF),
    R1BY=((2, 4, 4, 32, 1024), BF),
    R1BZ=((2, 4, 4, 32, 1024), BF),
    S2AY=((2, 4, 32, 512), BF),
    S2AZ=((2, 4, 32, 512), BF),
    S2BY=((2, 4, 32, 1024), BF),
    S2BZ=((2, 4, 32, 1024), BF),
    R2AY=((2, 4, 32, 512), BF),
    R2AZ=((2, 4, 32, 512), BF),
    R2BY=((2, 4, 32, 1024), BF),
    R2BZ=((2, 4, 32, 1024), BF),
    QKV=((2, ROWS, 384), BF),
    O=((2, ROWS, 128), BF),
    PR=((2, 4, 2 * BLK, ROWS), F32),
    A=((2, ROWS, 512), BF),
    GP=((2, ROWS, 512), F32),
    DU=((ROWS, 512), BF),
    DQKV=((ROWS, 384), BF),
    DK=((ROWS, 128), F32),
    DV=((ROWS, 128), F32),
    PART=((NH, 4, 2, OWN, D), BF),
    SND=((NH, 4, OWN, D), BF),
    CR=((NH, 4, OWN, D), BF),
    XR=((NH, 4, OWN, D), BF),
    OWNSUM=((NH, OWN, D), F32),
    RES=((NH, OWN, D), F32),
    XH=((4, NH, OWN, D), F32),
    SC=((4, NH, OWN, 128), F32),
    COT=((NH, OWN, D), BF),
    COTF=((2, NH, OWN, D), BF),
    COTM=((2, NH, OWN, D), BF),
    QS0=((ROWS, 128), F32),
    KC0=((8, ROWS), F32),
    QS=((ROWS, 128), F32),
    KC=((8, ROWS), F32),
    WQF=((2, 3, 64, 128), F32),
    WOF=((2, 64, 128), F32),
    WUF=((2, 64, 512), F32),
    WDF=((2, 64, 512), F32),
    PQ=((2, 64, 384), BF),
    PO=((2, 64, 128), BF),
    PB=((2, 64, 1024), BF),
    GNS=((2, 2, D), F32),
    BIS=((2, 4, D), F32),
    HBB=((2, 2, 128), F32),
    UBB=((2, 512), F32),
    GQ=((2, 3, 64, 128), F32),
    GO=((2, 64, 128), F32),
    GU=((2, 64, 512), F32),
    GD=((2, 64, 512), F32),
    GHB=((2, 2, 128), F32),
    GUB=((2, 512), F32),
    GGN=((2, 2, D), F32),
    GBI=((2, 4, D), F32),
    LOB=((ROWS, D), BF),
    GTB=((ROWS, D), BF),
    FIN=((2, NH, OWN, D), BF),
    COL=((8, 512), F32),
    CY=((4, 8, 512), F32),
    COL2=((8, 512), F32),
    CZ=((4, 8, 512), F32),
    ROWP=((16, D), F32),
    RA=((8, 16, 128), F32),
    RW1=((16, 128), F32),
    RY=((4, 16, 128), F32),
    RW2=((16, 128), F32),
    RZ=((4, 16, 128), F32),
    RW3=((16, 128), F32),
    RC=((8, 16, 128), F32),
)
SEMS = dict(
    wsy1=6, wry1=6, wsy2=6, wry2=6, wsz1=6, wrz1=6, wsz2=6, wrz2=6,
    gsy1=4, gry1=4, gsy2=4, gry2=4, gsz1=4, grz1=4, gsz2=4, grz2=4,
    cs=NH, cr=NH, xs=NH, xr=NH, ags=NH, acr=NH, ax1=NH, ax2=NH,
    fs=2 * NH, fr=2 * NH, fzs=2 * NH, fzr=2 * NH, fxs=2 * NH, ras=1, rar=1, rys=1, ryr=1, rzs=1, rzr=1,
    rcs=1, rcr=1, cys=1, cyr=1, czs=1, czr=1, ms=6, mr=6, ld=6 + 2 * NH, st=10,
)
N_IN, N_OUT = 12, 10


class Refs:
    pass


def loop(n, body):
    def step(k, carry):
        body(k)
        return carry

    lax.fori_loop(0, n, step, 0)


def dot(a, b, dims=NN):
    return lax.dot_general(a, b, dims, preferred_element_type=F32)


def kernel(*refs):
    tok, cot, bucket, lens, wq, hb, wo, wu, ub, wd, gains, biases = refs[:N_IN]
    outs = refs[N_IN : N_IN + N_OUT]
    r = Refs()
    for name, ref in zip(list(SCRATCH) + list(SEMS), refs[N_IN + N_OUT :], strict=True):
        setattr(r, name, ref)

    y, zl, c = lax.axis_index("y"), lax.axis_index("zl"), lax.axis_index("core")
    x, zh = lax.axis_index("x"), lax.axis_index("zh")
    z = zh * 2 + zl
    q_me = zl * 2 + c
    t_me = x * 2 + c
    h_me = x * 2 + zh
    home = c == zh
    away = c != zh
    sib = (y, zl, 1 - c, x, zh)

    def xdev(j):
        return (y, zl, c, j, zh)

    def ydev(yy):
        return (yy, zl, c, x, zh)

    def zout(zz):
        return (y, lax.rem(zz, 2), zh, x, lax.div(zz, 2))

    def zin(q):
        return (y, lax.div(q, 2), lax.rem(q, 2), x, c)

    def remote(src, dst, ss, rs, dev):
        return pltpu.make_async_remote_copy(
            src_ref=src, dst_ref=dst, send_sem=ss, recv_sem=rs, device_id=dev, device_id_type=MESH
        )

    def got(dst, sem):
        remote(dst, dst, sem, sem, sib).wait_recv()

    def sent(src, sem):
        remote(src, src, sem, sem, sib).wait_send()

    def when(cond, body):
        pl.when(cond)(body)

    def unless(cond, body):
        pl.when(jnp.logical_not(cond))(body)

    def others(me, body):
        for d in (2, 1, 3):
            body(lax.rem(me + d, 4))

    bar = pltpu.get_barrier_semaphore()

    def greet(dev):
        pl.semaphore_signal(bar, inc=1, device_id=dev, device_id_type=MESH)

    def greet_plane(i):
        cc, rest = lax.rem(i, 2), lax.div(i, 2)
        hh, xx = lax.rem(rest, 2), lax.div(rest, 2)
        unless((cc == c) & (hh == zh) & (xx == x), lambda: greet((y, zl, cc, xx, hh)))

    others(y, lambda yy: greet(ydev(yy)))
    for n in range(2):
        greet((y, 1 - zl, zh, x, n))
        greet((y, 1 - zl, n, x, c))
    loop(16, greet_plane)

    def rows_of(u, j, core):
        return pl.ds(pl.multiple_of(u * HALF + (j * 2 + core) * OWN, OWN), OWN)

    def half_at(u):
        return pl.ds(u * HALF, HALF)

    loads = [
        (wq, r.WQF), (wo, r.WOF), (wu, r.WUF), (wd, r.WDF), (gains, r.GNS), (biases, r.BIS)
    ]
    for u in range(NH):
        for core in range(2):
            loads.append((cot.at[rows_of(u, x, core)], r.COTF.at[core, u]))
    loads = [pltpu.make_async_copy(a, b, r.ld.at[n]) for n, (a, b) in enumerate(loads)]
    for load in loads:
        load.start()
    for load in loads[:2]:
        load.wait()
    for layer in range(LAYERS):
        for n in range(3):
            r.PQ[layer, :, n * 128 : (n + 1) * 128] = r.WQF[layer, n].astype(BF)
        r.PO[layer] = r.WOF[layer].astype(BF)
    b = bucket[0]
    slots = jnp.where(b == 0, 1, jnp.where(b == 1, 2, jnp.where(b == 2, 4, 8)))
    size = jnp.where(b == 0, 512, jnp.where(b == 1, 256, jnp.where(b == 2, 128, 64)))

    def slot_and_valid(pos):
        slot = lax.shift_right_logical(pos * slots, 9)
        length = jnp.zeros_like(pos)
        for n in range(8):
            length = jnp.where(slot == n, lens[0, n], length)
        return slot, pos - slot * size < length

    pos = lax.broadcasted_iota(jnp.int32, (8, ROWS), 1)
    slot, valid = slot_and_valid(pos)
    r.KC0[...] = jnp.where(valid, slot, -1).astype(F32)
    pos = lax.broadcasted_iota(jnp.int32, (ROWS, 128), 0)
    r.QS0[...] = lax.shift_right_logical(pos * slots, 9).astype(F32)
    for load in loads[6:]:
        load.wait()
    for u in range(NH):
        for core in range(2):
            first = u * HALF + (x * 2 + core) * OWN
            slot, valid = slot_and_valid(first + lax.broadcasted_iota(jnp.int32, (OWN, 128), 0))
            keep = jnp.where(valid, 1.0, 0.0)[:, 0:1]
            r.COTM[core, u] = (r.COTF[core, u].astype(F32) * keep).astype(BF)
    pl.semaphore_wait(bar, 22)

    def y_send(src, dst, ss, rs):
        others(y, lambda yy: remote(src(yy), dst, ss, rs, ydev(yy)).start())

    def z_send(src, dst, ss, rs, me, dev):
        def one(k):
            n = lax.rem(me + k, 4)
            local = home & (k == 0)
            when(local, pltpu.make_async_copy(src(n), dst, rs).start)
            unless(local, remote(src(n), dst, ss, rs, dev(n)).start)

        loop(4, one)

    def z_sent(all_four, ss):
        when(home, lambda: sent(all_four.at[0:3], ss))
        when(away, lambda: sent(all_four, ss))

    def w_refs(lp):
        layer, part = divmod(lp, 3)
        src, mid, dst = ((r.PQ, r.SYQ, r.WQ), (r.PO, r.SYO, r.WO), (r.PB, r.SYB, r.WB))[part]
        return src.at[layer], mid.at[layer], dst.at[layer]

    low_rows, high_rows = pl.ds(0, 32), pl.ds(32, 32)

    def w_one(lp):
        src, mid, dst = w_refs(lp)
        low, high = src.at[low_rows], src.at[high_rows]
        y_send(lambda _: low, mid.at[y], r.wsy1.at[lp], r.wry1.at[lp])
        mid[y] = low[...]
        z_send(
            lambda _: high, dst.at[y, q_me, high_rows], r.wsz1.at[lp], r.wrz1.at[lp], z, zout
        )

    def w_two(lp):
        src, mid, dst = w_refs(lp)
        got(mid.at[0:3], r.wry1.at[lp])
        z_send(lambda _: mid, dst.at[:, q_me, low_rows], r.wsy2.at[lp], r.wry2.at[lp], z, zout)
        mine = dst.at[y, :, high_rows]
        got(mine, r.wrz1.at[lp])
        y_send(lambda _: mine, mine, r.wsz2.at[lp], r.wrz2.at[lp])

    def w_wait(lp):
        src, mid, dst = w_refs(lp)
        got(dst.at[:, :, low_rows], r.wry2.at[lp])
        got(dst.at[0:3, :, high_rows], r.wrz2.at[lp])

    def w_done(lp):
        src, mid, dst = w_refs(lp)
        sent(mid.at[0:3], r.wsy1.at[lp])
        z_sent(dst.at[0, :, high_rows], r.wsz1.at[lp])
        z_sent(dst.at[:, :, low_rows], r.wsy2.at[lp])
        sent(dst.at[0:3, :, high_rows], r.wsz2.at[lp])

    def g_refs(lp):
        layer, part = divmod(lp, 2)
        if part == 0:
            group = (r.GA, r.R1AY, r.R1AZ, r.S2AY, r.S2AZ, r.R2AY, r.R2AZ)
        else:
            group = (r.GB, r.R1BY, r.R1BZ, r.S2BY, r.S2BZ, r.R2BY, r.R2BZ)
        return [ref.at[layer] for ref in group]

    def g_one(lp):
        full, r1y, r1z = g_refs(lp)[:3]
        z_send(
            lambda q: full.at[:, q, low_rows], r1y.at[z], r.gsy1.at[lp], r.gry1.at[lp], q_me, zin
        )
        y_send(lambda yy: full.at[yy, :, high_rows], r1z.at[y], r.gsz1.at[lp], r.grz1.at[lp])

    def g_two(lp):
        full, r1y, r1z, s2y, s2z, r2y, r2z = g_refs(lp)
        got(r1y, r.gry1.at[lp])

        def sum_y(n):
            total = r1y[0, n].astype(F32)
            for k in range(1, 4):
                total = total + r1y[k, n].astype(F32)
            s2y[n] = total.astype(BF)

        loop(4, sum_y)
        y_send(lambda yy: s2y.at[yy], r2y.at[y], r.gsy2.at[lp], r.gry2.at[lp])
        got(r1z.at[0:3], r.grz1.at[lp])

        def sum_z(n):
            total = full[y, n, 32:64, :].astype(F32)
            for d in (1, 2, 3):
                total = total + r1z[lax.rem(y + d, 4), n].astype(F32)
            s2z[n] = total.astype(BF)

        loop(4, sum_z)
        z_send(lambda q: s2z.at[q], r2z.at[z], r.gsz2.at[lp], r.grz2.at[lp], q_me, zin)

    def g_three(lp):
        full, r1y, r1z, s2y, s2z, r2y, r2z = g_refs(lp)
        layer, part = divmod(lp, 2)

        def put(rows, total):
            if part == 0:
                for n in range(3):
                    r.GQ[layer, n, rows, :] = total[:, n * 128 : (n + 1) * 128]
                r.GO[layer, rows, :] = total[:, 384:512]
            else:
                r.GU[layer, rows, :] = total[:, 0:512]
                r.GD[layer, rows, :] = total[:, 512:1024]

        got(r2y.at[0:3], r.gry2.at[lp])
        total = s2y[y].astype(F32)
        for d in (1, 2, 3):
            total = total + r2y[lax.rem(y + d, 4)].astype(F32)
        put(low_rows, total)
        got(r2z, r.grz2.at[lp])
        total = r2z[0].astype(F32)
        for k in range(1, 4):
            total = total + r2z[k].astype(F32)
        put(high_rows, total)

    def g_done(lp):
        full, r1y, r1z, s2y, s2z, r2y, r2z = g_refs(lp)
        z_sent(r1y, r.gsy1.at[lp])
        sent(r1z.at[0:3], r.gsz1.at[lp])
        sent(r2y.at[0:3], r.gsy2.at[lp])
        z_sent(r2z, r.gsz2.at[lp])

    def ag_sent(u):
        sent(r.XB.at[0, 0 : 7 * OWN], r.ags.at[u])

    def ag_start(u, buf, first=False):
        if not first:
            ag_sent(u)
        own = buf.at[rows_of(u, x, c)]
        remote(own, own, r.ags.at[u], r.acr.at[u], sib).start()
        for d, arrived in ((2, r.ax2), (1, r.ax1), (3, r.ax1)):
            remote(own, own, r.ags.at[u], arrived.at[u], xdev(lax.rem(x + d, 4))).start()

    def ag_forward(u, buf):
        got(buf.at[0 : 2 * OWN], r.ax1.at[u])
        for d in (1, 3, 2):
            part = buf.at[rows_of(u, lax.rem(x + d, 4), c)]
            if d == 2:
                got(part, r.ax2.at[u])
            remote(part, part, r.ags.at[u], r.acr.at[u], sib).start()

    def ag_wait(u, buf):
        got(buf.at[0 : 4 * OWN], r.acr.at[u])

    def ag_stage(buf, body):
        ag_forward(0, buf)
        for u in range(NH):
            if u < NH - 1:
                ag_forward(u + 1, buf)
            ag_wait(u, buf)
            body(u)

    def ag_rs_stage(buf, first_half, second_half):
        ag_forward(0, buf)
        for u in range(NH):
            if u < NH - 1:
                ag_forward(u + 1, buf)
            ag_wait(u, buf)
            rs_push(u, second_half(u, first_half(u)))
            if u > 0:
                rs_comb(u - 1)
        rs_comb(NH - 1)

    def rs_sent(u):
        sent(r.SND.at[u, 0:3], r.xs.at[u])
        sent(r.PART.at[u, :, 1 - c], r.cs.at[u])

    def rs_push(u, part, first=False):
        if not first:
            rs_sent(u)
        r.PART[u] = part.astype(BF).reshape(4, 2, OWN, D)
        remote(r.PART.at[u, :, 1 - c], r.CR.at[u], r.cs.at[u], r.cr.at[u], sib).start()

    def rs_comb(u):
        got(r.CR.at[u], r.cr.at[u])
        both = r.PART[u, :, c].astype(F32) + r.CR[u].astype(F32)
        r.SND[u] = both.astype(BF)
        others(
            x,
            lambda j: remote(
                r.SND.at[u, j], r.XR.at[u, x], r.xs.at[u], r.xr.at[u], xdev(j)
            ).start(),
        )
        r.OWNSUM[u] = r.PART[u, x, c].astype(F32) + r.CR[u, x].astype(F32)

    def rs_finish(u):
        got(r.XR.at[u, 0:3], r.xr.at[u])
        total = r.OWNSUM[u]
        for d in (1, 3, 2):
            total = total + r.XR[u, lax.rem(x + d, 4)].astype(F32)
        return total

    def gb_row(layer, n):
        return r.GNS[layer, n : n + 1, :] if n < 2 else r.BIS[layer, n - 2 : n - 1, :]

    def norm(values, n, u, gain, shift):
        centred = values - jnp.mean(values, axis=-1, keepdims=True)
        scale = lax.rsqrt(jnp.mean(centred * centred, axis=-1, keepdims=True) + eps_norm)
        hat = centred * scale
        r.XH[n, u] = hat
        r.SC[n, u] = jnp.broadcast_to(scale, (OWN, 128))
        return hat * gain + shift

    def norm_back(dy, n, u, layer, which):
        hat = r.XH[n, u]
        scale = r.SC[n, u][:, 0:1]
        dyg = dy * gb_row(layer, which)
        one = jnp.mean(dyg, axis=-1, keepdims=True)
        two = jnp.mean(dyg * hat, axis=-1, keepdims=True)
        return scale * (dyg - one - hat * two)

    def norm_sums(dy, dz, n, u, layer, which):
        def add(row, values):
            at = layer * 6 + row
            r.ROWP[at : at + 1, :] += jnp.sum(values, axis=0, keepdims=True)

        add(which, dy * r.XH[n, u])
        add(3 + 2 * which, dy)
        add(2 + 2 * which, dz)

    lane = lax.broadcasted_iota(jnp.int32, (BLK, 128), 1)
    low_half = lane < 64

    def two_heads(v):
        zero = jnp.zeros_like(v)
        return jnp.concatenate(
            [jnp.where(low_half, v, zero), jnp.where(low_half, zero, v)], axis=0
        )

    def one_row(v):
        return jnp.where(low_half, v[:BLK], v[BLK:])

    def whole(ref):
        return ref[...].reshape(D, ref.shape[-1])

    w_one(0)
    w_one(1)

    @pl.when(home)
    def _():
        for n, (src, dst) in enumerate(
            ((tok, r.XB.at[0]), (r.QS0, r.QS), (r.KC0, r.KC), (hb, r.HBB), (ub, r.UBB))
        ):
            pltpu.make_async_copy(src, dst, r.mr.at[n]).start()
            if n < 3:
                remote(src, dst, r.ms.at[n], r.mr.at[n], sib).start()
        pltpu.make_async_copy(r.COTM.at[c], r.COT, r.mr.at[5]).start()
        remote(r.COTM.at[1 - c], r.COT, r.ms.at[5], r.mr.at[5], sib).start()

    @pl.when(away)
    def _():
        for n, (src, dst) in ((3, (hb, r.HBB)), (4, (ub, r.UBB))):
            remote(src, dst, r.ms.at[n], r.mr.at[n], (y, zl, zh, x, c)).start()

    for load in loads[2:6]:
        load.wait()
    for layer in range(LAYERS):
        r.PB[layer, :, 0:512] = r.WUF[layer].astype(BF)
        r.PB[layer, :, 512:1024] = r.WDF[layer].astype(BF)
    w_two(0)
    w_two(1)
    w_one(2)
    for n, dst in enumerate((r.XB.at[0], r.QS, r.KC, r.HBB, r.UBB, r.COT)):
        got(dst, r.mr.at[n])

    def f_far(n, u, buf):
        m = NH * n + u
        there = buf.at[rows_of(u, x, c)]
        remote(r.FIN.at[n, u], there, r.fzs.at[m], r.fzr.at[m], (y, zl, zh, x, 1 - zh)).start()

    def f_near(n, u, buf):
        there, m = buf.at[rows_of(u, x, c)], NH * n + u
        for d in (2, 1, 3):
            dev = (y, zl, zh, lax.rem(x + d, 4), zh)
            remote(r.FIN.at[n, u], there, r.fs.at[m], r.fr.at[m], dev).start()
        when(home, pltpu.make_async_copy(r.FIN.at[n, u], there, r.fr.at[m]).start)
        when(away, remote(r.FIN.at[n, u], there, r.fs.at[m], r.fr.at[m], sib).start)

    def f_relay(n, u, buf):
        m = NH * n + u
        both = buf.at[pl.ds(pl.multiple_of(u * HALF + x * 2 * OWN, 2 * OWN), 2 * OWN)]

        @pl.when(away)
        def _():
            got(both, r.fzr.at[m])
            others(x, lambda j: remote(both, both, r.fxs.at[m], r.fr.at[m], xdev(j)).start())

    def f_wait(n, u, buf):
        m = NH * n + u
        when(home, lambda: got(buf.at[0 : 8 * OWN], r.fr.at[m]))
        when(away, lambda: got(buf.at[0 : 6 * OWN], r.fr.at[m]))

    def f_done(n, u):
        m = NH * n + u
        sent(r.LOB.at[0:OWN], r.fzs.at[m])
        when(home, lambda: sent(r.LOB.at[0 : 3 * OWN], r.fs.at[m]))

        @pl.when(away)
        def _():
            sent(r.LOB.at[0 : 4 * OWN], r.fs.at[m])
            sent(r.LOB.at[0 : 6 * OWN], r.fxs.at[m])

    for layer in range(LAYERS):
        w_q, w_o, w_b = r.WQ.at[layer], r.WO.at[layer], r.WB.at[layer]
        w_up, w_down = w_b.at[:, :, :, 0:512], w_b.at[:, :, :, 512:1024]
        qkv = r.QKV.at[layer]

        def project(at, layer=layer, w_q=w_q, qkv=qkv):
            out = dot(r.XB[layer, at, :], whole(w_q))
            qkv[at, 0:128] = (out[:, 0:128] + r.HBB[layer, 0:1, :]).astype(BF)
            qkv[at, 128:256] = out[:, 128:256].astype(BF)
            qkv[at, 256:384] = (out[:, 256:384] + r.HBB[layer, 1:2, :]).astype(BF)

        def attend(j, layer=layer, qkv=qkv):
            at = pl.ds(j * BLK, BLK)
            score = dot(two_heads(qkv[at, 0:128]), qkv[:, 128:256], NT) * 0.125
            allowed = r.QS[at, 0:1] == r.KC[0:1, :]
            score = jnp.where(jnp.concatenate([allowed, allowed], axis=0), score, masked_score)
            weight = jnp.exp(score - jnp.max(score, axis=-1, keepdims=True))
            prob = weight * (1.0 / jnp.sum(weight, axis=-1, keepdims=True))
            r.PR[layer, j] = prob
            r.O[layer, at, :] = one_row(dot(prob.astype(BF), qkv[:, 256:384])).astype(BF)

        w_wait(3 * layer)
        if layer == 0:
            w_two(2)
            for lp in (3, 4, 5):
                w_one(lp)
            for u in range(2):
                project(pl.ds(u * 256, 256))
        else:
            ag_stage(r.XB.at[1], lambda u: project(half_at(u)))
        w_wait(3 * layer + 1)
        for u in range(NH):
            for j in range(u * 4 // NH, (u + 1) * 4 // NH):
                attend(j)
            if u > 0:
                rs_comb(u - 1)
            rs_push(u, dot(r.O[layer, half_at(u), :], whole(w_o), NT), first=layer == 0)
        rs_comb(NH - 1)
        for u in range(NH):
            if layer == 0:
                stream = r.XB[0, rows_of(u, x, c), :].astype(F32)
            else:
                stream = r.RES[u]
            z_one = rs_finish(u) + stream + gb_row(layer, 2)
            h_val = norm(z_one, 2 * layer, u, gb_row(layer, 0), gb_row(layer, 3))
            r.HB[layer, rows_of(u, x, c), :] = h_val.astype(BF)
            ag_start(u, r.HB.at[layer], first=layer == 0)
            r.RES[u] = h_val
        w_wait(3 * layer + 2)
        if layer == 0:
            w_two(3)
            w_two(4)

        def feed(u, layer=layer, w_up=w_up):
            at = half_at(u)
            up = dot(r.HB[layer, at, :], whole(w_up)) + r.UBB[layer : layer + 1, :]
            phi = 0.5 * (1.0 + lax.erf(up * 0.7071067811865476))
            act = (up * phi).astype(BF)
            r.A[layer, at, :] = act
            r.GP[layer, at, :] = phi + up * jnp.exp(-0.5 * up * up) * 0.3989422804014327
            return act

        ag_rs_stage(
            r.HB.at[layer], feed, lambda u, act, w_down=w_down: dot(act, whole(w_down), NT)
        )
        if layer == 0:
            w_two(5)
        for u in range(NH):
            z_two = rs_finish(u) + r.RES[u] + gb_row(layer, 4)
            x_val = norm(z_two, 2 * layer + 1, u, gb_row(layer, 1), gb_row(layer, 5))
            if layer == 0:
                r.XB[1, rows_of(u, x, c), :] = x_val.astype(BF)
                ag_start(u, r.XB.at[1])
                r.RES[u] = x_val
            else:
                r.FIN[0, u] = x_val.astype(BF)
                f_far(0, u, r.LOB)

    def ra_send(k):
        cc, xx = lax.rem(k, 2), lax.div(k, 2)
        piece = r.ROWP.at[:, pl.ds(pl.multiple_of(k * 128, 128), 128)]
        when(k == t_me, pltpu.make_async_copy(piece, r.RA.at[t_me], r.rar.at[0]).start)
        unless(
            k == t_me,
            remote(piece, r.RA.at[t_me], r.ras.at[0], r.rar.at[0], (y, zl, cc, xx, zh)).start,
        )

    def row_one():
        got(r.RA, r.rar.at[0])
        r.RW1[...] = jnp.sum(r.RA[...], axis=0)
        y_send(lambda _: r.RW1, r.RY.at[y], r.rys.at[0], r.ryr.at[0])
        r.RY[y] = r.RW1[...]

    def row_two():
        got(r.RY.at[0:3], r.ryr.at[0])
        r.RW2[...] = jnp.sum(r.RY[...], axis=0)
        z_send(lambda _: r.RW2, r.RZ.at[z], r.rzs.at[0], r.rzr.at[0], q_me, zin)

    def row_three():
        got(r.RZ, r.rzr.at[0])
        r.RW3[...] = jnp.sum(r.RZ[...], axis=0)

        def rc_send(k):
            hh, xx = lax.rem(k, 2), lax.div(k, 2)
            there = r.RC.at[h_me]
            when(k == h_me, pltpu.make_async_copy(r.RW3, there, r.rcr.at[0]).start)
            unless(
                k == h_me,
                remote(r.RW3, there, r.rcs.at[0], r.rcr.at[0], (y, zl, c, xx, hh)).start,
            )

        loop(8, rc_send)

    def col_one():
        y_send(lambda _: r.COL, r.CY.at[y], r.cys.at[0], r.cyr.at[0])
        r.CY[y] = r.COL[...]

    def col_two():
        got(r.CY.at[0:3], r.cyr.at[0])
        r.COL2[...] = jnp.sum(r.CY[...], axis=0)
        z_send(lambda _: r.COL2, r.CZ.at[z], r.czs.at[0], r.czr.at[0], q_me, zin)

    r.ROWP[...] = jnp.zeros_like(r.ROWP)
    r.COL[...] = jnp.zeros_like(r.COL)

    late = []
    for layer in (1, 0):
        w_q, w_o, w_b = r.WQ.at[layer], r.WO.at[layer], r.WB.at[layer]
        w_up, w_down = w_b.at[:, :, :, 0:512], w_b.at[:, :, :, 512:1024]
        qkv = r.QKV.at[layer]
        df, ds = r.DFB.at[layer], r.DSB.at[layer]

        def grad_a(t, layer=layer):
            at = pl.ds(t * 256, 256)
            one = dot(r.XB[layer, :, at], r.DQKV[...], TN)
            r.GA[layer, t, :, :, 0:384] = one.astype(BF).reshape(4, 64, 384)
            two = dot(r.DSB[layer, :, at], r.O[layer], TN)
            r.GA[layer, t, :, :, 384:512] = two.astype(BF).reshape(4, 64, 128)

        def grad_b(t, layer=layer):
            at = pl.ds(t * 256, 256)
            one = dot(r.HB[layer, :, at], r.DU[...], TN)
            r.GB[layer, t, :, :, 0:512] = one.astype(BF).reshape(4, 64, 512)
            two = dot(r.DFB[layer, :, at], r.A[layer], TN)
            r.GB[layer, t, :, :, 512:1024] = two.astype(BF).reshape(4, 64, 512)

        for u in range(NH):
            dy = r.COT[u].astype(F32) if layer == 1 else rs_finish(u) + r.RES[u]
            dz = norm_back(dy, 2 * layer + 1, u, layer, 1)
            df[rows_of(u, x, c), :] = dz.astype(BF)
            ag_start(u, df)
            r.RES[u] = dz
            norm_sums(dy, dz, 2 * layer + 1, u, layer, 1)
            if late and u < NH - 1:
                late.pop()()
        while late:
            late.pop()()
        if layer == 0:
            g_one(2)
            g_two(3)

        def feed_back(u, layer=layer, w_down=w_down):
            at = half_at(u)
            da = dot(r.DFB[layer, at, :], whole(w_down))
            du = (da * r.GP[layer, at, :]).astype(BF)
            r.DU[at, :] = du
            return du

        ag_rs_stage(df, feed_back, lambda u, du, w_up=w_up: dot(du, whole(w_up), NT))
        r.COL[4 * layer + 1 : 4 * layer + 2, :] = jnp.sum(
            r.DU[...].astype(F32), axis=0, keepdims=True
        )
        late = [lambda t=t: grad_b(t) for t in (3, 2)]
        grad_b(0)
        grad_b(1)
        for u in range(NH):
            dh = rs_finish(u) + r.RES[u]
            dz = norm_back(dh, 2 * layer, u, layer, 0)
            ds[rows_of(u, x, c), :] = dz.astype(BF)
            ag_start(u, ds)
            r.RES[u] = dz
            norm_sums(dh, dz, 2 * layer, u, layer, 0)
            if late and u < NH - 1:
                late.pop()()
        while late:
            late.pop()()
        g_one(2 * layer + 1)
        if layer == 0:
            loop(8, ra_send)
            g_two(2)

        r.DK[...] = jnp.zeros_like(r.DK)
        r.DV[...] = jnp.zeros_like(r.DV)

        def attend_back(j, layer=layer, w_o=w_o, qkv=qkv):
            at = pl.ds(j * BLK, BLK)
            do = two_heads(dot(r.DSB[layer, at, :], whole(w_o)).astype(BF))
            prob = r.PR[layer, j]
            dp = dot(do, qkv[:, 256:384], NT)
            inner = jnp.sum(prob * dp, axis=-1, keepdims=True)
            dscore = (prob * (dp - inner)).astype(BF)
            dq = one_row(dot(dscore, qkv[:, 128:256])) * 0.125
            r.DQKV[at, 0:128] = dq.astype(BF)
            r.DK[...] += dot(dscore, two_heads(qkv[at, 0:128]), TN)
            r.DV[...] += dot(prob.astype(BF), do, TN)

        def chunk_back(u, layer=layer):
            for j in range(u * 4 // NH, (u + 1) * 4 // NH):
                attend_back(j)
            if u >= NH - 2:
                step = f_near if u == NH - 2 else f_relay
                for n in range(NH // 2):
                    step(0, n + (1 - layer) * NH // 2, r.LOB)
            if u == 0 and layer == 0:
                row_one()

        ag_stage(ds, chunk_back)
        r.DQKV[:, 128:256] = (r.DK[...] * 0.125).astype(BF)
        r.DQKV[:, 256:384] = r.DV[...].astype(BF)
        for u in range(NH):
            part = dot(r.DQKV[half_at(u), :], whole(w_q), NT)
            if u > 0:
                rs_comb(u - 1)
            rs_push(u, part)
        rs_comb(NH - 1)
        r.COL[4 * layer : 4 * layer + 1, 0:384] = jnp.sum(
            r.DQKV[...].astype(F32), axis=0, keepdims=True
        )
        if layer == 0:
            col_one()
            row_two()
        late = [lambda t=t, f=grad_a: f(t) for t in (3, 2, 1)]
        grad_a(0)

    for u in range(NH):
        r.FIN[1, u] = (rs_finish(u) + r.RES[u]).astype(BF)
        f_far(1, u, r.GTB)
        f_near(1, u, r.GTB)
        if late:
            late.pop()()
        if u == NH - 2:
            while late:
                late.pop()()
            g_one(0)
            g_two(1)
    stores = []

    def store(n, src):
        copy = pltpu.make_async_copy(src, outs[n], r.st.at[n])
        copy.start()
        stores.append(copy)

    for u in range(NH):
        f_relay(1, u, r.GTB)
    row_three()
    col_two()
    g_two(0)
    g_three(3)
    g_three(2)
    g_three(1)
    store(4, r.GU)
    store(5, r.GD)
    for u in range(NH):
        f_wait(0, u, r.LOB)
    store(0, r.LOB)
    got(r.CZ, r.czr.at[0])
    z_sent(r.CZ, r.czs.at[0])
    r.COL2[...] = jnp.sum(r.CZ[...], axis=0)
    for layer in range(LAYERS):
        at = 4 * layer
        r.GHB[layer, 0:1, :] = r.COL2[at : at + 1, 0:128]
        r.GHB[layer, 1:2, :] = r.COL2[at : at + 1, 256:384]
        r.GUB[layer : layer + 1, :] = r.COL2[at + 1 : at + 2, :]
    store(6, r.GHB)
    store(7, r.GUB)
    got(r.RC, r.rcr.at[0])
    for p in range(8):
        for layer in range(LAYERS):
            at = 6 * layer
            r.GGN[layer, :, p * 128 : (p + 1) * 128] = r.RC[p, at : at + 2, :]
            r.GBI[layer, :, p * 128 : (p + 1) * 128] = r.RC[p, at + 2 : at + 6, :]
    store(8, r.GGN)
    store(9, r.GBI)
    g_three(0)
    store(2, r.GQ)
    store(3, r.GO)
    for u in range(NH):
        f_wait(1, u, r.GTB)
    store(1, r.GTB)

    for lp in range(6):
        w_done(lp)
    for lp in range(4):
        g_done(lp)
    for u in range(NH):
        ag_sent(u)
        rs_sent(u)
        f_done(0, u)
        f_done(1, u)
    sent(r.RY.at[0:3], r.rys.at[0])
    z_sent(r.RZ, r.rzs.at[0])
    sent(r.CY.at[0:3], r.cys.at[0])
    sent(r.RA.at[0:7], r.ras.at[0])
    sent(r.RC.at[0:7], r.rcs.at[0])

    @pl.when(home)
    def _():
        for n, src in ((0, tok), (1, r.QS0), (2, r.KC0), (5, r.COT)):
            sent(src, r.ms.at[n])

    @pl.when(away)
    def _():
        sent(hb, r.ms.at[3])
        sent(ub, r.ms.at[4])

    for copy in stores:
        copy.wait()


SHAPES = (
    ((2, 3, 64, 128), True, step_rate),
    ((2, 2, 128), False, bias_rate),
    ((2, 64, 128), True, output_rate),
    ((2, 64, 512), True, step_rate),
    ((2, 512), False, bias_rate),
    ((2, 64, 512), True, step_rate),
    ((2, 2, D), False, gain_rate),
    ((2, 4, D), False, bias_rate),
)
N_W = len(SHAPES)


def adam_kernel(*refs):
    lo_in, gt_in = refs[:2]
    grads, states = refs[2 : 2 + N_W], refs[2 + N_W : 2 + 4 * N_W]
    refs = refs[2 + 4 * N_W :]
    lo_out, gt_out = refs[:2]
    outs = refs[2 : 2 + 4 * N_W]
    refs = refs[2 + 4 * N_W :]
    gt_low, gt_full, lo_low = refs[:3]
    held = refs[3 : 3 + 4 * N_W]
    in_sem, out_sem = refs[3 + 4 * N_W :]

    def copy(src, dst, sem):
        made = pltpu.make_async_copy(src, dst, sem)
        made.start()
        return made

    gt_load = copy(gt_in, gt_low, in_sem.at[4 * N_W])
    lo_load = copy(lo_in, lo_low, in_sem.at[4 * N_W + 1])
    loads = []
    for n in range(N_W):
        srcs = (grads[n],) + tuple(states[3 * n : 3 * n + 3])
        loads.append(
            [copy(a, held[4 * n + k], in_sem.at[4 * n + k]) for k, a in enumerate(srcs)]
        )
    gt_load.wait()
    gt_full[...] = gt_low[...].astype(F32)
    last = [copy(gt_full, gt_out, out_sem.at[4 * N_W + 1])]
    lo_load.wait()
    last.append(copy(lo_low, lo_out, out_sem.at[4 * N_W]))
    for n, (_, with_decay, rate) in enumerate(SHAPES):
        for load in loads[n]:
            load.wait()
        g_ref, w_ref, m_ref, v_ref = held[4 * n : 4 * n + 4]
        grad, weight = g_ref[...], w_ref[...]
        first_new = beta_one * m_ref[...] + (1.0 - beta_one) * grad
        second_new = beta_two * v_ref[...] + (1.0 - beta_two) * grad * grad
        first_hat = first_new / (1.0 - beta_one**STEP)
        second_hat = second_new / (1.0 - beta_two**STEP)
        change = first_hat / (jnp.sqrt(second_hat) + eps_adam)
        if with_decay:
            change = change + weight_decay * weight
        m_ref[...] = first_new
        v_ref[...] = second_new
        w_ref[...] = weight - rate * change
        for k, ref in enumerate((g_ref, m_ref, v_ref, w_ref)):
            last.append(copy(ref, outs[4 * n + k], out_sem.at[4 * n + k]))
    for made in last:
        made.wait()


def local(
    tokens, cotangent, bucket_of, seq_lens, w_qkv, head_bias, w_out, w_up, up_bias, w_down, gains,
    biases, first_qkv, second_qkv, first_head, second_head, first_out, second_out, first_up,
    second_up, first_up_bias, second_up_bias, first_down, second_down, first_gains, second_gains,
    first_biases, second_biases,
):
    def turned(v):
        return jnp.swapaxes(v, 1, 2)

    any_ref = pl.BlockSpec(memory_space=pl.ANY)
    smem = pl.BlockSpec(memory_space=pltpu.SMEM)
    wq, wo, wd = turned(w_qkv), turned(w_out), turned(w_down)
    grad_shapes = tuple(jax.ShapeDtypeStruct(shape, F32) for shape, _, _ in SHAPES)
    order = (0, 2, 3, 5, 1, 4, 6, 7)
    rows_low = jax.ShapeDtypeStruct((ROWS, D), BF)
    layer_low, grad_low, *grads = pl.pallas_call(
        kernel,
        out_shape=(rows_low, rows_low) + tuple(grad_shapes[n] for n in order),
        in_specs=[any_ref] * 2 + [smem] * 2 + [any_ref] * 8,
        out_specs=(any_ref,) * N_OUT,
        scratch_shapes=[pltpu.VMEM(s, t) for s, t in SCRATCH.values()]
        + [pltpu.SemaphoreType.DMA((n,)) for n in SEMS.values()],
        compiler_params=pltpu.CompilerParams(
            collective_id=0, has_side_effects=True, vmem_limit_bytes=63 << 20
        ),
    )(
        tokens, cotangent, bucket_of, seq_lens, wq, head_bias, wo, w_up, up_bias, wd, gains, biases
    )
    grads = [grads[order.index(n)] for n in range(N_W)]
    states = (
        wq, turned(first_qkv), turned(second_qkv), head_bias, first_head, second_head,
        wo, turned(first_out), turned(second_out), w_up, first_up, second_up,
        up_bias, first_up_bias, second_up_bias, wd, turned(first_down), turned(second_down),
        gains, first_gains, second_gains, biases, first_biases, second_biases,
    )
    held = [pltpu.VMEM(shape, F32) for shape, _, _ in SHAPES for _ in range(4)]
    layer_out, grad_tokens, *results = pl.pallas_call(
        adam_kernel,
        out_shape=(rows_low, jax.ShapeDtypeStruct((ROWS, D), F32))
        + tuple(shape for shape in grad_shapes for _ in range(4)),
        in_specs=[any_ref] * (2 + 4 * N_W),
        out_specs=(any_ref,) * (2 + 4 * N_W),
        scratch_shapes=[pltpu.VMEM((ROWS, D), t) for t in (BF, F32, BF)]
        + held
        + [pltpu.SemaphoreType.DMA((4 * N_W + 2,))] * 2,
        compiler_params=pltpu.CompilerParams(vmem_limit_bytes=63 << 20),
    )(layer_low, grad_low, *grads, *states)
    for n in (0, 2, 5):
        results[4 * n : 4 * n + 4] = [turned(v) for v in results[4 * n : 4 * n + 4]]
    return (layer_out, grad_tokens, *results)


def solution(mesh):
    fine = Mesh(mesh.devices.reshape(4, 2, 2, 4, 2), ("y", "zl", "core", "x", "zh"))
    b, t = ("y", "zl", "core"), ("x", "zh")
    qkv, head = P(None, b, None, t), P(None, None, t)
    out, up, up_bias, down, rep = P(None, t, b), P(None, b, t), P(None, t), P(None, t, b), P()
    in_specs = (
        P(b, None), P(b, None), P(b), P(b, None), qkv, head, out, up, up_bias, down, rep, rep,
        qkv, qkv, head, head, out, out, up, up, up_bias, up_bias, down, down, rep, rep, rep, rep,
    )
    out_specs = (P(b, None), P(b, None))
    for spec in (qkv, head, out, up, up_bias, down, rep, rep):
        out_specs += (spec,) * 4
    return jax.shard_map(
        local, mesh=fine, in_specs=in_specs, out_specs=out_specs, check_vma=False
    )
```

```python
import jax
import jax.numpy as jnp
from jax import lax
from jax.experimental import pallas as pl
from jax.experimental.pallas import tpu as pltpu
from jax.sharding import Mesh
from jax.sharding import PartitionSpec as P

LAYERS = 2
STEP = 10
ROWS = 512
D = 1024
BLK = 128
NH = 4
HALF = ROWS // NH
OWN = 64 // NH

eps_norm = 1e-05
beta_one = 0.9
beta_two = 0.999
eps_adam = 1e-08
step_rate = 0.1
output_rate = 0.3
bias_rate = 0.3
gain_rate = 1.0
weight_decay = 0.01
masked_score = -1000000000.0

MESH = pl.DeviceIdType.MESH
BF = jnp.bfloat16
F32 = jnp.float32
NT = (((1,), (1,)), ((), ()))
TN = (((0,), (0,)), ((), ()))
NN = (((1,), (0,)), ((), ()))

SCRATCH = dict(
    XB=((2, ROWS, D), BF),
    HB=((2, ROWS, D), BF),
    DFB=((2, ROWS, D), BF),
    DSB=((2, ROWS, D), BF),
    WQ=((2, 4, 4, 64, 384), BF),
    WO=((2, 4, 4, 64, 128), BF),
    WB=((2, 4, 4, 64, 1024), BF),
    SYQ=((2, 4, 32, 384), BF),
    SYO=((2, 4, 32, 128), BF),
    SYB=((2, 4, 32, 1024), BF),
    GA=((2, 4, 4, 64, 512), BF),
    GB=((2, 4, 4, 64, 1024), BF),
    R1AY=((2, 4, 4, 32, 512), BF),
    R1AZ=((2, 4, 4, 32, 512), BF),
    R1BY=((2, 4, 4, 32, 1024), BF),
    R1BZ=((2, 4, 4, 32, 1024), BF),
    S2AY=((2, 4, 32, 512), BF),
    S2AZ=((2, 4, 32, 512), BF),
    S2BY=((2, 4, 32, 1024), BF),
    S2BZ=((2, 4, 32, 1024), BF),
    R2AY=((2, 4, 32, 512), BF),
    R2AZ=((2, 4, 32, 512), BF),
    R2BY=((2, 4, 32, 1024), BF),
    R2BZ=((2, 4, 32, 1024), BF),
    QKV=((2, ROWS, 384), BF),
    O=((2, ROWS, 128), BF),
    PR=((2, 4, 2 * BLK, ROWS), F32),
    A=((2, ROWS, 512), BF),
    GP=((2, ROWS, 512), F32),
    UP=((ROWS, 512), F32),
    DU=((ROWS, 512), BF),
    DQKV=((ROWS, 384), BF),
    DK=((ROWS, 128), F32),
    DV=((ROWS, 128), F32),
    PART=((NH, 4, 2, OWN, D), BF),
    SND=((NH, 4, OWN, D), BF),
    CR=((NH, 4, OWN, D), BF),
    XR=((NH, 4, OWN, D), BF),
    OWNSUM=((NH, OWN, D), F32),
    RES=((NH, OWN, D), F32),
    XH=((4, NH, OWN, D), F32),
    SC=((4, NH, OWN, 128), F32),
    COT=((NH, OWN, D), BF),
    COTF=((2, NH, OWN, D), BF),
    COTM=((2, NH, OWN, D), BF),
    QS0=((ROWS, 128), F32),
    KC0=((8, ROWS), F32),
    QS=((ROWS, 128), F32),
    KC=((8, ROWS), F32),
    WQF=((2, 3, 64, 128), F32),
    WOF=((2, 64, 128), F32),
    WUF=((2, 64, 512), F32),
    WDF=((2, 64, 512), F32),
    PQ=((2, 64, 384), BF),
    PO=((2, 64, 128), BF),
    PB=((2, 64, 1024), BF),
    GNS=((2, 2, D), F32),
    BIS=((2, 4, D), F32),
    HBB=((2, 2, 128), F32),
    UBB=((2, 512), F32),
    GQ=((2, 3, 64, 128), F32),
    GO=((2, 64, 128), F32),
    GU=((2, 64, 512), F32),
    GD=((2, 64, 512), F32),
    GHB=((2, 2, 128), F32),
    GUB=((2, 512), F32),
    GGN=((2, 2, D), F32),
    GBI=((2, 4, D), F32),
    LOB=((ROWS, D), BF),
    GTB=((ROWS, D), BF),
    FIN=((2, NH, OWN, D), BF),
    COL=((8, 512), F32),
    CY=((4, 8, 512), F32),
    COL2=((8, 512), F32),
    CZ=((4, 8, 512), F32),
    ROWP=((16, D), F32),
    RA=((8, 16, 128), F32),
    RW1=((16, 128), F32),
    RY=((4, 16, 128), F32),
    RW2=((16, 128), F32),
    RZ=((4, 16, 128), F32),
    RW3=((16, 128), F32),
    RC=((8, 16, 128), F32),
)
SEMS = dict(
    wsy1=6, wry1=6, wsy2=6, wry2=6, wsz1=6, wrz1=6, wsz2=6, wrz2=6,
    gsy1=4, gry1=4, gsy2=4, gry2=4, gsz1=4, grz1=4, gsz2=4, grz2=4,
    cs=NH, cr=NH, xs=NH, xr=NH, ags=NH, acr=NH, ax1=NH, ax2=NH,
    fs=2 * NH, fr=2 * NH, fzs=2 * NH, fzr=2 * NH, fxs=2 * NH, ras=1, rar=1, rys=1, ryr=1, rzs=1, rzr=1,
    rcs=1, rcr=1, cys=1, cyr=1, czs=1, czr=1, ms=6, mr=6, ld=6 + 2 * NH, st=10 + NH,
)
N_IN, N_OUT = 12, 10


class Refs:
    pass


def loop(n, body):
    def step(k, carry):
        body(k)
        return carry

    lax.fori_loop(0, n, step, 0)


def dot(a, b, dims=NN):
    return lax.dot_general(a, b, dims, preferred_element_type=F32)


def kernel(*refs):
    tok, cot, bucket, lens, wq, hb, wo, wu, ub, wd, gains, biases = refs[:N_IN]
    outs = refs[N_IN : N_IN + N_OUT]
    r = Refs()
    for name, ref in zip(list(SCRATCH) + list(SEMS), refs[N_IN + N_OUT :], strict=True):
        setattr(r, name, ref)

    y, zl, c = lax.axis_index("y"), lax.axis_index("zl"), lax.axis_index("core")
    x, zh = lax.axis_index("x"), lax.axis_index("zh")
    z = zh * 2 + zl
    q_me = zl * 2 + c
    t_me = x * 2 + c
    h_me = x * 2 + zh
    home = c == zh
    away = c != zh
    sib = (y, zl, 1 - c, x, zh)

    def xdev(j):
        return (y, zl, c, j, zh)

    def ydev(yy):
        return (yy, zl, c, x, zh)

    def zout(zz):
        return (y, lax.rem(zz, 2), zh, x, lax.div(zz, 2))

    def zin(q):
        return (y, lax.div(q, 2), lax.rem(q, 2), x, c)

    def remote(src, dst, ss, rs, dev):
        return pltpu.make_async_remote_copy(
            src_ref=src, dst_ref=dst, send_sem=ss, recv_sem=rs, device_id=dev, device_id_type=MESH
        )

    def got(dst, sem):
        remote(dst, dst, sem, sem, sib).wait_recv()

    def sent(src, sem):
        remote(src, src, sem, sem, sib).wait_send()

    def when(cond, body):
        pl.when(cond)(body)

    def unless(cond, body):
        pl.when(jnp.logical_not(cond))(body)

    def others(me, body):
        for d in (2, 1, 3):
            body(lax.rem(me + d, 4))

    bar = pltpu.get_barrier_semaphore()

    def greet(dev):
        pl.semaphore_signal(bar, inc=1, device_id=dev, device_id_type=MESH)

    def greet_plane(i):
        cc, rest = lax.rem(i, 2), lax.div(i, 2)
        hh, xx = lax.rem(rest, 2), lax.div(rest, 2)
        unless((cc == c) & (hh == zh) & (xx == x), lambda: greet((y, zl, cc, xx, hh)))

    others(y, lambda yy: greet(ydev(yy)))
    for n in range(2):
        greet((y, 1 - zl, zh, x, n))
        greet((y, 1 - zl, n, x, c))
    loop(16, greet_plane)

    def rows_of(u, j, core):
        return pl.ds(pl.multiple_of(u * HALF + (j * 2 + core) * OWN, OWN), OWN)

    def half_at(u):
        return pl.ds(u * HALF, HALF)

    loads = [
        (wq, r.WQF), (wo, r.WOF), (wu, r.WUF), (wd, r.WDF), (gains, r.GNS), (biases, r.BIS)
    ]
    for u in range(NH):
        for core in range(2):
            loads.append((cot.at[rows_of(u, x, core)], r.COTF.at[core, u]))
    loads = [pltpu.make_async_copy(a, b, r.ld.at[n]) for n, (a, b) in enumerate(loads)]
    for load in loads:
        load.start()
    for load in loads[:2]:
        load.wait()
    for layer in range(LAYERS):
        for n in range(3):
            r.PQ[layer, :, n * 128 : (n + 1) * 128] = r.WQF[layer, n].astype(BF)
        r.PO[layer] = r.WOF[layer].astype(BF)
    b = bucket[0]
    slots = jnp.where(b == 0, 1, jnp.where(b == 1, 2, jnp.where(b == 2, 4, 8)))
    size = jnp.where(b == 0, 512, jnp.where(b == 1, 256, jnp.where(b == 2, 128, 64)))

    def slot_and_valid(pos):
        slot = lax.shift_right_logical(pos * slots, 9)
        length = jnp.zeros_like(pos)
        for n in range(8):
            length = jnp.where(slot == n, lens[0, n], length)
        return slot, pos - slot * size < length

    pos = lax.broadcasted_iota(jnp.int32, (8, ROWS), 1)
    slot, valid = slot_and_valid(pos)
    r.KC0[...] = jnp.where(valid, slot, -1).astype(F32)
    pos = lax.broadcasted_iota(jnp.int32, (ROWS, 128), 0)
    r.QS0[...] = lax.shift_right_logical(pos * slots, 9).astype(F32)
    for load in loads[2:4]:
        load.wait()
    for layer in range(LAYERS):
        r.PB[layer, :, 0:512] = r.WUF[layer].astype(BF)
        r.PB[layer, :, 512:1024] = r.WDF[layer].astype(BF)
    for load in loads[6:]:
        load.wait()
    for u in range(NH):
        for core in range(2):
            first = u * HALF + (x * 2 + core) * OWN
            slot, valid = slot_and_valid(first + lax.broadcasted_iota(jnp.int32, (OWN, 128), 0))
            keep = jnp.where(valid, 1.0, 0.0)[:, 0:1]
            r.COTM[core, u] = (r.COTF[core, u].astype(F32) * keep).astype(BF)
    pl.semaphore_wait(bar, 22)

    def y_send(src, dst, ss, rs):
        others(y, lambda yy: remote(src(yy), dst, ss, rs, ydev(yy)).start())

    def z_send(src, dst, ss, rs, me, dev):
        def one(k):
            n = lax.rem(me + k, 4)
            local = home & (k == 0)
            when(local, pltpu.make_async_copy(src(n), dst, rs).start)
            unless(local, remote(src(n), dst, ss, rs, dev(n)).start)

        loop(4, one)

    def z_sent(all_four, ss):
        when(home, lambda: sent(all_four.at[0:3], ss))
        when(away, lambda: sent(all_four, ss))

    def w_refs(lp):
        layer, part = divmod(lp, 3)
        src, mid, dst = ((r.PQ, r.SYQ, r.WQ), (r.PO, r.SYO, r.WO), (r.PB, r.SYB, r.WB))[part]
        return src.at[layer], mid.at[layer], dst.at[layer]

    low_rows, high_rows = pl.ds(0, 32), pl.ds(32, 32)

    def w_one(lp):
        src, mid, dst = w_refs(lp)
        low, high = src.at[low_rows], src.at[high_rows]
        y_send(lambda _: low, mid.at[y], r.wsy1.at[lp], r.wry1.at[lp])
        mid[y] = low[...]
        z_send(
            lambda _: high, dst.at[y, q_me, high_rows], r.wsz1.at[lp], r.wrz1.at[lp], z, zout
        )

    def w_two(lp):
        src, mid, dst = w_refs(lp)
        got(mid.at[0:3], r.wry1.at[lp])
        z_send(lambda _: mid, dst.at[:, q_me, low_rows], r.wsy2.at[lp], r.wry2.at[lp], z, zout)
        mine = dst.at[y, :, high_rows]
        got(mine, r.wrz1.at[lp])
        y_send(lambda _: mine, mine, r.wsz2.at[lp], r.wrz2.at[lp])

    def w_wait(lp):
        src, mid, dst = w_refs(lp)
        got(dst.at[:, :, low_rows], r.wry2.at[lp])
        got(dst.at[0:3, :, high_rows], r.wrz2.at[lp])

    def w_done(lp):
        src, mid, dst = w_refs(lp)
        sent(mid.at[0:3], r.wsy1.at[lp])
        z_sent(dst.at[0, :, high_rows], r.wsz1.at[lp])
        z_sent(dst.at[:, :, low_rows], r.wsy2.at[lp])
        sent(dst.at[0:3, :, high_rows], r.wsz2.at[lp])

    def g_refs(lp):
        layer, part = divmod(lp, 2)
        if part == 0:
            group = (r.GA, r.R1AY, r.R1AZ, r.S2AY, r.S2AZ, r.R2AY, r.R2AZ)
        else:
            group = (r.GB, r.R1BY, r.R1BZ, r.S2BY, r.S2BZ, r.R2BY, r.R2BZ)
        return [ref.at[layer] for ref in group]

    def g_one(lp):
        full, r1y, r1z = g_refs(lp)[:3]
        z_send(
            lambda q: full.at[:, q, low_rows], r1y.at[z], r.gsy1.at[lp], r.gry1.at[lp], q_me, zin
        )
        y_send(lambda yy: full.at[yy, :, high_rows], r1z.at[y], r.gsz1.at[lp], r.grz1.at[lp])

    def g_two(lp):
        full, r1y, r1z, s2y, s2z, r2y, r2z = g_refs(lp)
        got(r1y, r.gry1.at[lp])

        def sum_y(n):
            total = r1y[0, n].astype(F32)
            for k in range(1, 4):
                total = total + r1y[k, n].astype(F32)
            s2y[n] = total.astype(BF)

        loop(4, sum_y)
        y_send(lambda yy: s2y.at[yy], r2y.at[y], r.gsy2.at[lp], r.gry2.at[lp])
        got(r1z.at[0:3], r.grz1.at[lp])

        def sum_z(n):
            total = full[y, n, 32:64, :].astype(F32)
            for d in (1, 2, 3):
                total = total + r1z[lax.rem(y + d, 4), n].astype(F32)
            s2z[n] = total.astype(BF)

        loop(4, sum_z)
        z_send(lambda q: s2z.at[q], r2z.at[z], r.gsz2.at[lp], r.grz2.at[lp], q_me, zin)

    def g_three(lp):
        full, r1y, r1z, s2y, s2z, r2y, r2z = g_refs(lp)
        layer, part = divmod(lp, 2)

        def put(rows, total):
            if part == 0:
                for n in range(3):
                    r.GQ[layer, n, rows, :] = total[:, n * 128 : (n + 1) * 128]
                r.GO[layer, rows, :] = total[:, 384:512]
            else:
                r.GU[layer, rows, :] = total[:, 0:512]
                r.GD[layer, rows, :] = total[:, 512:1024]

        got(r2y.at[0:3], r.gry2.at[lp])
        total = s2y[y].astype(F32)
        for d in (1, 2, 3):
            total = total + r2y[lax.rem(y + d, 4)].astype(F32)
        put(low_rows, total)
        got(r2z, r.grz2.at[lp])
        total = r2z[0].astype(F32)
        for k in range(1, 4):
            total = total + r2z[k].astype(F32)
        put(high_rows, total)

    def g_done(lp):
        full, r1y, r1z, s2y, s2z, r2y, r2z = g_refs(lp)
        z_sent(r1y, r.gsy1.at[lp])
        sent(r1z.at[0:3], r.gsz1.at[lp])
        sent(r2y.at[0:3], r.gsy2.at[lp])
        z_sent(r2z, r.gsz2.at[lp])

    def ag_sent(u):
        sent(r.XB.at[0, 0 : 7 * OWN], r.ags.at[u])

    def ag_start(u, buf, first=False):
        if not first:
            ag_sent(u)
        own = buf.at[rows_of(u, x, c)]
        remote(own, own, r.ags.at[u], r.acr.at[u], sib).start()
        for d, arrived in ((2, r.ax2), (1, r.ax1), (3, r.ax1)):
            remote(own, own, r.ags.at[u], arrived.at[u], xdev(lax.rem(x + d, 4))).start()

    def ag_forward(u, buf):
        got(buf.at[0 : 2 * OWN], r.ax1.at[u])
        for d in (1, 3, 2):
            part = buf.at[rows_of(u, lax.rem(x + d, 4), c)]
            if d == 2:
                got(part, r.ax2.at[u])
            remote(part, part, r.ags.at[u], r.acr.at[u], sib).start()

    def ag_wait(u, buf):
        got(buf.at[0 : 4 * OWN], r.acr.at[u])

    def ag_stage(buf, body):
        ag_forward(0, buf)
        for u in range(NH):
            if u < NH - 1:
                ag_forward(u + 1, buf)
            ag_wait(u, buf)
            body(u)

    def ag_rs_stage(buf, first_half, second_half, after=None):
        ag_forward(0, buf)
        for u in range(NH):
            if u < NH - 1:
                ag_forward(u + 1, buf)
            ag_wait(u, buf)
            mid = first_half(u)
            rs_push(u, second_half(mid))
            if u > 0:
                rs_comb(u - 1)
            if after:
                after(u, mid)
        rs_comb(NH - 1)

    def rs_sent(u):
        sent(r.SND.at[u, 0:3], r.xs.at[u])
        sent(r.PART.at[u, :, 1 - c], r.cs.at[u])

    def rs_push(u, part, first=False):
        if not first:
            rs_sent(u)
        r.PART[u] = part.astype(BF).reshape(4, 2, OWN, D)
        remote(r.PART.at[u, :, 1 - c], r.CR.at[u], r.cs.at[u], r.cr.at[u], sib).start()

    def rs_comb(u):
        got(r.CR.at[u], r.cr.at[u])
        both = r.PART[u, :, c].astype(F32) + r.CR[u].astype(F32)
        r.SND[u] = both.astype(BF)
        others(
            x,
            lambda j: remote(
                r.SND.at[u, j], r.XR.at[u, x], r.xs.at[u], r.xr.at[u], xdev(j)
            ).start(),
        )
        r.OWNSUM[u] = r.PART[u, x, c].astype(F32) + r.CR[u, x].astype(F32)

    def rs_finish(u):
        got(r.XR.at[u, 0:3], r.xr.at[u])
        total = r.OWNSUM[u]
        for d in (1, 3, 2):
            total = total + r.XR[u, lax.rem(x + d, 4)].astype(F32)
        return total

    def gb_row(layer, n):
        return r.GNS[layer, n : n + 1, :] if n < 2 else r.BIS[layer, n - 2 : n - 1, :]

    def norm(values, n, u, gain, shift):
        centred = values - jnp.mean(values, axis=-1, keepdims=True)
        scale = lax.rsqrt(jnp.mean(centred * centred, axis=-1, keepdims=True) + eps_norm)
        hat = centred * scale
        r.XH[n, u] = hat
        r.SC[n, u] = jnp.broadcast_to(scale, (OWN, 128))
        return hat * gain + shift

    def norm_back(dy, n, u, layer, which):
        hat = r.XH[n, u]
        scale = r.SC[n, u][:, 0:1]
        dyg = dy * gb_row(layer, which)
        one = jnp.mean(dyg, axis=-1, keepdims=True)
        two = jnp.mean(dyg * hat, axis=-1, keepdims=True)
        return scale * (dyg - one - hat * two)

    def norm_sums(dy, dz, n, u, layer, which):
        def add(row, values):
            at = layer * 6 + row
            r.ROWP[at : at + 1, :] += jnp.sum(values, axis=0, keepdims=True)

        add(which, dy * r.XH[n, u])
        add(3 + 2 * which, dy)
        add(2 + 2 * which, dz)

    lane = lax.broadcasted_iota(jnp.int32, (BLK, 128), 1)
    low_half = lane < 64

    def two_heads(v):
        zero = jnp.zeros_like(v)
        return jnp.concatenate(
            [jnp.where(low_half, v, zero), jnp.where(low_half, zero, v)], axis=0
        )

    def one_row(v):
        return jnp.where(low_half, v[:BLK], v[BLK:])

    def whole(ref):
        return ref[...].reshape(D, ref.shape[-1])

    w_one(0)
    w_one(1)
    w_one(2)

    @pl.when(home)
    def _():
        for n, (src, dst) in enumerate(
            ((tok, r.XB.at[0]), (r.QS0, r.QS), (r.KC0, r.KC), (hb, r.HBB), (ub, r.UBB))
        ):
            pltpu.make_async_copy(src, dst, r.mr.at[n]).start()
            if n < 3:
                remote(src, dst, r.ms.at[n], r.mr.at[n], sib).start()
        pltpu.make_async_copy(r.COTM.at[c], r.COT, r.mr.at[5]).start()
        remote(r.COTM.at[1 - c], r.COT, r.ms.at[5], r.mr.at[5], sib).start()

    @pl.when(away)
    def _():
        for n, (src, dst) in ((3, (hb, r.HBB)), (4, (ub, r.UBB))):
            remote(src, dst, r.ms.at[n], r.mr.at[n], (y, zl, zh, x, c)).start()

    w_two(0)
    w_two(1)
    for load in loads[4:6]:
        load.wait()
    for n, dst in enumerate((r.XB.at[0], r.QS, r.KC, r.HBB, r.UBB, r.COT)):
        got(dst, r.mr.at[n])

    def f_far(n, u, buf):
        m = NH * n + u
        there = buf.at[rows_of(u, x, c)]
        remote(r.FIN.at[n, u], there, r.fzs.at[m], r.fzr.at[m], (y, zl, zh, x, 1 - zh)).start()

    def f_near(n, u, buf):
        there, m = buf.at[rows_of(u, x, c)], NH * n + u
        for d in (2, 1, 3):
            dev = (y, zl, zh, lax.rem(x + d, 4), zh)
            remote(r.FIN.at[n, u], there, r.fs.at[m], r.fr.at[m], dev).start()
        when(home, pltpu.make_async_copy(r.FIN.at[n, u], there, r.fr.at[m]).start)
        when(away, remote(r.FIN.at[n, u], there, r.fs.at[m], r.fr.at[m], sib).start)

    def f_relay(n, u, buf):
        m = NH * n + u
        both = buf.at[pl.ds(pl.multiple_of(u * HALF + x * 2 * OWN, 2 * OWN), 2 * OWN)]

        @pl.when(away)
        def _():
            got(both, r.fzr.at[m])
            others(x, lambda j: remote(both, both, r.fxs.at[m], r.fr.at[m], xdev(j)).start())

    def f_wait(n, u, buf):
        m = NH * n + u
        when(home, lambda: got(buf.at[0 : 8 * OWN], r.fr.at[m]))
        when(away, lambda: got(buf.at[0 : 6 * OWN], r.fr.at[m]))

    def f_done(n, u):
        m = NH * n + u
        sent(r.LOB.at[0:OWN], r.fzs.at[m])
        when(home, lambda: sent(r.LOB.at[0 : 3 * OWN], r.fs.at[m]))

        @pl.when(away)
        def _():
            sent(r.LOB.at[0 : 4 * OWN], r.fs.at[m])
            sent(r.LOB.at[0 : 6 * OWN], r.fxs.at[m])

    for layer in range(LAYERS):
        w_q, w_o, w_b = r.WQ.at[layer], r.WO.at[layer], r.WB.at[layer]
        w_up, w_down = w_b.at[:, :, :, 0:512], w_b.at[:, :, :, 512:1024]
        qkv = r.QKV.at[layer]

        def project(at, layer=layer, w_q=w_q, qkv=qkv):
            out = dot(r.XB[layer, at, :], whole(w_q))
            qkv[at, 0:128] = (out[:, 0:128] + r.HBB[layer, 0:1, :]).astype(BF)
            qkv[at, 128:256] = out[:, 128:256].astype(BF)
            qkv[at, 256:384] = (out[:, 256:384] + r.HBB[layer, 1:2, :]).astype(BF)

        def attend(j, layer=layer, qkv=qkv):
            at = pl.ds(j * BLK, BLK)
            score = dot(two_heads(qkv[at, 0:128]), qkv[:, 128:256], NT) * 0.125
            allowed = r.QS[at, 0:1] == r.KC[0:1, :]
            score = jnp.where(jnp.concatenate([allowed, allowed], axis=0), score, masked_score)
            weight = jnp.exp(score - jnp.max(score, axis=-1, keepdims=True))
            prob = weight * (1.0 / jnp.sum(weight, axis=-1, keepdims=True))
            r.PR[layer, j] = prob
            r.O[layer, at, :] = one_row(dot(prob.astype(BF), qkv[:, 256:384])).astype(BF)

        w_wait(3 * layer)
        if layer == 0:
            w_two(2)
            for u in range(2):
                project(pl.ds(u * 256, 256))
        else:
            w_two(5)
            ag_stage(r.XB.at[1], lambda u: project(half_at(u)))
        w_wait(3 * layer + 1)
        for u in range(NH):
            for j in range(u * 4 // NH, (u + 1) * 4 // NH):
                attend(j)
            if u > 0:
                rs_comb(u - 1)
            rs_push(u, dot(r.O[layer, half_at(u), :], whole(w_o), NT), first=layer == 0)
        rs_comb(NH - 1)
        for u in range(NH):
            if layer == 0:
                stream = r.XB[0, rows_of(u, x, c), :].astype(F32)
            else:
                stream = r.RES[u]
            z_one = rs_finish(u) + stream + gb_row(layer, 2)
            h_val = norm(z_one, 2 * layer, u, gb_row(layer, 0), gb_row(layer, 3))
            r.HB[layer, rows_of(u, x, c), :] = h_val.astype(BF)
            ag_start(u, r.HB.at[layer], first=layer == 0)
            r.RES[u] = h_val
        w_wait(3 * layer + 2)
        if layer == 0:
            for lp in (3, 4, 5):
                w_one(lp)

        def feed(u, layer=layer, w_up=w_up):
            at = half_at(u)
            up = dot(r.HB[layer, at, :], whole(w_up)) + r.UBB[layer : layer + 1, :]
            phi = 0.5 * (1.0 + lax.erf(up * 0.7071067811865476))
            r.GP[layer, at, :] = phi
            r.UP[at, :] = up
            return (up * phi).astype(BF)

        def feed_after(u, act, layer=layer):
            at = half_at(u)
            r.A[layer, at, :] = act
            up = r.UP[at, :]
            r.GP[layer, at, :] += up * jnp.exp(-0.5 * up * up) * 0.3989422804014327

        ag_rs_stage(
            r.HB.at[layer], feed, lambda act, w_down=w_down: dot(act, whole(w_down), NT), feed_after
        )
        if layer == 0:
            w_two(3)
            w_two(4)
        for u in range(NH):
            z_two = rs_finish(u) + r.RES[u] + gb_row(layer, 4)
            x_val = norm(z_two, 2 * layer + 1, u, gb_row(layer, 1), gb_row(layer, 5))
            if layer == 0:
                r.XB[1, rows_of(u, x, c), :] = x_val.astype(BF)
                ag_start(u, r.XB.at[1])
                r.RES[u] = x_val
            else:
                r.FIN[0, u] = x_val.astype(BF)
                f_far(0, u, r.LOB)

    def ra_send(k):
        cc, xx = lax.rem(k, 2), lax.div(k, 2)
        piece = r.ROWP.at[:, pl.ds(pl.multiple_of(k * 128, 128), 128)]
        when(k == t_me, pltpu.make_async_copy(piece, r.RA.at[t_me], r.rar.at[0]).start)
        unless(
            k == t_me,
            remote(piece, r.RA.at[t_me], r.ras.at[0], r.rar.at[0], (y, zl, cc, xx, zh)).start,
        )

    def row_one():
        got(r.RA, r.rar.at[0])
        r.RW1[...] = jnp.sum(r.RA[...], axis=0)
        y_send(lambda _: r.RW1, r.RY.at[y], r.rys.at[0], r.ryr.at[0])
        r.RY[y] = r.RW1[...]

    def row_two():
        got(r.RY.at[0:3], r.ryr.at[0])
        r.RW2[...] = jnp.sum(r.RY[...], axis=0)
        z_send(lambda _: r.RW2, r.RZ.at[z], r.rzs.at[0], r.rzr.at[0], q_me, zin)

    def row_three():
        got(r.RZ, r.rzr.at[0])
        r.RW3[...] = jnp.sum(r.RZ[...], axis=0)

        def rc_send(k):
            hh, xx = lax.rem(k, 2), lax.div(k, 2)
            there = r.RC.at[h_me]
            when(k == h_me, pltpu.make_async_copy(r.RW3, there, r.rcr.at[0]).start)
            unless(
                k == h_me,
                remote(r.RW3, there, r.rcs.at[0], r.rcr.at[0], (y, zl, c, xx, hh)).start,
            )

        loop(8, rc_send)

    def col_one():
        y_send(lambda _: r.COL, r.CY.at[y], r.cys.at[0], r.cyr.at[0])
        r.CY[y] = r.COL[...]

    def col_two():
        got(r.CY.at[0:3], r.cyr.at[0])
        r.COL2[...] = jnp.sum(r.CY[...], axis=0)
        z_send(lambda _: r.COL2, r.CZ.at[z], r.czs.at[0], r.czr.at[0], q_me, zin)

    r.ROWP[...] = jnp.zeros_like(r.ROWP)
    r.COL[...] = jnp.zeros_like(r.COL)

    late = []
    for layer in (1, 0):
        w_q, w_o, w_b = r.WQ.at[layer], r.WO.at[layer], r.WB.at[layer]
        w_up, w_down = w_b.at[:, :, :, 0:512], w_b.at[:, :, :, 512:1024]
        qkv = r.QKV.at[layer]
        df, ds = r.DFB.at[layer], r.DSB.at[layer]

        def grad_a(t, layer=layer):
            at = pl.ds(t * 256, 256)
            one = dot(r.XB[layer, :, at], r.DQKV[...], TN)
            r.GA[layer, t, :, :, 0:384] = one.astype(BF).reshape(4, 64, 384)
            two = dot(r.DSB[layer, :, at], r.O[layer], TN)
            r.GA[layer, t, :, :, 384:512] = two.astype(BF).reshape(4, 64, 128)

        def grad_b(t, layer=layer):
            at = pl.ds(t * 256, 256)
            one = dot(r.HB[layer, :, at], r.DU[...], TN)
            r.GB[layer, t, :, :, 0:512] = one.astype(BF).reshape(4, 64, 512)
            two = dot(r.DFB[layer, :, at], r.A[layer], TN)
            r.GB[layer, t, :, :, 512:1024] = two.astype(BF).reshape(4, 64, 512)

        for u in range(NH):
            dy = r.COT[u].astype(F32) if layer == 1 else rs_finish(u) + r.RES[u]
            dz = norm_back(dy, 2 * layer + 1, u, layer, 1)
            df[rows_of(u, x, c), :] = dz.astype(BF)
            ag_start(u, df)
            r.RES[u] = dz
            norm_sums(dy, dz, 2 * layer + 1, u, layer, 1)
            if late and u < NH - 1:
                late.pop()()
        while late:
            late.pop()()
        if layer == 0:
            g_one(2)
            g_two(3)

        def feed_back(u, layer=layer, w_down=w_down):
            at = half_at(u)
            da = dot(r.DFB[layer, at, :], whole(w_down))
            du = (da * r.GP[layer, at, :]).astype(BF)
            r.DU[at, :] = du
            return du

        def up_sums(layer=layer):
            r.COL[4 * layer + 1 : 4 * layer + 2, :] = jnp.sum(
                r.DU[...].astype(F32), axis=0, keepdims=True
            )

        def head_sums(layer=layer):
            r.COL[4 * layer : 4 * layer + 1, 0:384] = jnp.sum(
                r.DQKV[...].astype(F32), axis=0, keepdims=True
            )

        ag_rs_stage(df, feed_back, lambda du, w_up=w_up: dot(du, whole(w_up), NT))
        late = [up_sums] + [lambda t=t: grad_b(t) for t in (3, 2)]
        grad_b(0)
        grad_b(1)
        for u in range(NH):
            dh = rs_finish(u) + r.RES[u]
            dz = norm_back(dh, 2 * layer, u, layer, 0)
            ds[rows_of(u, x, c), :] = dz.astype(BF)
            ag_start(u, ds)
            r.RES[u] = dz
            norm_sums(dh, dz, 2 * layer, u, layer, 0)
            if late and u < NH - 1:
                late.pop()()
        while late:
            late.pop()()
        g_one(2 * layer + 1)
        if layer == 0:
            loop(8, ra_send)
            g_two(2)

        r.DK[...] = jnp.zeros_like(r.DK)
        r.DV[...] = jnp.zeros_like(r.DV)

        def attend_back(j, layer=layer, w_o=w_o, qkv=qkv):
            at = pl.ds(j * BLK, BLK)
            do = two_heads(dot(r.DSB[layer, at, :], whole(w_o)).astype(BF))
            prob = r.PR[layer, j]
            dp = dot(do, qkv[:, 256:384], NT)
            inner = jnp.sum(prob * dp, axis=-1, keepdims=True)
            dscore = (prob * (dp - inner)).astype(BF)
            dq = one_row(dot(dscore, qkv[:, 128:256])) * 0.125
            r.DQKV[at, 0:128] = dq.astype(BF)
            r.DK[...] += dot(dscore, two_heads(qkv[at, 0:128]), TN)
            r.DV[...] += dot(prob.astype(BF), do, TN)

        def chunk_back(u, layer=layer):
            for j in range(u * 4 // NH, (u + 1) * 4 // NH):
                attend_back(j)
            if 0 < u < 3:
                step = f_near if u == 1 else f_relay
                for n in range(NH // 2):
                    step(0, n + (1 - layer) * NH // 2, r.LOB)
            if u == 0 and layer == 0:
                row_one()

        ag_stage(ds, chunk_back)
        r.DQKV[:, 128:256] = (r.DK[...] * 0.125).astype(BF)
        r.DQKV[:, 256:384] = r.DV[...].astype(BF)
        for u in range(NH):
            part = dot(r.DQKV[half_at(u), :], whole(w_q), NT)
            if u > 0:
                rs_comb(u - 1)
            rs_push(u, part)
        rs_comb(NH - 1)
        if layer == 0:
            head_sums()
            col_one()
            row_two()
        late = [lambda t=t, f=grad_a: f(t) for t in (3, 2, 1)]
        if layer == 1:
            late = [head_sums] + late
        grad_a(0)

    for u in range(NH):
        r.FIN[1, u] = (rs_finish(u) + r.RES[u]).astype(BF)
        f_far(1, u, r.GTB)
        f_near(1, u, r.GTB)
        if late:
            late.pop()()
        if u == NH - 2:
            while late:
                late.pop()()
            g_one(0)
            g_two(1)
    stores = []

    def store(n, src):
        copy = pltpu.make_async_copy(src, outs[n], r.st.at[n])
        copy.start()
        stores.append(copy)

    for u in range(NH):
        f_relay(1, u, r.GTB)
    row_three()
    col_two()
    g_two(0)
    g_three(3)
    g_three(2)
    g_three(1)
    store(4, r.GU)
    store(5, r.GD)
    for u in range(NH):
        f_wait(0, u, r.LOB)
    store(0, r.LOB)
    got(r.CZ, r.czr.at[0])
    z_sent(r.CZ, r.czs.at[0])
    r.COL2[...] = jnp.sum(r.CZ[...], axis=0)
    for layer in range(LAYERS):
        at = 4 * layer
        r.GHB[layer, 0:1, :] = r.COL2[at : at + 1, 0:128]
        r.GHB[layer, 1:2, :] = r.COL2[at : at + 1, 256:384]
        r.GUB[layer : layer + 1, :] = r.COL2[at + 1 : at + 2, :]
    store(6, r.GHB)
    store(7, r.GUB)
    got(r.RC, r.rcr.at[0])
    for p in range(8):
        for layer in range(LAYERS):
            at = 6 * layer
            r.GGN[layer, :, p * 128 : (p + 1) * 128] = r.RC[p, at : at + 2, :]
            r.GBI[layer, :, p * 128 : (p + 1) * 128] = r.RC[p, at + 2 : at + 6, :]
    store(8, r.GGN)
    store(9, r.GBI)
    g_three(0)
    store(2, r.GQ)
    store(3, r.GO)

    for lp in range(6):
        w_done(lp)
    for lp in range(1, 4):
        g_done(lp)
    for u in range(NH):
        ag_sent(u)
        rs_sent(u)
        f_done(0, u)
    for u in range(NH):
        f_wait(1, u, r.GTB)
        copy = pltpu.make_async_copy(
            r.GTB.at[half_at(u)], outs[1].at[half_at(u)], r.st.at[10 + u]
        )
        copy.start()
        stores.append(copy)
    g_done(0)
    for u in range(NH):
        f_done(1, u)
    sent(r.RY.at[0:3], r.rys.at[0])
    z_sent(r.RZ, r.rzs.at[0])
    sent(r.CY.at[0:3], r.cys.at[0])
    sent(r.RA.at[0:7], r.ras.at[0])
    sent(r.RC.at[0:7], r.rcs.at[0])

    @pl.when(home)
    def _():
        for n, src in ((0, tok), (1, r.QS0), (2, r.KC0), (5, r.COT)):
            sent(src, r.ms.at[n])

    @pl.when(away)
    def _():
        sent(hb, r.ms.at[3])
        sent(ub, r.ms.at[4])

    for copy in stores:
        copy.wait()


SHAPES = (
    ((2, 3, 64, 128), True, step_rate),
    ((2, 2, 128), False, bias_rate),
    ((2, 64, 128), True, output_rate),
    ((2, 64, 512), True, step_rate),
    ((2, 512), False, bias_rate),
    ((2, 64, 512), True, step_rate),
    ((2, 2, D), False, gain_rate),
    ((2, 4, D), False, bias_rate),
)
N_W = len(SHAPES)


def adam_kernel(*refs):
    lo_in, gt_in = refs[:2]
    grads, states = refs[2 : 2 + N_W], refs[2 + N_W : 2 + 4 * N_W]
    refs = refs[2 + 4 * N_W :]
    lo_out, gt_out = refs[:2]
    outs = refs[2 : 2 + 4 * N_W]
    refs = refs[2 + 4 * N_W :]
    gt_low, gt_full, lo_low = refs[:3]
    held = refs[3 : 3 + 4 * N_W]
    in_sem, out_sem = refs[3 + 4 * N_W :]

    def copy(src, dst, sem):
        made = pltpu.make_async_copy(src, dst, sem)
        made.start()
        return made

    gt_load = copy(gt_in, gt_low, in_sem.at[4 * N_W])
    lo_load = copy(lo_in, lo_low, in_sem.at[4 * N_W + 1])
    loads = []
    for n in range(N_W):
        srcs = (grads[n],) + tuple(states[3 * n : 3 * n + 3])
        loads.append(
            [copy(a, held[4 * n + k], in_sem.at[4 * n + k]) for k, a in enumerate(srcs)]
        )
    gt_load.wait()
    gt_full[...] = gt_low[...].astype(F32)
    last = [copy(gt_full, gt_out, out_sem.at[4 * N_W + 1])]
    lo_load.wait()
    last.append(copy(lo_low, lo_out, out_sem.at[4 * N_W]))
    for n, (_, with_decay, rate) in enumerate(SHAPES):
        for load in loads[n]:
            load.wait()
        g_ref, w_ref, m_ref, v_ref = held[4 * n : 4 * n + 4]
        grad, weight = g_ref[...], w_ref[...]
        first_new = beta_one * m_ref[...] + (1.0 - beta_one) * grad
        second_new = beta_two * v_ref[...] + (1.0 - beta_two) * grad * grad
        first_hat = first_new / (1.0 - beta_one**STEP)
        second_hat = second_new / (1.0 - beta_two**STEP)
        change = first_hat / (jnp.sqrt(second_hat) + eps_adam)
        if with_decay:
            change = change + weight_decay * weight
        m_ref[...] = first_new
        v_ref[...] = second_new
        w_ref[...] = weight - rate * change
        for k, ref in enumerate((g_ref, m_ref, v_ref, w_ref)):
            last.append(copy(ref, outs[4 * n + k], out_sem.at[4 * n + k]))
    for made in last:
        made.wait()


def local(
    tokens, cotangent, bucket_of, seq_lens, w_qkv, head_bias, w_out, w_up, up_bias, w_down, gains,
    biases, first_qkv, second_qkv, first_head, second_head, first_out, second_out, first_up,
    second_up, first_up_bias, second_up_bias, first_down, second_down, first_gains, second_gains,
    first_biases, second_biases,
):
    def turned(v):
        return jnp.swapaxes(v, 1, 2)

    any_ref = pl.BlockSpec(memory_space=pl.ANY)
    smem = pl.BlockSpec(memory_space=pltpu.SMEM)
    wq, wo, wd = turned(w_qkv), turned(w_out), turned(w_down)
    grad_shapes = tuple(jax.ShapeDtypeStruct(shape, F32) for shape, _, _ in SHAPES)
    order = (0, 2, 3, 5, 1, 4, 6, 7)
    rows_low = jax.ShapeDtypeStruct((ROWS, D), BF)
    layer_low, grad_low, *grads = pl.pallas_call(
        kernel,
        out_shape=(rows_low, rows_low) + tuple(grad_shapes[n] for n in order),
        in_specs=[any_ref] * 2 + [smem] * 2 + [any_ref] * 8,
        out_specs=(any_ref,) * N_OUT,
        scratch_shapes=[pltpu.VMEM(s, t) for s, t in SCRATCH.values()]
        + [pltpu.SemaphoreType.DMA((n,)) for n in SEMS.values()],
        compiler_params=pltpu.CompilerParams(
            collective_id=0, has_side_effects=True, vmem_limit_bytes=63 << 20
        ),
    )(
        tokens, cotangent, bucket_of, seq_lens, wq, head_bias, wo, w_up, up_bias, wd, gains, biases
    )
    grads = [grads[order.index(n)] for n in range(N_W)]
    states = (
        wq, turned(first_qkv), turned(second_qkv), head_bias, first_head, second_head,
        wo, turned(first_out), turned(second_out), w_up, first_up, second_up,
        up_bias, first_up_bias, second_up_bias, wd, turned(first_down), turned(second_down),
        gains, first_gains, second_gains, biases, first_biases, second_biases,
    )
    held = [pltpu.VMEM(shape, F32) for shape, _, _ in SHAPES for _ in range(4)]
    layer_out, grad_tokens, *results = pl.pallas_call(
        adam_kernel,
        out_shape=(rows_low, jax.ShapeDtypeStruct((ROWS, D), F32))
        + tuple(shape for shape in grad_shapes for _ in range(4)),
        in_specs=[any_ref] * (2 + 4 * N_W),
        out_specs=(any_ref,) * (2 + 4 * N_W),
        scratch_shapes=[pltpu.VMEM((ROWS, D), t) for t in (BF, F32, BF)]
        + held
        + [pltpu.SemaphoreType.DMA((4 * N_W + 2,))] * 2,
        compiler_params=pltpu.CompilerParams(vmem_limit_bytes=63 << 20),
    )(layer_low, grad_low, *grads, *states)
    for n in (0, 2, 5):
        results[4 * n : 4 * n + 4] = [turned(v) for v in results[4 * n : 4 * n + 4]]
    return (layer_out, grad_tokens, *results)


def solution(mesh):
    fine = Mesh(mesh.devices.reshape(4, 2, 2, 4, 2), ("y", "zl", "core", "x", "zh"))
    b, t = ("y", "zl", "core"), ("x", "zh")
    qkv, head = P(None, b, None, t), P(None, None, t)
    out, up, up_bias, down, rep = P(None, t, b), P(None, b, t), P(None, t), P(None, t, b), P()
    in_specs = (
        P(b, None), P(b, None), P(b), P(b, None), qkv, head, out, up, up_bias, down, rep, rep,
        qkv, qkv, head, head, out, out, up, up, up_bias, up_bias, down, down, rep, rep, rep, rep,
    )
    out_specs = (P(b, None), P(b, None))
    for spec in (qkv, head, out, up, up_bias, down, rep, rep):
        out_specs += (spec,) * 4
    return jax.shard_map(
        local, mesh=fine, in_specs=in_specs, out_specs=out_specs, check_vma=False
    )
```

```python
import jax
import jax.numpy as jnp
from jax import lax
from jax.experimental import pallas as pl
from jax.experimental.pallas import tpu as pltpu
from jax.sharding import Mesh
from jax.sharding import PartitionSpec as P

LAYERS = 2
STEP = 10
ROWS = 512
D = 1024
BLK = 128
NH = 4
HALF = ROWS // NH
OWN = 64 // NH

eps_norm = 1e-05
beta_one = 0.9
beta_two = 0.999
eps_adam = 1e-08
step_rate = 0.1
output_rate = 0.3
bias_rate = 0.3
gain_rate = 1.0
weight_decay = 0.01
masked_score = -1000000000.0

MESH = pl.DeviceIdType.MESH
BF = jnp.bfloat16
F32 = jnp.float32
NT = (((1,), (1,)), ((), ()))
TN = (((0,), (0,)), ((), ()))
NN = (((1,), (0,)), ((), ()))

SCRATCH = dict(
    XB=((2, ROWS, D), BF),
    HB=((2, ROWS, D), BF),
    DFB=((2, ROWS, D), BF),
    DSB=((2, ROWS, D), BF),
    WQ=((2, 4, 4, 64, 384), BF),
    WO=((2, 4, 4, 64, 128), BF),
    WB=((2, 4, 4, 64, 1024), BF),
    SYQ=((2, 4, 32, 384), BF),
    SYO=((2, 4, 32, 128), BF),
    SYB=((2, 4, 32, 1024), BF),
    GA=((2, 4, 4, 64, 512), BF),
    GB=((2, 4, 4, 64, 1024), BF),
    R1AY=((2, 4, 4, 32, 512), BF),
    R1AZ=((2, 4, 4, 32, 512), BF),
    R1BY=((2, 4, 4, 32, 1024), BF),
    R1BZ=((2, 4, 4, 32, 1024), BF),
    S2AY=((2, 4, 32, 512), BF),
    S2AZ=((2, 4, 32, 512), BF),
    S2BY=((2, 4, 32, 1024), BF),
    S2BZ=((2, 4, 32, 1024), BF),
    R2AY=((2, 4, 32, 512), BF),
    R2AZ=((2, 4, 32, 512), BF),
    R2BY=((2, 4, 32, 1024), BF),
    R2BZ=((2, 4, 32, 1024), BF),
    QKV=((2, ROWS, 384), BF),
    O=((2, ROWS, 128), BF),
    PR=((2, 4, 2 * BLK, ROWS), F32),
    A=((2, ROWS, 512), BF),
    GP=((2, ROWS, 512), F32),
    UP=((ROWS, 512), F32),
    DU=((ROWS, 512), BF),
    DQKV=((ROWS, 384), BF),
    DK=((ROWS, 128), F32),
    DV=((ROWS, 128), F32),
    PART=((NH, 4, 2, OWN, D), BF),
    SND=((NH, 4, OWN, D), BF),
    CR=((NH, 4, OWN, D), BF),
    XR=((NH, 4, OWN, D), BF),
    OWNSUM=((NH, OWN, D), F32),
    RES=((NH, OWN, D), F32),
    XH=((4, NH, OWN, D), F32),
    SC=((4, NH, OWN, 128), F32),
    COT=((NH, OWN, D), BF),
    COTF=((2, NH, OWN, D), BF),
    COTM=((2, NH, OWN, D), BF),
    QS0=((ROWS, 128), F32),
    KC0=((8, ROWS), F32),
    QS=((ROWS, 128), F32),
    KC=((8, ROWS), F32),
    WQF=((2, 3, 64, 128), F32),
    WOF=((2, 64, 128), F32),
    WUF=((2, 64, 512), F32),
    WDF=((2, 64, 512), F32),
    PQ=((2, 64, 384), BF),
    PO=((2, 64, 128), BF),
    PB=((2, 64, 1024), BF),
    GNS=((2, 2, D), F32),
    BIS=((2, 4, D), F32),
    HBB=((2, 2, 128), F32),
    UBB=((2, 512), F32),
    GQ=((2, 3, 64, 128), F32),
    GO=((2, 64, 128), F32),
    GU=((2, 64, 512), F32),
    GD=((2, 64, 512), F32),
    GHB=((2, 2, 128), F32),
    GUB=((2, 512), F32),
    GGN=((2, 2, D), F32),
    GBI=((2, 4, D), F32),
    LOB=((ROWS, D), BF),
    GTB=((ROWS, D), BF),
    FIN=((2, NH, OWN, D), BF),
    COL=((8, 512), F32),
    CY=((4, 8, 512), F32),
    COL2=((8, 512), F32),
    CZ=((4, 8, 512), F32),
    ROWP=((16, D), F32),
    RA=((8, 16, 128), F32),
    RW1=((16, 128), F32),
    RY=((4, 16, 128), F32),
    RW2=((16, 128), F32),
    RZ=((4, 16, 128), F32),
    RW3=((16, 128), F32),
    RC=((8, 16, 128), F32),
)
SEMS = dict(
    wsy1=6, wry1=6, wsy2=6, wry2=6, wsz1=6, wrz1=6, wsz2=6, wrz2=6,
    gsy1=4, gry1=4, gsy2=4, gry2=4, gsz1=4, grz1=4, gsz2=4, grz2=4,
    cs=NH, cr=NH, xs=NH, xr=NH, ags=NH, acr=NH, ax1=NH, ax2=NH,
    fs=2 * NH, fr=2 * NH, fzs=2 * NH, fzr=2 * NH, fxs=2 * NH, ras=1, rar=1, rys=1, ryr=1, rzs=1, rzr=1,
    rcs=1, rcr=1, cys=1, cyr=1, czs=1, czr=1, ms=6, mr=6, ld=6 + 2 * NH, st=10 + NH,
)
N_IN, N_OUT = 12, 10


class Refs:
    pass


def loop(n, body):
    def step(k, carry):
        body(k)
        return carry

    lax.fori_loop(0, n, step, 0)


def dot(a, b, dims=NN):
    return lax.dot_general(a, b, dims, preferred_element_type=F32)


def kernel(*refs):
    tok, cot, bucket, lens, wq, hb, wo, wu, ub, wd, gains, biases = refs[:N_IN]
    outs = refs[N_IN : N_IN + N_OUT]
    r = Refs()
    for name, ref in zip(list(SCRATCH) + list(SEMS), refs[N_IN + N_OUT :], strict=True):
        setattr(r, name, ref)

    y, zl, c = lax.axis_index("y"), lax.axis_index("zl"), lax.axis_index("core")
    x, zh = lax.axis_index("x"), lax.axis_index("zh")
    z = zh * 2 + zl
    q_me = zl * 2 + c
    t_me = x * 2 + c
    h_me = x * 2 + zh
    home = c == zh
    away = c != zh
    sib = (y, zl, 1 - c, x, zh)

    def xdev(j):
        return (y, zl, c, j, zh)

    def ydev(yy):
        return (yy, zl, c, x, zh)

    def zout(zz):
        return (y, lax.rem(zz, 2), zh, x, lax.div(zz, 2))

    def zin(q):
        return (y, lax.div(q, 2), lax.rem(q, 2), x, c)

    def remote(src, dst, ss, rs, dev):
        return pltpu.make_async_remote_copy(
            src_ref=src, dst_ref=dst, send_sem=ss, recv_sem=rs, device_id=dev, device_id_type=MESH
        )

    def got(dst, sem):
        remote(dst, dst, sem, sem, sib).wait_recv()

    def sent(src, sem):
        remote(src, src, sem, sem, sib).wait_send()

    def when(cond, body):
        pl.when(cond)(body)

    def unless(cond, body):
        pl.when(jnp.logical_not(cond))(body)

    def others(me, body):
        for d in (2, 1, 3):
            body(lax.rem(me + d, 4))

    bar = pltpu.get_barrier_semaphore()

    def greet(dev):
        pl.semaphore_signal(bar, inc=1, device_id=dev, device_id_type=MESH)

    others(y, lambda yy: greet(ydev(yy)))
    for n in range(2):
        greet((y, 1 - zl, zh, x, n))
        greet((y, 1 - zl, n, x, c))
    for n in range(1, 16):
        cc, hh = (1 - c if n % 2 else c), (1 - zh if n // 2 % 2 else zh)
        greet((y, zl, cc, lax.rem(x + n // 4, 4), hh))

    def rows_of(u, j, core):
        return pl.ds(pl.multiple_of(u * HALF + (j * 2 + core) * OWN, OWN), OWN)

    def half_at(u):
        return pl.ds(u * HALF, HALF)

    loads = [
        (wq, r.WQF), (wo, r.WOF), (wu, r.WUF), (wd, r.WDF), (gains, r.GNS), (biases, r.BIS)
    ]
    for u in range(NH):
        for core in range(2):
            loads.append((cot.at[rows_of(u, x, core)], r.COTF.at[core, u]))
    loads = [pltpu.make_async_copy(a, b, r.ld.at[n]) for n, (a, b) in enumerate(loads)]
    for load in loads:
        load.start()
    for load in loads[:2]:
        load.wait()
    for layer in range(LAYERS):
        for n in range(3):
            r.PQ[layer, :, n * 128 : (n + 1) * 128] = r.WQF[layer, n].astype(BF)
        r.PO[layer] = r.WOF[layer].astype(BF)
    b = bucket[0]
    slots = jnp.where(b == 0, 1, jnp.where(b == 1, 2, jnp.where(b == 2, 4, 8)))
    size = jnp.where(b == 0, 512, jnp.where(b == 1, 256, jnp.where(b == 2, 128, 64)))

    def slot_and_valid(pos):
        slot = lax.shift_right_logical(pos * slots, 9)
        length = jnp.zeros_like(pos)
        for n in range(8):
            length = jnp.where(slot == n, lens[0, n], length)
        return slot, pos - slot * size < length

    pos = lax.broadcasted_iota(jnp.int32, (8, ROWS), 1)
    slot, valid = slot_and_valid(pos)
    r.KC0[...] = jnp.where(valid, slot, -1).astype(F32)
    pos = lax.broadcasted_iota(jnp.int32, (ROWS, 128), 0)
    r.QS0[...] = lax.shift_right_logical(pos * slots, 9).astype(F32)
    for load in loads[2:4]:
        load.wait()
    for layer in range(LAYERS):
        r.PB[layer, :, 0:512] = r.WUF[layer].astype(BF)
        r.PB[layer, :, 512:1024] = r.WDF[layer].astype(BF)
    for load in loads[6:]:
        load.wait()
    for u in range(NH):
        for core in range(2):
            first = u * HALF + (x * 2 + core) * OWN
            slot, valid = slot_and_valid(first + lax.broadcasted_iota(jnp.int32, (OWN, 128), 0))
            keep = jnp.where(valid, 1.0, 0.0)[:, 0:1]
            r.COTM[core, u] = (r.COTF[core, u].astype(F32) * keep).astype(BF)
    pl.semaphore_wait(bar, 22)

    def y_send(src, dst, ss, rs):
        others(y, lambda yy: remote(src(yy), dst, ss, rs, ydev(yy)).start())

    def z_send(src, dst, ss, rs, me, dev):
        others(me, lambda n: remote(src(n), dst, ss, rs, dev(n)).start())
        when(home, lambda: pltpu.make_async_copy(src(me), dst, rs).start())
        when(away, lambda: remote(src(me), dst, ss, rs, dev(me)).start())

    def z_sent(all_four, ss):
        when(home, lambda: sent(all_four.at[0:3], ss))
        when(away, lambda: sent(all_four, ss))

    def w_refs(lp):
        layer, part = divmod(lp, 3)
        src, mid, dst = ((r.PQ, r.SYQ, r.WQ), (r.PO, r.SYO, r.WO), (r.PB, r.SYB, r.WB))[part]
        return src.at[layer], mid.at[layer], dst.at[layer]

    low_rows, high_rows = pl.ds(0, 32), pl.ds(32, 32)

    def w_one(lp):
        src, mid, dst = w_refs(lp)
        low, high = src.at[low_rows], src.at[high_rows]
        y_send(lambda _: low, mid.at[y], r.wsy1.at[lp], r.wry1.at[lp])
        mid[y] = low[...]
        z_send(
            lambda _: high, dst.at[y, q_me, high_rows], r.wsz1.at[lp], r.wrz1.at[lp], z, zout
        )

    def w_two(lp):
        src, mid, dst = w_refs(lp)
        got(mid.at[0:3], r.wry1.at[lp])
        z_send(lambda _: mid, dst.at[:, q_me, low_rows], r.wsy2.at[lp], r.wry2.at[lp], z, zout)
        mine = dst.at[y, :, high_rows]
        got(mine, r.wrz1.at[lp])
        y_send(lambda _: mine, mine, r.wsz2.at[lp], r.wrz2.at[lp])

    def w_wait(lp):
        src, mid, dst = w_refs(lp)
        got(dst.at[:, :, low_rows], r.wry2.at[lp])
        got(dst.at[0:3, :, high_rows], r.wrz2.at[lp])

    def w_done(lp):
        src, mid, dst = w_refs(lp)
        sent(mid.at[0:3], r.wsy1.at[lp])
        z_sent(dst.at[0, :, high_rows], r.wsz1.at[lp])
        z_sent(dst.at[:, :, low_rows], r.wsy2.at[lp])
        sent(dst.at[0:3, :, high_rows], r.wsz2.at[lp])

    def g_refs(lp):
        layer, part = divmod(lp, 2)
        if part == 0:
            group = (r.GA, r.R1AY, r.R1AZ, r.S2AY, r.S2AZ, r.R2AY, r.R2AZ)
        else:
            group = (r.GB, r.R1BY, r.R1BZ, r.S2BY, r.S2BZ, r.R2BY, r.R2BZ)
        return [ref.at[layer] for ref in group]

    def g_one(lp):
        full, r1y, r1z = g_refs(lp)[:3]
        z_send(
            lambda q: full.at[:, q, low_rows], r1y.at[z], r.gsy1.at[lp], r.gry1.at[lp], q_me, zin
        )
        y_send(lambda yy: full.at[yy, :, high_rows], r1z.at[y], r.gsz1.at[lp], r.grz1.at[lp])

    def g_two(lp):
        full, r1y, r1z, s2y, s2z, r2y, r2z = g_refs(lp)
        got(r1y, r.gry1.at[lp])

        def sum_y(n):
            total = r1y[0, n].astype(F32)
            for k in range(1, 4):
                total = total + r1y[k, n].astype(F32)
            s2y[n] = total.astype(BF)

        loop(4, sum_y)
        y_send(lambda yy: s2y.at[yy], r2y.at[y], r.gsy2.at[lp], r.gry2.at[lp])
        got(r1z.at[0:3], r.grz1.at[lp])

        def sum_z(n):
            total = full[y, n, 32:64, :].astype(F32)
            for d in (1, 2, 3):
                total = total + r1z[lax.rem(y + d, 4), n].astype(F32)
            s2z[n] = total.astype(BF)

        loop(4, sum_z)
        z_send(lambda q: s2z.at[q], r2z.at[z], r.gsz2.at[lp], r.grz2.at[lp], q_me, zin)

    def g_three(lp):
        full, r1y, r1z, s2y, s2z, r2y, r2z = g_refs(lp)
        layer, part = divmod(lp, 2)

        def put(rows, total):
            if part == 0:
                for n in range(3):
                    r.GQ[layer, n, rows, :] = total[:, n * 128 : (n + 1) * 128]
                r.GO[layer, rows, :] = total[:, 384:512]
            else:
                r.GU[layer, rows, :] = total[:, 0:512]
                r.GD[layer, rows, :] = total[:, 512:1024]

        got(r2y.at[0:3], r.gry2.at[lp])
        total = s2y[y].astype(F32)
        for d in (1, 2, 3):
            total = total + r2y[lax.rem(y + d, 4)].astype(F32)
        put(low_rows, total)
        got(r2z, r.grz2.at[lp])
        total = r2z[0].astype(F32)
        for k in range(1, 4):
            total = total + r2z[k].astype(F32)
        put(high_rows, total)

    def g_done(lp):
        full, r1y, r1z, s2y, s2z, r2y, r2z = g_refs(lp)
        z_sent(r1y, r.gsy1.at[lp])
        sent(r1z.at[0:3], r.gsz1.at[lp])
        sent(r2y.at[0:3], r.gsy2.at[lp])
        z_sent(r2z, r.gsz2.at[lp])

    def ag_sent(u):
        sent(r.XB.at[0, 0 : 7 * OWN], r.ags.at[u])

    def ag_start(u, buf, first=False):
        if not first:
            ag_sent(u)
        own = buf.at[rows_of(u, x, c)]
        for d, arrived in ((2, r.ax2), (1, r.ax1), (3, r.ax1)):
            remote(own, own, r.ags.at[u], arrived.at[u], xdev(lax.rem(x + d, 4))).start()
        remote(own, own, r.ags.at[u], r.acr.at[u], sib).start()

    def ag_forward(u, buf):
        got(buf.at[0 : 2 * OWN], r.ax1.at[u])
        for d in (1, 3, 2):
            part = buf.at[rows_of(u, lax.rem(x + d, 4), c)]
            if d == 2:
                got(part, r.ax2.at[u])
            remote(part, part, r.ags.at[u], r.acr.at[u], sib).start()

    def ag_wait(u, buf):
        got(buf.at[0 : 4 * OWN], r.acr.at[u])

    def ag_stage(buf, body):
        ag_forward(0, buf)
        for u in range(NH):
            if u < NH - 1:
                ag_forward(u + 1, buf)
            ag_wait(u, buf)
            body(u)

    def ag_rs_stage(buf, first_half, second_half, after=None):
        ag_forward(0, buf)
        for u in range(NH):
            if u < NH - 1:
                ag_forward(u + 1, buf)
            ag_wait(u, buf)
            mid = first_half(u)
            rs_push(u, second_half(mid))
            if u > 0:
                rs_comb(u - 1)
            if after:
                after(u, mid)
        rs_comb(NH - 1)

    def rs_sent(u):
        sent(r.SND.at[u, 0:3], r.xs.at[u])
        sent(r.PART.at[u, :, 1 - c], r.cs.at[u])

    def rs_push(u, part, first=False):
        if not first:
            rs_sent(u)
        r.PART[u] = part.astype(BF).reshape(4, 2, OWN, D)
        remote(r.PART.at[u, :, 1 - c], r.CR.at[u], r.cs.at[u], r.cr.at[u], sib).start()

    def rs_comb(u):
        got(r.CR.at[u], r.cr.at[u])
        both = r.PART[u, :, c].astype(F32) + r.CR[u].astype(F32)
        r.SND[u] = both.astype(BF)
        others(
            x,
            lambda j: remote(
                r.SND.at[u, j], r.XR.at[u, x], r.xs.at[u], r.xr.at[u], xdev(j)
            ).start(),
        )
        r.OWNSUM[u] = r.PART[u, x, c].astype(F32) + r.CR[u, x].astype(F32)

    def rs_finish(u):
        got(r.XR.at[u, 0:3], r.xr.at[u])
        total = r.OWNSUM[u]
        for d in (1, 3, 2):
            total = total + r.XR[u, lax.rem(x + d, 4)].astype(F32)
        return total

    def gb_row(layer, n):
        return r.GNS[layer, n : n + 1, :] if n < 2 else r.BIS[layer, n - 2 : n - 1, :]

    def norm(values, n, u, gain, shift):
        centred = values - jnp.mean(values, axis=-1, keepdims=True)
        scale = lax.rsqrt(jnp.mean(centred * centred, axis=-1, keepdims=True) + eps_norm)
        hat = centred * scale
        r.XH[n, u] = hat
        r.SC[n, u] = jnp.broadcast_to(scale, (OWN, 128))
        return hat * gain + shift

    def norm_back(dy, n, u, layer, which):
        hat = r.XH[n, u]
        scale = r.SC[n, u][:, 0:1]
        dyg = dy * gb_row(layer, which)
        one = jnp.mean(dyg, axis=-1, keepdims=True)
        two = jnp.mean(dyg * hat, axis=-1, keepdims=True)
        return scale * (dyg - one - hat * two)

    def norm_sums(dy, dz, n, u, layer, which):
        def add(row, values):
            at = layer * 6 + row
            r.ROWP[at : at + 1, :] += jnp.sum(values, axis=0, keepdims=True)

        add(which, dy * r.XH[n, u])
        add(3 + 2 * which, dy)
        add(2 + 2 * which, dz)

    lane = lax.broadcasted_iota(jnp.int32, (BLK, 128), 1)
    low_half = lane < 64

    def two_heads(v):
        zero = jnp.zeros_like(v)
        return jnp.concatenate(
            [jnp.where(low_half, v, zero), jnp.where(low_half, zero, v)], axis=0
        )

    def one_row(v):
        return jnp.where(low_half, v[:BLK], v[BLK:])

    def whole(ref):
        return ref[...].reshape(D, ref.shape[-1])

    w_one(0)
    w_one(1)
    w_one(2)

    @pl.when(home)
    def _():
        for n, (src, dst) in enumerate(
            ((tok, r.XB.at[0]), (r.QS0, r.QS), (r.KC0, r.KC), (hb, r.HBB), (ub, r.UBB))
        ):
            pltpu.make_async_copy(src, dst, r.mr.at[n]).start()
            if n < 3:
                remote(src, dst, r.ms.at[n], r.mr.at[n], sib).start()
        pltpu.make_async_copy(r.COTM.at[c], r.COT, r.mr.at[5]).start()
        remote(r.COTM.at[1 - c], r.COT, r.ms.at[5], r.mr.at[5], sib).start()

    @pl.when(away)
    def _():
        for n, (src, dst) in ((3, (hb, r.HBB)), (4, (ub, r.UBB))):
            remote(src, dst, r.ms.at[n], r.mr.at[n], (y, zl, zh, x, c)).start()

    w_two(0)
    w_two(1)
    for load in loads[4:6]:
        load.wait()
    for n, dst in enumerate((r.XB.at[0], r.QS, r.KC, r.HBB, r.UBB, r.COT)):
        got(dst, r.mr.at[n])

    def f_far(n, u, buf):
        m = NH * n + u
        there = buf.at[rows_of(u, x, c)]
        remote(r.FIN.at[n, u], there, r.fzs.at[m], r.fzr.at[m], (y, zl, zh, x, 1 - zh)).start()

    def f_near(n, u, buf):
        there, m = buf.at[rows_of(u, x, c)], NH * n + u
        for d in (2, 1, 3):
            dev = (y, zl, zh, lax.rem(x + d, 4), zh)
            remote(r.FIN.at[n, u], there, r.fs.at[m], r.fr.at[m], dev).start()
        when(home, pltpu.make_async_copy(r.FIN.at[n, u], there, r.fr.at[m]).start)
        when(away, remote(r.FIN.at[n, u], there, r.fs.at[m], r.fr.at[m], sib).start)

    def f_relay(n, u, buf):
        m = NH * n + u
        both = buf.at[pl.ds(pl.multiple_of(u * HALF + x * 2 * OWN, 2 * OWN), 2 * OWN)]

        @pl.when(away)
        def _():
            got(both, r.fzr.at[m])
            others(x, lambda j: remote(both, both, r.fxs.at[m], r.fr.at[m], xdev(j)).start())

    def f_wait(n, u, buf):
        m = NH * n + u
        when(home, lambda: got(buf.at[0 : 8 * OWN], r.fr.at[m]))
        when(away, lambda: got(buf.at[0 : 6 * OWN], r.fr.at[m]))

    def f_done(n, u):
        m = NH * n + u
        sent(r.LOB.at[0:OWN], r.fzs.at[m])
        when(home, lambda: sent(r.LOB.at[0 : 3 * OWN], r.fs.at[m]))

        @pl.when(away)
        def _():
            sent(r.LOB.at[0 : 4 * OWN], r.fs.at[m])
            sent(r.LOB.at[0 : 6 * OWN], r.fxs.at[m])

    for layer in range(LAYERS):
        w_q, w_o, w_b = r.WQ.at[layer], r.WO.at[layer], r.WB.at[layer]
        w_up, w_down = w_b.at[:, :, :, 0:512], w_b.at[:, :, :, 512:1024]
        qkv = r.QKV.at[layer]

        def project(at, layer=layer, w_q=w_q, qkv=qkv):
            out = dot(r.XB[layer, at, :], whole(w_q))
            qkv[at, 0:128] = (out[:, 0:128] + r.HBB[layer, 0:1, :]).astype(BF)
            qkv[at, 128:256] = out[:, 128:256].astype(BF)
            qkv[at, 256:384] = (out[:, 256:384] + r.HBB[layer, 1:2, :]).astype(BF)

        def attend(j, layer=layer, qkv=qkv):
            at = pl.ds(j * BLK, BLK)
            score = dot(two_heads(qkv[at, 0:128]), qkv[:, 128:256], NT) * 0.125
            allowed = r.QS[at, 0:1] == r.KC[0:1, :]
            score = jnp.where(jnp.concatenate([allowed, allowed], axis=0), score, masked_score)
            weight = jnp.exp(score - jnp.max(score, axis=-1, keepdims=True))
            prob = weight * (1.0 / jnp.sum(weight, axis=-1, keepdims=True))
            r.PR[layer, j] = prob
            r.O[layer, at, :] = one_row(dot(prob.astype(BF), qkv[:, 256:384])).astype(BF)

        w_wait(3 * layer)
        if layer == 0:
            w_two(2)
            for u in range(2):
                project(pl.ds(u * 256, 256))
        else:
            w_two(5)
            ag_stage(r.XB.at[1], lambda u: project(half_at(u)))
        w_wait(3 * layer + 1)
        for u in range(NH):
            for j in range(u * 4 // NH, (u + 1) * 4 // NH):
                attend(j)
            if u > 0:
                rs_comb(u - 1)
            rs_push(u, dot(r.O[layer, half_at(u), :], whole(w_o), NT), first=layer == 0)
        rs_comb(NH - 1)
        for u in range(NH):
            if layer == 0:
                stream = r.XB[0, rows_of(u, x, c), :].astype(F32)
            else:
                stream = r.RES[u]
            z_one = rs_finish(u) + stream + gb_row(layer, 2)
            h_val = norm(z_one, 2 * layer, u, gb_row(layer, 0), gb_row(layer, 3))
            r.HB[layer, rows_of(u, x, c), :] = h_val.astype(BF)
            ag_start(u, r.HB.at[layer], first=layer == 0)
            r.RES[u] = h_val
        w_wait(3 * layer + 2)
        if layer == 0:
            for lp in (3, 4, 5):
                w_one(lp)

        def feed(u, layer=layer, w_up=w_up):
            at = half_at(u)
            up = dot(r.HB[layer, at, :], whole(w_up)) + r.UBB[layer : layer + 1, :]
            phi = 0.5 * (1.0 + lax.erf(up * 0.7071067811865476))
            r.GP[layer, at, :] = phi
            r.UP[at, :] = up
            return (up * phi).astype(BF)

        def feed_after(u, act, layer=layer):
            at = half_at(u)
            r.A[layer, at, :] = act
            up = r.UP[at, :]
            r.GP[layer, at, :] += up * jnp.exp(-0.5 * up * up) * 0.3989422804014327

        ag_rs_stage(
            r.HB.at[layer], feed, lambda act, w_down=w_down: dot(act, whole(w_down), NT), feed_after
        )
        if layer == 0:
            w_two(3)
            w_two(4)
        for u in range(NH):
            z_two = rs_finish(u) + r.RES[u] + gb_row(layer, 4)
            x_val = norm(z_two, 2 * layer + 1, u, gb_row(layer, 1), gb_row(layer, 5))
            if layer == 0:
                r.XB[1, rows_of(u, x, c), :] = x_val.astype(BF)
                ag_start(u, r.XB.at[1])
                r.RES[u] = x_val
            else:
                r.FIN[0, u] = x_val.astype(BF)
                f_far(0, u, r.LOB)

    def ra_send(k):
        cc, xx = lax.rem(k, 2), lax.div(k, 2)
        piece = r.ROWP.at[:, pl.ds(pl.multiple_of(k * 128, 128), 128)]
        when(k == t_me, pltpu.make_async_copy(piece, r.RA.at[t_me], r.rar.at[0]).start)
        unless(
            k == t_me,
            remote(piece, r.RA.at[t_me], r.ras.at[0], r.rar.at[0], (y, zl, cc, xx, zh)).start,
        )

    def row_one():
        got(r.RA, r.rar.at[0])
        r.RW1[...] = jnp.sum(r.RA[...], axis=0)
        y_send(lambda _: r.RW1, r.RY.at[y], r.rys.at[0], r.ryr.at[0])
        r.RY[y] = r.RW1[...]

    def row_two():
        got(r.RY.at[0:3], r.ryr.at[0])
        r.RW2[...] = jnp.sum(r.RY[...], axis=0)
        z_send(lambda _: r.RW2, r.RZ.at[z], r.rzs.at[0], r.rzr.at[0], q_me, zin)

    def row_three():
        got(r.RZ, r.rzr.at[0])
        r.RW3[...] = jnp.sum(r.RZ[...], axis=0)

        def rc_send(k):
            hh, xx = lax.rem(k, 2), lax.div(k, 2)
            there = r.RC.at[h_me]
            when(k == h_me, pltpu.make_async_copy(r.RW3, there, r.rcr.at[0]).start)
            unless(
                k == h_me,
                remote(r.RW3, there, r.rcs.at[0], r.rcr.at[0], (y, zl, c, xx, hh)).start,
            )

        loop(8, rc_send)

    def col_one():
        y_send(lambda _: r.COL, r.CY.at[y], r.cys.at[0], r.cyr.at[0])
        r.CY[y] = r.COL[...]

    def col_two():
        got(r.CY.at[0:3], r.cyr.at[0])
        r.COL2[...] = jnp.sum(r.CY[...], axis=0)
        z_send(lambda _: r.COL2, r.CZ.at[z], r.czs.at[0], r.czr.at[0], q_me, zin)

    r.ROWP[...] = jnp.zeros_like(r.ROWP)
    r.COL[...] = jnp.zeros_like(r.COL)

    late = []
    for layer in (1, 0):
        w_q, w_o, w_b = r.WQ.at[layer], r.WO.at[layer], r.WB.at[layer]
        w_up, w_down = w_b.at[:, :, :, 0:512], w_b.at[:, :, :, 512:1024]
        qkv = r.QKV.at[layer]
        df, ds = r.DFB.at[layer], r.DSB.at[layer]

        def grad_a(t, layer=layer):
            at = pl.ds(t * 256, 256)
            one = dot(r.XB[layer, :, at], r.DQKV[...], TN)
            r.GA[layer, t, :, :, 0:384] = one.astype(BF).reshape(4, 64, 384)
            two = dot(r.DSB[layer, :, at], r.O[layer], TN)
            r.GA[layer, t, :, :, 384:512] = two.astype(BF).reshape(4, 64, 128)

        def grad_b(t, layer=layer):
            at = pl.ds(t * 256, 256)
            one = dot(r.HB[layer, :, at], r.DU[...], TN)
            r.GB[layer, t, :, :, 0:512] = one.astype(BF).reshape(4, 64, 512)
            two = dot(r.DFB[layer, :, at], r.A[layer], TN)
            r.GB[layer, t, :, :, 512:1024] = two.astype(BF).reshape(4, 64, 512)

        for u in range(NH):
            dy = r.COT[u].astype(F32) if layer == 1 else rs_finish(u) + r.RES[u]
            dz = norm_back(dy, 2 * layer + 1, u, layer, 1)
            df[rows_of(u, x, c), :] = dz.astype(BF)
            ag_start(u, df)
            r.RES[u] = dz
            norm_sums(dy, dz, 2 * layer + 1, u, layer, 1)
            if late and u < NH - 1:
                late.pop()()
        while late:
            late.pop()()
        if layer == 0:
            g_one(2)
            g_two(3)

        def feed_back(u, layer=layer, w_down=w_down):
            at = half_at(u)
            da = dot(r.DFB[layer, at, :], whole(w_down))
            du = (da * r.GP[layer, at, :]).astype(BF)
            r.DU[at, :] = du
            return du

        def up_sums(layer=layer):
            r.COL[4 * layer + 1 : 4 * layer + 2, :] = jnp.sum(
                r.DU[...].astype(F32), axis=0, keepdims=True
            )

        def head_sums(layer=layer):
            r.COL[4 * layer : 4 * layer + 1, 0:384] = jnp.sum(
                r.DQKV[...].astype(F32), axis=0, keepdims=True
            )

        ag_rs_stage(df, feed_back, lambda du, w_up=w_up: dot(du, whole(w_up), NT))
        late = [up_sums] + [lambda t=t: grad_b(t) for t in (3, 2)]
        grad_b(0)
        grad_b(1)
        for u in range(NH):
            dh = rs_finish(u) + r.RES[u]
            dz = norm_back(dh, 2 * layer, u, layer, 0)
            ds[rows_of(u, x, c), :] = dz.astype(BF)
            ag_start(u, ds)
            r.RES[u] = dz
            norm_sums(dh, dz, 2 * layer, u, layer, 0)
            if late and u < NH - 1:
                late.pop()()
        while late:
            late.pop()()
        g_one(2 * layer + 1)
        if layer == 0:
            loop(8, ra_send)
            g_two(2)

        r.DK[...] = jnp.zeros_like(r.DK)
        r.DV[...] = jnp.zeros_like(r.DV)

        def attend_back(j, layer=layer, w_o=w_o, qkv=qkv):
            at = pl.ds(j * BLK, BLK)
            do = two_heads(dot(r.DSB[layer, at, :], whole(w_o)).astype(BF))
            prob = r.PR[layer, j]
            dp = dot(do, qkv[:, 256:384], NT)
            inner = jnp.sum(prob * dp, axis=-1, keepdims=True)
            dscore = (prob * (dp - inner)).astype(BF)
            dq = one_row(dot(dscore, qkv[:, 128:256])) * 0.125
            r.DQKV[at, 0:128] = dq.astype(BF)
            r.DK[...] += dot(dscore, two_heads(qkv[at, 0:128]), TN)
            r.DV[...] += dot(prob.astype(BF), do, TN)

        def chunk_back(u, layer=layer):
            for j in range(u * 4 // NH, (u + 1) * 4 // NH):
                attend_back(j)
            if 0 < u < 3:
                step = f_near if u == 1 else f_relay
                for n in range(NH // 2):
                    step(0, n + (1 - layer) * NH // 2, r.LOB)
            if u == 0 and layer == 0:
                row_one()

        ag_stage(ds, chunk_back)
        r.DQKV[:, 128:256] = (r.DK[...] * 0.125).astype(BF)
        r.DQKV[:, 256:384] = r.DV[...].astype(BF)
        for u in range(NH):
            part = dot(r.DQKV[half_at(u), :], whole(w_q), NT)
            if u > 0:
                rs_comb(u - 1)
            rs_push(u, part)
        rs_comb(NH - 1)
        if layer == 0:
            head_sums()
            col_one()
            row_two()
        late = [lambda t=t, f=grad_a: f(t) for t in (3, 2, 1)]
        if layer == 1:
            late = [head_sums] + late
        grad_a(0)

    for u in range(NH):
        r.FIN[1, u] = (rs_finish(u) + r.RES[u]).astype(BF)
        f_far(1, u, r.GTB)
        f_near(1, u, r.GTB)
        if late:
            late.pop()()
        if u == NH - 2:
            while late:
                late.pop()()
            g_one(0)
            g_two(1)
    stores = []

    def store(n, src):
        copy = pltpu.make_async_copy(src, outs[n], r.st.at[n])
        copy.start()
        stores.append(copy)

    for u in range(NH):
        f_relay(1, u, r.GTB)
    row_three()
    col_two()
    g_two(0)
    g_three(3)
    g_three(2)
    g_three(1)
    store(4, r.GU)
    store(5, r.GD)
    for u in range(NH):
        f_wait(0, u, r.LOB)
    store(0, r.LOB)
    got(r.CZ, r.czr.at[0])
    z_sent(r.CZ, r.czs.at[0])
    r.COL2[...] = jnp.sum(r.CZ[...], axis=0)
    for layer in range(LAYERS):
        at = 4 * layer
        r.GHB[layer, 0:1, :] = r.COL2[at : at + 1, 0:128]
        r.GHB[layer, 1:2, :] = r.COL2[at : at + 1, 256:384]
        r.GUB[layer : layer + 1, :] = r.COL2[at + 1 : at + 2, :]
    store(6, r.GHB)
    store(7, r.GUB)
    got(r.RC, r.rcr.at[0])
    for p in range(8):
        for layer in range(LAYERS):
            at = 6 * layer
            r.GGN[layer, :, p * 128 : (p + 1) * 128] = r.RC[p, at : at + 2, :]
            r.GBI[layer, :, p * 128 : (p + 1) * 128] = r.RC[p, at + 2 : at + 6, :]
    store(8, r.GGN)
    store(9, r.GBI)
    g_three(0)
    store(2, r.GQ)
    store(3, r.GO)

    for lp in range(6):
        w_done(lp)
    for lp in range(1, 4):
        g_done(lp)
    for u in range(NH):
        ag_sent(u)
        rs_sent(u)
        f_done(0, u)
    for u in range(NH):
        f_wait(1, u, r.GTB)
        copy = pltpu.make_async_copy(
            r.GTB.at[half_at(u)], outs[1].at[half_at(u)], r.st.at[10 + u]
        )
        copy.start()
        stores.append(copy)
    g_done(0)
    for u in range(NH):
        f_done(1, u)
    sent(r.RY.at[0:3], r.rys.at[0])
    z_sent(r.RZ, r.rzs.at[0])
    sent(r.CY.at[0:3], r.cys.at[0])
    sent(r.RA.at[0:7], r.ras.at[0])
    sent(r.RC.at[0:7], r.rcs.at[0])

    @pl.when(home)
    def _():
        for n, src in ((0, tok), (1, r.QS0), (2, r.KC0), (5, r.COT)):
            sent(src, r.ms.at[n])

    @pl.when(away)
    def _():
        sent(hb, r.ms.at[3])
        sent(ub, r.ms.at[4])

    for copy in stores:
        copy.wait()


SHAPES = (
    ((2, 3, 64, 128), True, step_rate),
    ((2, 2, 128), False, bias_rate),
    ((2, 64, 128), True, output_rate),
    ((2, 64, 512), True, step_rate),
    ((2, 512), False, bias_rate),
    ((2, 64, 512), True, step_rate),
    ((2, 2, D), False, gain_rate),
    ((2, 4, D), False, bias_rate),
)
N_W = len(SHAPES)


def adam_kernel(*refs):
    lo_in, gt_in = refs[:2]
    grads, states = refs[2 : 2 + N_W], refs[2 + N_W : 2 + 4 * N_W]
    refs = refs[2 + 4 * N_W :]
    lo_out, gt_out = refs[:2]
    outs = refs[2 : 2 + 4 * N_W]
    refs = refs[2 + 4 * N_W :]
    gt_low, gt_full, lo_low = refs[:3]
    held = refs[3 : 3 + 4 * N_W]
    in_sem, out_sem = refs[3 + 4 * N_W :]

    def copy(src, dst, sem):
        made = pltpu.make_async_copy(src, dst, sem)
        made.start()
        return made

    gt_load = copy(gt_in, gt_low, in_sem.at[4 * N_W])
    lo_load = copy(lo_in, lo_low, in_sem.at[4 * N_W + 1])
    loads = []
    for n in range(N_W):
        srcs = (grads[n],) + tuple(states[3 * n : 3 * n + 3])
        loads.append(
            [copy(a, held[4 * n + k], in_sem.at[4 * n + k]) for k, a in enumerate(srcs)]
        )
    gt_load.wait()
    gt_full[...] = gt_low[...].astype(F32)
    last = [copy(gt_full, gt_out, out_sem.at[4 * N_W + 1])]
    lo_load.wait()
    last.append(copy(lo_low, lo_out, out_sem.at[4 * N_W]))
    for n, (_, with_decay, rate) in enumerate(SHAPES):
        for load in loads[n]:
            load.wait()
        g_ref, w_ref, m_ref, v_ref = held[4 * n : 4 * n + 4]
        grad, weight = g_ref[...], w_ref[...]
        first_new = beta_one * m_ref[...] + (1.0 - beta_one) * grad
        second_new = beta_two * v_ref[...] + (1.0 - beta_two) * grad * grad
        first_hat = first_new / (1.0 - beta_one**STEP)
        second_hat = second_new / (1.0 - beta_two**STEP)
        change = first_hat / (jnp.sqrt(second_hat) + eps_adam)
        if with_decay:
            change = change + weight_decay * weight
        m_ref[...] = first_new
        v_ref[...] = second_new
        w_ref[...] = weight - rate * change
        for k, ref in enumerate((g_ref, m_ref, v_ref, w_ref)):
            last.append(copy(ref, outs[4 * n + k], out_sem.at[4 * n + k]))
    for made in last:
        made.wait()


def local(
    tokens, cotangent, bucket_of, seq_lens, w_qkv, head_bias, w_out, w_up, up_bias, w_down, gains,
    biases, first_qkv, second_qkv, first_head, second_head, first_out, second_out, first_up,
    second_up, first_up_bias, second_up_bias, first_down, second_down, first_gains, second_gains,
    first_biases, second_biases,
):
    def turned(v):
        return jnp.swapaxes(v, 1, 2)

    any_ref = pl.BlockSpec(memory_space=pl.ANY)
    smem = pl.BlockSpec(memory_space=pltpu.SMEM)
    wq, wo, wd = turned(w_qkv), turned(w_out), turned(w_down)
    grad_shapes = tuple(jax.ShapeDtypeStruct(shape, F32) for shape, _, _ in SHAPES)
    order = (0, 2, 3, 5, 1, 4, 6, 7)
    rows_low = jax.ShapeDtypeStruct((ROWS, D), BF)
    layer_low, grad_low, *grads = pl.pallas_call(
        kernel,
        out_shape=(rows_low, rows_low) + tuple(grad_shapes[n] for n in order),
        in_specs=[any_ref] * 2 + [smem] * 2 + [any_ref] * 8,
        out_specs=(any_ref,) * N_OUT,
        scratch_shapes=[pltpu.VMEM(s, t) for s, t in SCRATCH.values()]
        + [pltpu.SemaphoreType.DMA((n,)) for n in SEMS.values()],
        compiler_params=pltpu.CompilerParams(
            collective_id=0, has_side_effects=True, vmem_limit_bytes=63 << 20
        ),
    )(
        tokens, cotangent, bucket_of, seq_lens, wq, head_bias, wo, w_up, up_bias, wd, gains, biases
    )
    grads = [grads[order.index(n)] for n in range(N_W)]
    states = (
        wq, turned(first_qkv), turned(second_qkv), head_bias, first_head, second_head,
        wo, turned(first_out), turned(second_out), w_up, first_up, second_up,
        up_bias, first_up_bias, second_up_bias, wd, turned(first_down), turned(second_down),
        gains, first_gains, second_gains, biases, first_biases, second_biases,
    )
    held = [pltpu.VMEM(shape, F32) for shape, _, _ in SHAPES for _ in range(4)]
    layer_out, grad_tokens, *results = pl.pallas_call(
        adam_kernel,
        out_shape=(rows_low, jax.ShapeDtypeStruct((ROWS, D), F32))
        + tuple(shape for shape in grad_shapes for _ in range(4)),
        in_specs=[any_ref] * (2 + 4 * N_W),
        out_specs=(any_ref,) * (2 + 4 * N_W),
        scratch_shapes=[pltpu.VMEM((ROWS, D), t) for t in (BF, F32, BF)]
        + held
        + [pltpu.SemaphoreType.DMA((4 * N_W + 2,))] * 2,
        compiler_params=pltpu.CompilerParams(vmem_limit_bytes=63 << 20),
    )(layer_low, grad_low, *grads, *states)
    for n in (0, 2, 5):
        results[4 * n : 4 * n + 4] = [turned(v) for v in results[4 * n : 4 * n + 4]]
    return (layer_out, grad_tokens, *results)


def solution(mesh):
    fine = Mesh(mesh.devices.reshape(4, 2, 2, 4, 2), ("y", "zl", "core", "x", "zh"))
    b, t = ("y", "zl", "core"), ("x", "zh")
    qkv, head = P(None, b, None, t), P(None, None, t)
    out, up, up_bias, down, rep = P(None, t, b), P(None, b, t), P(None, t), P(None, t, b), P()
    in_specs = (
        P(b, None), P(b, None), P(b), P(b, None), qkv, head, out, up, up_bias, down, rep, rep,
        qkv, qkv, head, head, out, out, up, up, up_bias, up_bias, down, down, rep, rep, rep, rep,
    )
    out_specs = (P(b, None), P(b, None))
    for spec in (qkv, head, out, up, up_bias, down, rep, rep):
        out_specs += (spec,) * 4
    return jax.shard_map(
        local, mesh=fine, in_specs=in_specs, out_specs=out_specs, check_vma=False
    )
```
